32 devices in a mesh: seq: 8 (over y, x, core), head: 4 (over z).
Axes of the slice: x: 2, y: 2, z: 4, core: 2. Of those that a mesh axis runs over, the one named last changes fastest.
Arguments:
- queries: bfloat16 [2048, 16, 128], P('seq'), may hold values from -6 to 6
- keys: bfloat16 [2048, 2, 128], P(('seq', 'head')), may hold values from -6 to 6
- values: bfloat16 [2048, 2, 128], P(('seq', 'head')), may hold values from -6 to 6
- block_ids: int32 [8], P('seq'), may hold values from 0 to 7, each once
Outputs:
- attended: bfloat16 [2048, 16, 128], P('seq', 'head')
The draws below stay inside these ranges and needn't reach their ends.
Inputs may be any that keep to these rules, and one draw needn't show every extreme that they name: `block_ids`: each block number appears exactly once.
All inputs are finite; a program needn't handle non-finite values.
Results may differ from the reference program's by a relative error of at most 0.014.
Values may be sent and summed in bfloat16 or wider, within the bound.
No kernel may reach another device: no remote copies, remote signals or barrier semaphores. Data moves between devices by JAX's collectives and lax.ppermute only.
A program may use at most 64 MiB of HBM per device.

```python
import math
import jax
import jax.numpy as jnp
from jax import lax

QH = 16
KVH = 2
HD = 128
TOK_DEV = 256
NBLK = 8
TOKENS = 2048


def planted_layout(key):
    signs = jnp.where(jax.random.bernoulli(key, 0.5, (HD,)), 1.0, -1.0).astype(jnp.float32)
    row_index = jnp.arange(TOKENS, dtype=jnp.int32)
    block_num = row_index // TOK_DEV
    offset = row_index % TOK_DEV
    chosen = block_num % 8 == 0
    level = 115.0 + 43.0 * (block_num // 8 % 3).astype(jnp.float32)
    strength = jnp.sqrt(level / jnp.sqrt(jnp.float32(HD)))
    return (signs, offset, chosen, strength)


def draw_keys(key, part):
    signs, offset, chosen, strength = planted_layout(key)
    key = jax.random.fold_in(key, 1)
    base = jnp.clip(jax.random.normal(key, (TOKENS, KVH, HD), jnp.float32), -6.0, 6.0)
    planted = strength[:, None, None] * signs[None, None, :]
    first = (chosen & (offset == 0))[:, None, None]
    second = (chosen & (offset == 1))[:, None, None]
    base = jnp.where(first, planted, jnp.where(second, 0.985 * planted, base))
    return base.astype(jnp.bfloat16)


def draw_queries(key, part):
    signs, offset, chosen, strength = planted_layout(key)
    key = jax.random.fold_in(key, 2)
    base = jnp.clip(jax.random.normal(key, (TOKENS, QH, HD), jnp.float32), -6.0, 6.0)
    planted = strength[:, None, None] * signs[None, None, :]
    last = (chosen & (offset == TOK_DEV - 1))[:, None, None]
    base = jnp.where(last, planted, base)
    return base.astype(jnp.bfloat16)


def level_of(key, shape, split, least, top_value):
    gain, own = 1.0, jax.random.fold_in(key, 6)
    for axis_at, shards_of in split:
        heights = jnp.exp(jax.random.uniform(jax.random.fold_in(own, axis_at), (shards_of,), jnp.float32, least / len(split), top_value / len(split)))
        gain = gain * jnp.repeat(heights, shape[axis_at] // shards_of).reshape([-1 if axis == axis_at else 1 for axis in range(len(shape))])
    return gain


def bell_draw(key, shape, spread, bound, pieces=(), kind=jnp.bfloat16):
    drawn = jax.random.normal(key, shape, jnp.float32) * spread
    if len(pieces) > 0:
        drawn = level_of(key, shape, pieces, -0.22, 0.18) * drawn
    return jnp.clip(drawn, min=-bound, max=bound).astype(kind)


def setup_inputs(seed: int = 0) -> dict:
    key_list = jax.random.split(jax.random.key(seed), 5)
    return {
        "queries": draw_queries(jax.random.fold_in(key_list[4], 71), 0),
        "keys": draw_keys(jax.random.fold_in(key_list[4], 71), 0),
        "values": bell_draw(key_list[2], (TOKENS, KVH, HD), 1.0, 6.0, ((0, 32),)),
        "block_ids": jax.random.permutation(key_list[3], NBLK).astype(jnp.int32),
    }


def placements(block_ids):
    row_index = jnp.arange(TOKENS, dtype=jnp.int32)
    return block_ids[row_index // TOK_DEV] * TOK_DEV + row_index % TOK_DEV


def reference(queries, keys, values, block_ids):
    place = placements(block_ids)
    group = QH // KVH
    query_rows = math.gcd(TOKENS, 256)
    key_float = keys.astype(jnp.float32)
    value_float = values.astype(jnp.float32)
    query_blocks = queries.reshape(TOKENS // query_rows, query_rows, KVH, group, HD)
    place_blocks = place.reshape(TOKENS // query_rows, query_rows)

    def one_block(pair):
        query_part, query_place = pair
        scores = jnp.einsum("qkgd,skd->kgqs", query_part.astype(jnp.float32), key_float) * (HD ** -0.5)
        visible = place[None, :] <= query_place[:, None]
        scores = jnp.where(visible, scores, -jnp.inf)
        highest = jnp.max(scores, axis=-1, keepdims=True)
        expo = jnp.where(visible, jnp.exp(scores - highest), 0.0)
        total = jnp.sum(expo, axis=-1)
        weights = lax.optimization_barrier(expo.astype(jnp.bfloat16)).astype(jnp.float32)
        summed = jnp.einsum("kgqs,skd->kgqd", weights, value_float)
        result = summed / total[..., None]
        result = jnp.transpose(result, (2, 0, 1, 3)).reshape(query_rows, QH, HD)
        return result.astype(jnp.bfloat16)

    outputs = lax.map(one_block, (query_blocks, place_blocks))
    return outputs.reshape(TOKENS, QH, HD)
```

```python
import functools
import math

import jax
import jax.numpy as jnp
from jax import lax
from jax.experimental import pallas as pl
from jax.experimental.pallas import tpu as pltpu
from jax.sharding import PartitionSpec as P

MARK = 16
DIRECT_BYTES = 8 * 1024 * 1024


def attend(kv_heads, part, scale, own_ref, query_ref, rows_ref, out_ref, high_ref, total_ref, accum_ref):
    blocks, pieces = rows_ref.shape[:2]
    block_rows = pieces * part
    query_rows, head_width = query_ref.shape
    group = query_rows // block_rows
    own = own_ref[0]
    kv_head = own_ref[1]
    step = pl.program_id(0)

    @pl.when(step == 0)
    def _():
        high_ref[...] = jnp.full_like(high_ref, -1e30)
        total_ref[...] = jnp.zeros_like(total_ref)
        accum_ref[...] = jnp.zeros_like(accum_ref)

    def fold(block, diagonal):
        key_rows = jnp.concatenate(
            [rows_ref[block, piece, pl.ds(pl.multiple_of(kv_head * part, part), part), :] for piece in range(pieces)]
        )
        value_rows = jnp.concatenate(
            [
                rows_ref[block, piece, pl.ds(pl.multiple_of((kv_heads + kv_head) * part, part), part), :]
                for piece in range(pieces)
            ]
        )
        scores = lax.dot_general(
            key_rows, query_ref[...], (((1,), (1,)), ((), ())), preferred_element_type=jnp.float32
        )
        if diagonal:
            key_at = lax.broadcasted_iota(jnp.int32, scores.shape, 0)
            query_at = lax.broadcasted_iota(jnp.int32, scores.shape, 1) // group
            scores = jnp.where(key_at <= query_at, scores, -1e30)
        old_high = high_ref[...]
        new_high = jnp.maximum(old_high, jnp.max(scores, axis=0, keepdims=True))
        expo = jnp.exp((scores - new_high) * scale)
        factor = jnp.exp((old_high - new_high) * scale)
        high_ref[...] = new_high
        total_ref[...] = total_ref[...] * factor + jnp.sum(expo, axis=0, keepdims=True)
        accum_ref[...] = accum_ref[...] * factor + lax.dot_general(
            value_rows, expo.astype(jnp.bfloat16), (((0,), (0,)), ((), ())), preferred_element_type=jnp.float32
        )

    for block in range(blocks):
        mark = rows_ref[block, 0, pl.ds(2 * kv_heads * part, MARK), :]
        place = jnp.max(mark.astype(jnp.float32)).astype(jnp.int32)

        @pl.when(place < own)
        def _():
            fold(block, False)

        @pl.when(place == own)
        def _():
            fold(block, True)

    @pl.when(step == pl.num_programs(0) - 1)
    def _():
        result = accum_ref[...] / total_ref[...]
        out_ref[...] = result.T.astype(out_ref.dtype)


def shards(queries, keys, values, block_ids):
    rows_dev, all_heads, head_width = queries.shape
    part, kv_heads = keys.shape[:2]
    head_index = lax.axis_index("head")
    head_shards = lax.axis_size("head")
    seq_shards = lax.axis_size("seq")
    heads_out = all_heads // head_shards
    kv_head = head_index * heads_out // (all_heads // kv_heads)
    own_queries = lax.dynamic_slice_in_dim(queries, head_index * heads_out, heads_out, 1)
    own_queries = own_queries.reshape(rows_dev * heads_out, head_width)
    mark = jnp.broadcast_to(block_ids.astype(jnp.bfloat16)[:, None], (MARK, head_width))
    packed = jnp.concatenate(
        [
            jnp.transpose(keys, (1, 0, 2)).reshape(kv_heads * part, head_width),
            jnp.transpose(values, (1, 0, 2)).reshape(kv_heads * part, head_width),
            mark,
        ]
    )
    if seq_shards * head_shards * packed.size * 2 <= DIRECT_BYTES:
        rows = lax.all_gather(packed, ("seq", "head"), axis=0, tiled=False)
        rows = rows.reshape(seq_shards, head_shards, packed.shape[0], head_width)
    else:
        rows = lax.all_gather(packed, "head", axis=0, tiled=False)
        sets = rows[:, : 2 * kv_heads * part].reshape(head_shards, 2, kv_heads, part, head_width)
        sets = lax.dynamic_index_in_dim(sets, kv_head, 2, keepdims=False)
        sets = sets.reshape(head_shards, 2 * part, head_width)
        rows = jnp.concatenate([sets, rows[:, 2 * kv_heads * part :]], axis=1)
        rows = lax.all_gather(rows, "seq", axis=0, tiled=False)
        kv_heads, kv_head = 1, jnp.int32(0)
    own = jnp.stack([block_ids[0], kv_head.astype(jnp.int32)])
    unit = math.gcd(seq_shards, 8)
    query_rows = rows_dev * heads_out
    result = pl.pallas_call(
        functools.partial(attend, kv_heads, part, head_width ** (-0.5)),
        grid=(seq_shards // unit,),
        out_shape=jax.ShapeDtypeStruct((query_rows, head_width), jnp.bfloat16),
        in_specs=[
            pl.BlockSpec(memory_space=pltpu.SMEM),
            pl.BlockSpec((query_rows, head_width), lambda i: (0, 0)),
            pl.BlockSpec((unit,) + rows.shape[1:], lambda i: (i, 0, 0, 0)),
        ],
        out_specs=pl.BlockSpec((query_rows, head_width), lambda i: (0, 0)),
        scratch_shapes=[
            pltpu.VMEM((1, query_rows), jnp.float32),
            pltpu.VMEM((1, query_rows), jnp.float32),
            pltpu.VMEM((head_width, query_rows), jnp.float32),
        ],
        compiler_params=pltpu.CompilerParams(vmem_limit_bytes=32 * 1024 * 1024),
    )(own, own_queries, rows)
    return result.reshape(rows_dev, heads_out, head_width)


def solution(mesh):
    return jax.shard_map(
        shards,
        mesh=mesh,
        in_specs=(
            P("seq", None, None),
            P(("seq", "head"), None, None),
            P(("seq", "head"), None, None),
            P("seq"),
        ),
        out_specs=P("seq", "head", None),
        check_vma=False,
    )
```

```python
import functools
import math

import jax
import jax.numpy as jnp
from jax import lax
from jax.experimental import pallas as pl
from jax.experimental.pallas import tpu as pltpu
from jax.sharding import PartitionSpec as P

MARK = 16
PERMUTES = 8


def pack(heads_out, group, keys_ref, values_ref, *out_refs):
    kv_heads = keys_ref.shape[1]
    part = keys_ref.shape[0]
    shards = len(out_refs)
    here = lax.axis_index("head")
    key_rows = [keys_ref[:, head, :] for head in range(kv_heads)]
    value_rows = [values_ref[:, head, :] for head in range(kv_heads)]
    for shift, out_ref in enumerate(out_refs):
        kv_head = lax.rem(here + shift, shards) * heads_out // group
        chosen_key, chosen_value = key_rows[0], value_rows[0]
        for head in range(1, kv_heads):
            chosen_key = jnp.where(kv_head == head, key_rows[head], chosen_key)
            chosen_value = jnp.where(kv_head == head, value_rows[head], chosen_value)
        out_ref[:part, :] = chosen_key
        out_ref[part:, :] = chosen_value


def attend(pieces, part, scale, own_ref, query_ref, *refs):
    near_refs, far_refs = refs[:pieces], refs[pieces:-4]
    out_ref, high_ref, total_ref, accum_ref = refs[-4:]
    query_rows = query_ref.shape[0]
    group = query_rows // (pieces * part)
    own = own_ref[0]
    here = lax.axis_index("head")
    step = pl.program_id(0)

    def fold(key_parts, value_parts, diagonal):
        key_rows = jnp.concatenate(key_parts)
        value_rows = jnp.concatenate(value_parts)
        scores = lax.dot_general(
            key_rows, query_ref[...], (((1,), (1,)), ((), ())), preferred_element_type=jnp.float32
        )
        if diagonal:
            row = lax.broadcasted_iota(jnp.int32, scores.shape, 0)
            piece = lax.rem(here + pieces - row // part, pieces)
            key_at = piece * part + row % part
            query_at = lax.broadcasted_iota(jnp.int32, scores.shape, 1) // group
            scores = jnp.where(key_at <= query_at, scores, -1e30)
        high = jnp.max(scores, axis=0, keepdims=True)
        if not diagonal:
            old_high = high_ref[...]
            high = jnp.maximum(old_high, high)
            factor = jnp.exp((old_high - high) * scale)
        expo = jnp.exp((scores - high) * scale)
        total = jnp.sum(expo, axis=0, keepdims=True)
        product = lax.dot_general(
            value_rows, expo.astype(jnp.bfloat16), (((0,), (0,)), ((), ())), preferred_element_type=jnp.float32
        )
        if not diagonal:
            total = total_ref[...] * factor + total
            product = accum_ref[...] * factor + product
        high_ref[...] = high
        total_ref[...] = total
        accum_ref[...] = product

    @pl.when(step == 0)
    def _():
        fold([ref[:part, :] for ref in near_refs], [ref[part:, :] for ref in near_refs], True)

    for far_ref in far_refs:
        for block in range(far_ref.shape[0]):
            mark = far_ref[block, pl.ds(2 * pieces * part, MARK), :]
            place = jnp.max(mark.astype(jnp.float32)).astype(jnp.int32)

            @pl.when(place < own)
            def _():
                fold(
                    [far_ref[block, pl.ds(2 * piece * part, part), :] for piece in range(pieces)],
                    [far_ref[block, pl.ds((2 * piece + 1) * part, part), :] for piece in range(pieces)],
                    False,
                )

    @pl.when(step == pl.num_programs(0) - 1)
    def _():
        result = accum_ref[...] / total_ref[...]
        out_ref[...] = result.T.astype(out_ref.dtype)


def shards(queries, keys, values, block_ids):
    rows_dev, all_heads, head_width = queries.shape
    part, kv_heads = keys.shape[:2]
    head_index = lax.axis_index("head")
    pieces = lax.axis_size("head")
    blocks = lax.axis_size("seq")
    heads_out = all_heads // pieces
    own_queries = lax.dynamic_slice_in_dim(queries, head_index * heads_out, heads_out, 1)
    own_queries = own_queries.reshape(rows_dev * heads_out, head_width)
    mark = jnp.broadcast_to(block_ids.astype(jnp.bfloat16)[:, None], (MARK, head_width))
    whole = pl.BlockSpec(memory_space=pltpu.VMEM)
    packed = pl.pallas_call(
        functools.partial(pack, heads_out, all_heads // kv_heads),
        out_shape=[jax.ShapeDtypeStruct((2 * part, head_width), jnp.bfloat16)] * pieces,
        in_specs=[whole, whole],
        out_specs=[whole] * pieces,
    )(keys, values)
    near = [packed[0]] + [
        lax.ppermute(packed[shift], "head", [(i, (i + shift) % pieces) for i in range(pieces)])
        for shift in range(1, pieces)
    ]
    block = jnp.concatenate(near + [mark])
    if blocks <= PERMUTES:
        far = [
            lax.ppermute(block, "seq", [(i, (i + shift) % blocks) for i in range(blocks)])[None]
            for shift in range(1, blocks)
        ]
        unit = steps = 1
    else:
        far = [lax.all_gather(block, "seq", axis=0, tiled=False)]
        unit = math.gcd(blocks, 8)
        steps = blocks // unit
    query_rows = rows_dev * heads_out
    result = pl.pallas_call(
        functools.partial(attend, pieces, part, head_width ** (-0.5)),
        grid=(steps,),
        out_shape=jax.ShapeDtypeStruct((query_rows, head_width), jnp.bfloat16),
        in_specs=[pl.BlockSpec(memory_space=pltpu.SMEM), pl.BlockSpec((query_rows, head_width), lambda i: (0, 0))]
        + [pl.BlockSpec(near[0].shape, lambda i: (0, 0))] * pieces
        + [pl.BlockSpec((unit,) + block.shape, lambda i: (i, 0, 0))] * len(far),
        out_specs=pl.BlockSpec((query_rows, head_width), lambda i: (0, 0)),
        scratch_shapes=[
            pltpu.VMEM((1, query_rows), jnp.float32),
            pltpu.VMEM((1, query_rows), jnp.float32),
            pltpu.VMEM((head_width, query_rows), jnp.float32),
        ],
        compiler_params=pltpu.CompilerParams(vmem_limit_bytes=32 * 1024 * 1024),
    )(block_ids, own_queries, *near, *far)
    return result.reshape(rows_dev, heads_out, head_width)


def solution(mesh):
    return jax.shard_map(
        shards,
        mesh=mesh,
        in_specs=(
            P("seq", None, None),
            P(("seq", "head"), None, None),
            P(("seq", "head"), None, None),
            P("seq"),
        ),
        out_specs=P("seq", "head", None),
        check_vma=False,
    )
```

```python
import functools
import math

import jax
import jax.numpy as jnp
from jax import lax
from jax.experimental import pallas as pl
from jax.experimental.pallas import tpu as pltpu
from jax.sharding import PartitionSpec as P

MARK = 16


def pack(copies, keys_ref, values_ref, *out_refs):
    part, kv_heads = keys_ref.shape[:2]
    kv_here = lax.axis_index("head") // copies
    key_rows = [keys_ref[:, head, :] for head in range(kv_heads)]
    value_rows = [values_ref[:, head, :] for head in range(kv_heads)]
    for shift, out_ref in enumerate(out_refs):
        kv_head = lax.rem(kv_here + shift, kv_heads)
        chosen_key, chosen_value = key_rows[0], value_rows[0]
        for head in range(1, kv_heads):
            chosen_key = jnp.where(kv_head == head, key_rows[head], chosen_key)
            chosen_value = jnp.where(kv_head == head, value_rows[head], chosen_value)
        out_ref[:part, :] = chosen_key
        out_ref[part:, :] = chosen_value


def attend(pieces, copies, part, scale, own_ref, query_ref, near_ref, *refs):
    far_refs = refs[:-4]
    out_ref, high_ref, total_ref, accum_ref = refs[-4:]
    query_rows = query_ref.shape[0]
    group = query_rows // (pieces * part)
    own = own_ref[0]
    here = lax.axis_index("head")
    step = pl.program_id(0)

    def fold(key_parts, value_parts, diagonal):
        key_rows = jnp.concatenate(key_parts)
        value_rows = jnp.concatenate(value_parts)
        scores = lax.dot_general(
            key_rows, query_ref[...], (((1,), (1,)), ((), ())), preferred_element_type=jnp.float32
        )
        if diagonal:
            row = lax.broadcasted_iota(jnp.int32, scores.shape, 0)
            slot = row // part
            kv_heads = pieces // copies
            kv_from = lax.rem(here // copies + kv_heads - slot % kv_heads, kv_heads)
            copy_from = lax.rem(here % copies + copies - slot // kv_heads, copies)
            piece = kv_from * copies + copy_from
            key_at = piece * part + row % part
            query_at = lax.broadcasted_iota(jnp.int32, scores.shape, 1) // group
            scores = jnp.where(key_at <= query_at, scores, -1e30)
        high = jnp.max(scores, axis=0, keepdims=True)
        if not diagonal:
            old_high = high_ref[...]
            high = jnp.maximum(old_high, high)
            factor = jnp.exp((old_high - high) * scale)
        expo = jnp.exp((scores - high) * scale)
        total = jnp.sum(expo, axis=0, keepdims=True)
        product = lax.dot_general(
            value_rows, expo.astype(jnp.bfloat16), (((0,), (0,)), ((), ())), preferred_element_type=jnp.float32
        )
        if not diagonal:
            total = total_ref[...] * factor + total
            product = accum_ref[...] * factor + product
        high_ref[...] = high
        total_ref[...] = total
        accum_ref[...] = product

    def fold_rows(rows_ref, diagonal):
        fold(
            [rows_ref[pl.ds(2 * piece * part, part), :] for piece in range(pieces)],
            [rows_ref[pl.ds((2 * piece + 1) * part, part), :] for piece in range(pieces)],
            diagonal,
        )

    @pl.when(step == 0)
    def _():
        fold_rows(near_ref, True)

    for far_ref in far_refs:
        for block in range(far_ref.shape[0]):
            rows_ref = far_ref.at[block]
            mark = rows_ref[pl.ds(2 * pieces * part, MARK), :]
            place = jnp.max(mark.astype(jnp.float32)).astype(jnp.int32)

            @pl.when(place < own)
            def _():
                fold_rows(rows_ref, False)

    @pl.when(step == pl.num_programs(0) - 1)
    def _():
        result = accum_ref[...] / total_ref[...]
        out_ref[...] = result.T.astype(out_ref.dtype)


def shards(queries, keys, values, block_ids):
    rows_dev, all_heads, head_width = queries.shape
    part, kv_heads = keys.shape[:2]
    head_index = lax.axis_index("head")
    pieces = lax.axis_size("head")
    blocks = lax.axis_size("seq")
    heads_out = all_heads // pieces
    own_queries = lax.dynamic_slice_in_dim(queries, head_index * heads_out, heads_out, 1)
    own_queries = own_queries.reshape(rows_dev * heads_out, head_width)
    mark = jnp.broadcast_to(block_ids.astype(jnp.bfloat16)[:, None], (MARK, head_width))
    whole = pl.BlockSpec(memory_space=pltpu.VMEM)
    copies = pieces // kv_heads
    packed = pl.pallas_call(
        functools.partial(pack, copies),
        out_shape=[jax.ShapeDtypeStruct((2 * part, head_width), jnp.bfloat16)] * kv_heads,
        in_specs=[whole, whole],
        out_specs=[whole] * kv_heads,
    )(keys, values)
    held = jnp.concatenate(
        [packed[0]]
        + [
            lax.ppermute(packed[shift], "head", [(i, (i + shift * copies) % pieces) for i in range(pieces)])
            for shift in range(1, kv_heads)
        ]
    )
    block = jnp.concatenate(
        [held]
        + [
            lax.ppermute(
                held, "head", [(i, i // copies * copies + (i + shift) % copies) for i in range(pieces)]
            )
            for shift in range(1, copies)
        ]
        + [mark]
    )[None]
    if blocks == 8:
        first = lax.ppermute(block, "seq", [(i, i ^ (4 if i & 1 else 2)) for i in range(blocks)])
        pair = jnp.concatenate([block, first])
        second = lax.ppermute(pair, "seq", [(i, i ^ (2 if i & 1 else 4)) for i in range(blocks)])
        third = lax.ppermute(jnp.concatenate([pair, second]), "seq", [(i, i ^ 1) for i in range(blocks)])
        far = [first, second, third]
        steps = 1
    else:
        far = [lax.all_gather(block, "seq", axis=0, tiled=True)]
        steps = blocks // math.gcd(blocks, 8)
    query_rows = rows_dev * heads_out
    result = pl.pallas_call(
        functools.partial(attend, pieces, copies, part, head_width ** (-0.5)),
        grid=(steps,),
        out_shape=jax.ShapeDtypeStruct((query_rows, head_width), jnp.bfloat16),
        in_specs=[pl.BlockSpec(memory_space=pltpu.SMEM), pl.BlockSpec((query_rows, head_width), lambda i: (0, 0))]
        + [pl.BlockSpec(block.shape[1:], lambda i: (0, 0))]
        + [pl.BlockSpec((rows.shape[0] // steps,) + rows.shape[1:], lambda i: (i, 0, 0)) for rows in far],
        out_specs=pl.BlockSpec((query_rows, head_width), lambda i: (0, 0)),
        scratch_shapes=[
            pltpu.VMEM((1, query_rows), jnp.float32),
            pltpu.VMEM((1, query_rows), jnp.float32),
            pltpu.VMEM((head_width, query_rows), jnp.float32),
        ],
        compiler_params=pltpu.CompilerParams(vmem_limit_bytes=32 * 1024 * 1024),
    )(block_ids, own_queries, block[0], *far)
    return result.reshape(rows_dev, heads_out, head_width)


def solution(mesh):
    return jax.shard_map(
        shards,
        mesh=mesh,
        in_specs=(
            P("seq", None, None),
            P(("seq", "head"), None, None),
            P(("seq", "head"), None, None),
            P("seq"),
        ),
        out_specs=P("seq", "head", None),
        check_vma=False,
    )
```

```python
import functools
import math

import jax
import jax.numpy as jnp
from jax import lax
from jax.experimental import pallas as pl
from jax.experimental.pallas import tpu as pltpu
from jax.sharding import PartitionSpec as P

MARK = 16
LANES = 256
LOW = -1e30
HIGH = 1e30
MIB = 1024 * 1024


def pack(heads_out, group, part, pieces, keys_ref, values_ref, *out_refs):
    here = lax.axis_index("head")
    rows = keys_ref.shape[0]
    kv_heads = rows // part
    at = lax.broadcasted_iota(jnp.int32, (part, rows), 0)
    source = lax.broadcasted_iota(jnp.int32, (part, rows), 1)
    chosen = []
    for head in range(kv_heads):
        pick = jnp.where(source == at * kv_heads + head, 1.0, 0.0).astype(jnp.bfloat16)
        chosen.append(
            [
                jnp.dot(pick, ref[...], preferred_element_type=jnp.float32).astype(jnp.bfloat16)
                for ref in (keys_ref, values_ref)
            ]
        )
    for shift, out_ref in enumerate(out_refs):
        kv_head = lax.rem(here + shift, pieces) * heads_out // group
        for half in range(2):
            rows_out = chosen[0][half]
            for head in range(1, kv_heads):
                rows_out = jnp.where(kv_head == head, chosen[head][half], rows_out)
            out_ref[pl.ds(half * part, part), :] = rows_out


def attend(pieces, part, scale, first, last, counts, own_ref, query_ref, *refs):
    refs = list(refs)
    state = None if first else [refs.pop(0) for _ in range(3)]
    near_ref = refs.pop(0) if first else None
    far_refs = [refs.pop(0) for _ in counts]
    outs = refs
    query_rows, head_width = query_ref.shape
    block_rows = pieces * part
    group = query_rows // block_rows
    factor = scale * math.log2(math.e)
    here = lax.axis_index("head")
    own = own_ref[0].astype(jnp.float32)

    blocks = []
    if first:
        blocks.append((near_ref, None))
    for count, ref in zip(counts, far_refs):
        for block in range(count):
            rows_ref = ref.at[block]
            mark = rows_ref[pl.ds(2 * block_rows, MARK), :].astype(jnp.float32)[:1]
            seen = jnp.concatenate([mark] * (LANES // head_width), axis=1) < own
            blocks.append((rows_ref, seen))

    def side(rows_ref, offset):
        return jnp.concatenate(
            [rows_ref[pl.ds((2 * piece + offset) * part, part), :] for piece in range(pieces)]
        )

    keys = [side(rows_ref, 0) for rows_ref, _ in blocks]
    values = [side(rows_ref, 1).T for rows_ref, _ in blocks]

    for lane in range(0, query_rows, LANES):
        span = pl.ds(lane, LANES)
        query = query_ref[span, :]
        scores, tops = [], []
        for key_rows, (_, seen) in zip(keys, blocks):
            score = lax.dot_general(
                key_rows, query, (((1,), (1,)), ((), ())), preferred_element_type=jnp.float32
            )
            if seen is None:
                row = lax.broadcasted_iota(jnp.int32, score.shape, 0)
                piece = lax.rem(here + pieces - row // part, pieces)
                key_at = piece * part + row % part
                query_at = (lane + lax.broadcasted_iota(jnp.int32, score.shape, 1)) // group
                score = jnp.where(key_at <= query_at, score, LOW)
            top = jnp.max(score, axis=0, keepdims=True)
            scores.append(score)
            tops.append(top if seen is None else jnp.where(seen, top, LOW))
        high = functools.reduce(jnp.maximum, tops)
        if not first:
            old_high = state[0][:, span]
            high = jnp.maximum(old_high, high)
        total = accum = None
        for score, value_rows, (_, seen) in zip(scores, values, blocks):
            base = high if seen is None else jnp.where(seen, high, HIGH)
            expo = jnp.exp2((score - base) * factor)
            part_total = jnp.sum(expo, axis=0, keepdims=True)
            product = jnp.dot(value_rows, expo.astype(jnp.bfloat16), preferred_element_type=jnp.float32)
            total = part_total if total is None else total + part_total
            accum = product if accum is None else accum + product
        if not first:
            keep = jnp.exp2((old_high - high) * factor)
            total = total + state[1][:, span] * keep
            accum = accum + state[2][:, span] * keep
        if last:
            outs[0][span, :] = (accum / total).T.astype(outs[0].dtype)
        else:
            outs[0][:, span] = high
            outs[1][:, span] = total
            outs[2][:, span] = accum


def attend_call(pieces, part, own, query, state, near, far, last):
    query_rows, head_width = query.shape
    whole = pl.BlockSpec(memory_space=pltpu.VMEM)
    first = near is not None
    counts = [rows.shape[0] for rows in far]
    operands = ([near] if first else list(state)) + list(far)
    if last:
        shapes = jax.ShapeDtypeStruct((query_rows, head_width), jnp.bfloat16)
        out_specs = whole
    else:
        shapes = [
            jax.ShapeDtypeStruct((1, query_rows), jnp.float32),
            jax.ShapeDtypeStruct((1, query_rows), jnp.float32),
            jax.ShapeDtypeStruct((head_width, query_rows), jnp.float32),
        ]
        out_specs = [whole] * 3
    blocks = sum(counts) + first
    pairs = blocks * query_rows * pieces * part
    return pl.pallas_call(
        functools.partial(attend, pieces, part, head_width ** (-0.5), first, last, counts),
        out_shape=shapes,
        in_specs=[pl.BlockSpec(memory_space=pltpu.SMEM)] + [whole] * (1 + len(operands)),
        out_specs=out_specs,
        compiler_params=pltpu.CompilerParams(vmem_limit_bytes=24 * MIB),
        cost_estimate=pl.CostEstimate(
            flops=4 * pairs * head_width, bytes_accessed=2 * MIB, transcendentals=pairs
        ),
    )(own, query, *operands)


def shards(queries, keys, values, block_ids):
    rows_dev, all_heads, head_width = queries.shape
    part, kv_heads = keys.shape[:2]
    head_index = lax.axis_index("head")
    pieces = lax.axis_size("head")
    blocks = lax.axis_size("seq")
    heads_out = all_heads // pieces
    own_queries = lax.dynamic_slice_in_dim(queries, head_index * heads_out, heads_out, 1)
    own_queries = own_queries.reshape(rows_dev * heads_out, head_width)
    mark = jnp.broadcast_to(block_ids.astype(jnp.bfloat16)[:, None], (MARK, head_width))
    whole = pl.BlockSpec(memory_space=pltpu.VMEM)
    packed = pl.pallas_call(
        functools.partial(pack, heads_out, all_heads // kv_heads, part, pieces),
        out_shape=[jax.ShapeDtypeStruct((2 * part, head_width), jnp.bfloat16)] * pieces,
        in_specs=[whole, whole],
        out_specs=[whole] * pieces,
        compiler_params=pltpu.CompilerParams(vmem_limit_bytes=4 * MIB),
    )(keys.reshape(part * kv_heads, head_width), values.reshape(part * kv_heads, head_width))
    near = [packed[0]] + [
        lax.ppermute(packed[shift], "head", [(i, (i + shift) % pieces) for i in range(pieces)])
        for shift in range(1, pieces)
    ]
    block = jnp.concatenate(near + [mark])
    fold = functools.partial(attend_call, pieces, part, block_ids, own_queries)
    if blocks == 8:

        def swap(rows, flip):
            return lax.ppermute(rows, "seq", [(i, i ^ flip) for i in range(blocks)])

        sent = block[None]
        along_x, along_y, across = swap(sent, 2), swap(sent, 4), swap(sent, 6)
        other = swap(sent, 1)
        state = fold(None, block, [other], False)
        along_x, along_y, across, state = lax.optimization_barrier((along_x, along_y, across, state))
        others = [swap(rows, 1) for rows in (along_x, along_y, across)]
        state = fold(state, None, [along_x, along_y, across], False)
        result = fold(state, None, others, True)
    else:
        far = lax.all_gather(block, "seq", axis=0, tiled=False)
        unit = math.gcd(blocks, 8)
        far = far.reshape((blocks // unit, unit) + block.shape)
        state = fold(None, block, [], False)
        state, _ = lax.scan(lambda held, rows: (tuple(fold(held, None, [rows], False)), None), tuple(state), far[:-1])
        result = fold(state, None, [far[-1]], True)
    return result.reshape(rows_dev, heads_out, head_width)


def solution(mesh):
    return jax.shard_map(
        shards,
        mesh=mesh,
        in_specs=(
            P("seq", None, None),
            P(("seq", "head"), None, None),
            P(("seq", "head"), None, None),
            P("seq"),
        ),
        out_specs=P("seq", "head", None),
        check_vma=False,
    )
```

```python
import functools
import math

import jax
import jax.numpy as jnp
from jax import lax
from jax.experimental import pallas as pl
from jax.experimental.pallas import tpu as pltpu
from jax.sharding import PartitionSpec as P

MARK = 16
LANES = 256
LOW = -1e30
HIGH = 1e30
MIB = 1024 * 1024


def pack(heads_out, group, part, pieces, keys_ref, values_ref, out_ref):
    rows = keys_ref.shape[0]
    kv_heads = rows // part
    at = lax.broadcasted_iota(jnp.int32, (part, rows), 0)
    source = lax.broadcasted_iota(jnp.int32, (part, rows), 1)
    chosen = []
    for head in range(kv_heads):
        pick = jnp.where(source == at * kv_heads + head, 1.0, 0.0).astype(jnp.bfloat16)
        chosen.append(
            [
                jnp.dot(pick, ref[...], preferred_element_type=jnp.float32).astype(jnp.bfloat16)
                for ref in (keys_ref, values_ref)
            ]
        )
    for target in range(pieces):
        for half in range(2):
            out_ref[target, pl.ds(half * part, part), :] = chosen[target * heads_out // group][half]


def attend(pieces, part, scale, first, last, counts, own_ref, query_ref, *refs):
    refs = list(refs)
    state = None if first else [refs.pop(0) for _ in range(3)]
    near_ref = refs.pop(0) if first else None
    far_refs = [refs.pop(0) for _ in counts]
    outs = refs
    query_rows, head_width = query_ref.shape
    block_rows = pieces * part
    group = query_rows // block_rows
    factor = scale * math.log2(math.e)
    own = own_ref[0].astype(jnp.float32)

    blocks = []
    if first:
        blocks.append((near_ref, None))
    for count, ref in zip(counts, far_refs):
        for block in range(count):
            rows_ref = ref.at[block]
            mark = rows_ref[pl.ds(2 * block_rows, MARK), :].astype(jnp.float32)[:1]
            seen = jnp.concatenate([mark] * (LANES // head_width), axis=1) < own
            blocks.append((rows_ref, seen))

    def side(rows_ref, offset):
        return jnp.concatenate(
            [rows_ref[pl.ds((2 * piece + offset) * part, part), :] for piece in range(pieces)]
        )

    keys = [side(rows_ref, 0) for rows_ref, _ in blocks]
    values = [side(rows_ref, 1).T for rows_ref, _ in blocks]

    for lane in range(0, query_rows, LANES):
        span = pl.ds(lane, LANES)
        query = query_ref[span, :]
        scores, tops = [], []
        for key_rows, (_, seen) in zip(keys, blocks):
            score = lax.dot_general(
                key_rows, query, (((1,), (1,)), ((), ())), preferred_element_type=jnp.float32
            )
            if seen is None:
                row = lax.broadcasted_iota(jnp.int32, score.shape, 0)
                query_at = (lane + lax.broadcasted_iota(jnp.int32, score.shape, 1)) // group
                score = jnp.where(row <= query_at, score, LOW)
            top = jnp.max(score, axis=0, keepdims=True)
            scores.append(score)
            tops.append(top if seen is None else jnp.where(seen, top, LOW))
        high = functools.reduce(jnp.maximum, tops)
        if not first:
            old_high = state[0][:, span]
            high = jnp.maximum(old_high, high)
        total = accum = None
        for score, value_rows, (_, seen) in zip(scores, values, blocks):
            base = high if seen is None else jnp.where(seen, high, HIGH)
            expo = jnp.exp2((score - base) * factor)
            part_total = jnp.sum(expo, axis=0, keepdims=True)
            product = jnp.dot(value_rows, expo.astype(jnp.bfloat16), preferred_element_type=jnp.float32)
            total = part_total if total is None else total + part_total
            accum = product if accum is None else accum + product
        if not first:
            keep = jnp.exp2((old_high - high) * factor)
            total = total + state[1][:, span] * keep
            accum = accum + state[2][:, span] * keep
        if last:
            outs[0][span, :] = (accum / total).T.astype(outs[0].dtype)
        else:
            outs[0][:, span] = high
            outs[1][:, span] = total
            outs[2][:, span] = accum


def attend_call(pieces, part, own, query, state, near, far, last):
    query_rows, head_width = query.shape
    whole = pl.BlockSpec(memory_space=pltpu.VMEM)
    first = near is not None
    counts = [rows.shape[0] for rows in far]
    operands = ([near] if first else list(state)) + list(far)
    if last:
        shapes = jax.ShapeDtypeStruct((query_rows, head_width), jnp.bfloat16)
        out_specs = whole
    else:
        shapes = [
            jax.ShapeDtypeStruct((1, query_rows), jnp.float32),
            jax.ShapeDtypeStruct((1, query_rows), jnp.float32),
            jax.ShapeDtypeStruct((head_width, query_rows), jnp.float32),
        ]
        out_specs = [whole] * 3
    blocks = sum(counts) + first
    pairs = blocks * query_rows * pieces * part
    return pl.pallas_call(
        functools.partial(attend, pieces, part, head_width ** (-0.5), first, last, counts),
        out_shape=shapes,
        in_specs=[pl.BlockSpec(memory_space=pltpu.SMEM)] + [whole] * (1 + len(operands)),
        out_specs=out_specs,
        compiler_params=pltpu.CompilerParams(vmem_limit_bytes=24 * MIB),
        cost_estimate=pl.CostEstimate(
            flops=4 * pairs * head_width, bytes_accessed=2 * MIB, transcendentals=pairs
        ),
    )(own, query, *operands)


def shards(queries, keys, values, block_ids):
    rows_dev, all_heads, head_width = queries.shape
    part, kv_heads = keys.shape[:2]
    head_index = lax.axis_index("head")
    pieces = lax.axis_size("head")
    blocks = lax.axis_size("seq")
    heads_out = all_heads // pieces
    own_queries = lax.dynamic_slice_in_dim(queries, head_index * heads_out, heads_out, 1)
    own_queries = own_queries.reshape(rows_dev * heads_out, head_width)
    mark = jnp.broadcast_to(block_ids.astype(jnp.bfloat16)[:, None], (MARK, head_width))
    whole = pl.BlockSpec(memory_space=pltpu.VMEM)
    packed = pl.pallas_call(
        functools.partial(pack, heads_out, all_heads // kv_heads, part, pieces),
        out_shape=jax.ShapeDtypeStruct((pieces, 2 * part, head_width), jnp.bfloat16),
        in_specs=[whole, whole],
        out_specs=whole,
        compiler_params=pltpu.CompilerParams(vmem_limit_bytes=4 * MIB),
    )(keys.reshape(part * kv_heads, head_width), values.reshape(part * kv_heads, head_width))
    near = lax.all_to_all(packed, "head", 0, 0, tiled=False).reshape(pieces * 2 * part, head_width)
    block = jnp.concatenate([near, mark])
    fold = functools.partial(attend_call, pieces, part, block_ids, own_queries)
    if blocks == 8:

        def swap(rows, flip):
            return lax.ppermute(rows, "seq", [(i, i ^ flip) for i in range(blocks)])

        plane = lax.all_to_all(
            jnp.broadcast_to(block[None], (4,) + block.shape),
            "seq",
            0,
            0,
            axis_index_groups=[[i for i in range(blocks) if i % 2 == core] for core in range(2)],
        )
        state = fold(None, block, [], False)
        plane, state = lax.optimization_barrier((plane, state))
        others = swap(plane, 1)
        state = fold(state, None, [plane], False)
        result = fold(state, None, [others], True)
    else:
        far = lax.all_gather(block, "seq", axis=0, tiled=False)
        unit = math.gcd(blocks, 8)
        far = far.reshape((blocks // unit, unit) + block.shape)
        state = fold(None, block, [], False)
        state, _ = lax.scan(lambda held, rows: (tuple(fold(held, None, [rows], False)), None), tuple(state), far[:-1])
        result = fold(state, None, [far[-1]], True)
    return result.reshape(rows_dev, heads_out, head_width)


def solution(mesh):
    return jax.shard_map(
        shards,
        mesh=mesh,
        in_specs=(
            P("seq", None, None),
            P(("seq", "head"), None, None),
            P(("seq", "head"), None, None),
            P("seq"),
        ),
        out_specs=P("seq", "head", None),
        check_vma=False,
    )
```

```python
import functools
import math

import jax
import jax.numpy as jnp
from jax import lax
from jax.experimental import pallas as pl
from jax.experimental.pallas import tpu as pltpu
from jax.sharding import PartitionSpec as P

MARK = 16
SUBLANES = 8
LANES = 256
LOW = -1e30
HIGH = 1e30
MIB = 1024 * 1024


def pack(heads_out, group, part, pieces, keys_hbm, values_hbm, *refs):
    out_refs = refs[:pieces]
    keys_ref, values_ref, sems = refs[pieces:]
    copies = [
        pltpu.make_async_copy(source, target, sems.at[i])
        for i, (source, target) in enumerate([(keys_hbm, keys_ref), (values_hbm, values_ref)])
    ]
    for copy in copies:
        copy.start()
    here = lax.axis_index("head")
    rows = keys_ref.shape[0]
    kv_heads = rows // part
    at = lax.broadcasted_iota(jnp.int32, (part, rows), 0)
    source = lax.broadcasted_iota(jnp.int32, (part, rows), 1)
    picks = [
        jnp.where(source == at * kv_heads + head, 1.0, 0.0).astype(jnp.bfloat16) for head in range(kv_heads)
    ]
    for half, ref in enumerate((keys_ref, values_ref)):
        copies[half].wait()
        chosen = [
            jnp.dot(pick, ref[...], preferred_element_type=jnp.float32).astype(jnp.bfloat16) for pick in picks
        ]
        for shift, out_ref in enumerate(out_refs):
            kv_head = lax.rem(here + shift, pieces) * heads_out // group
            rows_out = chosen[0]
            for head in range(1, kv_heads):
                rows_out = jnp.where(kv_head == head, chosen[head], rows_out)
            out_ref[pl.ds(half * part, part), :] = rows_out


def scale_queries(scale, query_ref, out_ref):
    head_width = query_ref.shape[1]
    scaled = query_ref[...].astype(jnp.float32) * (scale * math.log2(math.e))
    coarse = scaled.astype(jnp.bfloat16)
    out_ref[:head_width, :] = coarse.T
    out_ref[head_width:, :] = (scaled - coarse.astype(jnp.float32)).astype(jnp.bfloat16).T


def attend(pieces, part, first, last, counts, own_ref, query_ref, *refs):
    refs = list(refs)
    state = None if first else [refs.pop(0) for _ in range(2)]
    near_ref = refs.pop(0) if first else None
    far_refs = [refs.pop(0) for _ in counts]
    outs = refs
    head_width = query_ref.shape[0] // 2
    query_rows = query_ref.shape[1]
    block_rows = pieces * part
    group = query_rows // block_rows
    here = lax.axis_index("head")
    own = own_ref[0].astype(jnp.float32)

    blocks = []
    if first:
        blocks.append((near_ref, None))
    for count, ref in zip(counts, far_refs):
        for block in range(count):
            rows_ref = ref.at[block]
            mark = rows_ref[pl.ds(2 * block_rows, MARK), :].astype(jnp.float32)[:SUBLANES]
            seen = jnp.concatenate([mark] * (LANES // head_width), axis=1) < own
            blocks.append((rows_ref, seen))

    def side(offset):
        return jnp.concatenate(
            [
                rows_ref[pl.ds((2 * piece + offset) * part, part), :]
                for rows_ref, _ in blocks
                for piece in range(pieces)
            ]
        )

    keys = side(0)
    keys = jnp.concatenate([keys, keys], axis=1)
    values = jnp.concatenate(
        [side(1).T, jnp.ones((MARK, len(blocks) * block_rows), jnp.bfloat16)]
    )
    spans = [pl.ds(lane, LANES) for lane in range(0, query_rows, LANES)]
    if not first:
        old = [(state[0][:, span], state[1][:, span]) for span in spans]

    results = []
    for at, span in enumerate(spans):
        scores = jnp.dot(keys, query_ref[:, span], preferred_element_type=jnp.float32)
        scores = [scores[i * block_rows : (i + 1) * block_rows] for i in range(len(blocks))]
        tops = []
        for i, (_, seen) in enumerate(blocks):
            if seen is None:
                row = lax.broadcasted_iota(jnp.int32, scores[i].shape, 0)
                piece = lax.rem(here + pieces - row // part, pieces)
                key_at = piece * part + row % part
                query_at = (at * LANES + lax.broadcasted_iota(jnp.int32, scores[i].shape, 1)) // group
                scores[i] = jnp.where(key_at <= query_at, scores[i], LOW)
            top = jnp.max(scores[i].reshape(-1, SUBLANES, LANES), axis=0)
            tops.append(top if seen is None else jnp.where(seen, top, LOW))
        high = jnp.max(functools.reduce(jnp.maximum, tops), axis=0, keepdims=True)
        if not first:
            high = jnp.maximum(old[at][0], high)
        weights = []
        for score, (_, seen) in zip(scores, blocks):
            base = high if seen is None else jnp.where(seen[:1], high, HIGH)
            weights.append(jnp.exp2(score - base).astype(jnp.bfloat16))
        accum = jnp.dot(values, jnp.concatenate(weights), preferred_element_type=jnp.float32)[
            : head_width + SUBLANES
        ]
        if not first:
            accum = accum + old[at][1] * jnp.exp2(old[at][0] - high)
        results.append((high, accum))

    for (high, accum), span in zip(results, spans):
        if last:
            inverse = 1.0 / accum[head_width : head_width + 1]
            outs[0][span, :] = (accum[:head_width] * inverse).T.astype(outs[0].dtype)
        else:
            outs[0][:, span] = high
            outs[1][:, span] = accum


def attend_call(pieces, part, own, query, state, near, far, last):
    head_width, query_rows = query.shape[0] // 2, query.shape[1]
    whole = pl.BlockSpec(memory_space=pltpu.VMEM)
    first = near is not None
    counts = [rows.shape[0] for rows in far]
    operands = ([near] if first else list(state)) + list(far)
    if last:
        shapes = jax.ShapeDtypeStruct((query_rows, head_width), jnp.bfloat16)
        out_specs = whole
    else:
        shapes = [
            jax.ShapeDtypeStruct((1, query_rows), jnp.float32),
            jax.ShapeDtypeStruct((head_width + SUBLANES, query_rows), jnp.float32),
        ]
        out_specs = [whole] * 2
    pairs = (sum(counts) + first) * query_rows * pieces * part
    return pl.pallas_call(
        functools.partial(attend, pieces, part, first, last, counts),
        out_shape=shapes,
        in_specs=[pl.BlockSpec(memory_space=pltpu.SMEM)] + [whole] * (1 + len(operands)),
        out_specs=out_specs,
        compiler_params=pltpu.CompilerParams(vmem_limit_bytes=24 * MIB),
        cost_estimate=pl.CostEstimate(
            flops=6 * pairs * head_width, bytes_accessed=2 * MIB, transcendentals=pairs
        ),
    )(own, query, *operands)


def shards(queries, keys, values, block_ids):
    rows_dev, all_heads, head_width = queries.shape
    part, kv_heads = keys.shape[:2]
    head_index = lax.axis_index("head")
    pieces = lax.axis_size("head")
    blocks = lax.axis_size("seq")
    heads_out = all_heads // pieces
    own_queries = lax.dynamic_slice_in_dim(queries, head_index * heads_out, heads_out, 1)
    own_queries = own_queries.reshape(rows_dev * heads_out, head_width)
    whole = pl.BlockSpec(memory_space=pltpu.VMEM)
    scaled = pl.pallas_call(
        functools.partial(scale_queries, head_width ** (-0.5)),
        out_shape=jax.ShapeDtypeStruct((2 * head_width, rows_dev * heads_out), jnp.bfloat16),
        in_specs=[whole],
        out_specs=whole,
        compiler_params=pltpu.CompilerParams(vmem_limit_bytes=8 * MIB),
    )(own_queries)
    mark = jnp.broadcast_to(block_ids.astype(jnp.bfloat16)[:, None], (MARK, head_width))
    packed = pl.pallas_call(
        functools.partial(pack, heads_out, all_heads // kv_heads, part, pieces),
        out_shape=[jax.ShapeDtypeStruct((2 * part, head_width), jnp.bfloat16)] * pieces,
        in_specs=[pl.BlockSpec(memory_space=pltpu.HBM)] * 2,
        out_specs=[whole] * pieces,
        scratch_shapes=[pltpu.VMEM((part * kv_heads, head_width), jnp.bfloat16)] * 2
        + [pltpu.SemaphoreType.DMA((2,))],
        compiler_params=pltpu.CompilerParams(vmem_limit_bytes=4 * MIB),
    )(keys.reshape(part * kv_heads, head_width), values.reshape(part * kv_heads, head_width))
    near = [packed[0]] + [
        lax.ppermute(packed[shift], "head", [(i, (i + shift) % pieces) for i in range(pieces)])
        for shift in range(1, pieces)
    ]
    block = jnp.concatenate(near + [mark])
    fold = functools.partial(attend_call, pieces, part, block_ids, scaled)
    if blocks == 8:

        def swap(rows, flip):
            return lax.ppermute(rows, "seq", [(i, i ^ flip) for i in range(blocks)])

        sent = block[None]
        along_x, along_y, across = swap(sent, 2), swap(sent, 4), swap(sent, 6)
        other = swap(sent, 1)
        state = fold(None, block, [other], False)
        along_x, along_y, across, state = lax.optimization_barrier((along_x, along_y, across, state))
        others = [swap(rows, 1) for rows in (along_x, along_y, across)]
        state = fold(state, None, [along_x, along_y, across], False)
        result = fold(state, None, others, True)
    else:
        far = lax.all_gather(block, "seq", axis=0, tiled=False)
        unit = math.gcd(blocks, 8)
        far = far.reshape((blocks // unit, unit) + block.shape)
        state = fold(None, block, [], False)
        state, _ = lax.scan(lambda held, rows: (tuple(fold(held, None, [rows], False)), None), tuple(state), far[:-1])
        result = fold(state, None, [far[-1]], True)
    return result.reshape(rows_dev, heads_out, head_width)


def solution(mesh):
    return jax.shard_map(
        shards,
        mesh=mesh,
        in_specs=(
            P("seq", None, None),
            P(("seq", "head"), None, None),
            P(("seq", "head"), None, None),
            P("seq"),
        ),
        out_specs=P("seq", "head", None),
        check_vma=False,
    )
```

```python
import functools
import math

import jax
import jax.numpy as jnp
from jax import lax
from jax.experimental import pallas as pl
from jax.experimental.pallas import tpu as pltpu
from jax.sharding import PartitionSpec as P

MARK = 16
SUBLANES = 8
LOW = -1e30
HIGH = 1e30
MIB = 1024 * 1024


def pack(heads_out, group, part, pieces, rows_ref, *out_refs):
    here = lax.axis_index("head")
    rows = rows_ref.shape[0] // 2
    kv_heads = rows // part
    at = lax.broadcasted_iota(jnp.int32, (part, rows), 0)
    source = lax.broadcasted_iota(jnp.int32, (part, rows), 1)
    picks = [
        jnp.where(source == at * kv_heads + head, 1.0, 0.0).astype(jnp.bfloat16) for head in range(kv_heads)
    ]
    for half in range(2):
        both = rows_ref[pl.ds(half * rows, rows), :]
        chosen = [jnp.dot(pick, both, preferred_element_type=jnp.float32).astype(jnp.bfloat16) for pick in picks]
        for shift, out_ref in enumerate(out_refs):
            kv_head = lax.rem(here + shift, pieces) * heads_out // group
            rows_out = chosen[0]
            for head in range(1, kv_heads):
                rows_out = jnp.where(kv_head == head, chosen[head], rows_out)
            out_ref[pl.ds(half * part, part), :] = rows_out


def scale_queries(scale, query_ref, out_ref):
    head_width = query_ref.shape[1]
    scaled = query_ref[...].astype(jnp.float32) * (scale * math.log2(math.e))
    coarse = scaled.astype(jnp.bfloat16)
    out_ref[:head_width, :] = coarse.T
    out_ref[head_width:, :] = (scaled - coarse.astype(jnp.float32)).astype(jnp.bfloat16).T


def attend(pieces, part, first, last, counts, own_ref, query_ref, *refs):
    refs = list(refs)
    state = None if first else [refs.pop(0) for _ in range(3)]
    near_ref = refs.pop(0) if first else None
    far_refs = [refs.pop(0) for _ in counts]
    outs = refs
    head_width = query_ref.shape[0] // 2
    query_rows = query_ref.shape[1]
    block_rows = pieces * part
    group = query_rows // block_rows
    here = lax.axis_index("head")
    own = own_ref[0].astype(jnp.float32)

    blocks = []
    if first:
        blocks.append((near_ref, None))
    for count, ref in zip(counts, far_refs):
        for block in range(count):
            rows_ref = ref.at[block]
            mark = rows_ref[pl.ds(2 * block_rows, MARK), :].astype(jnp.float32)[:SUBLANES]
            seen = jnp.concatenate([mark] * (query_rows // head_width), axis=1) < own
            blocks.append((rows_ref, seen))

    def side(offset):
        return jnp.concatenate(
            [
                rows_ref[pl.ds((2 * piece + offset) * part, part), :]
                for rows_ref, _ in blocks
                for piece in range(pieces)
            ]
        )

    keys = side(0)
    keys = jnp.concatenate([keys, keys], axis=1)
    values = side(1).T
    scores = jnp.dot(keys, query_ref[...], preferred_element_type=jnp.float32)
    scores = [scores[i * block_rows : (i + 1) * block_rows] for i in range(len(blocks))]
    tops = []
    for i, (_, seen) in enumerate(blocks):
        if seen is None:
            row = lax.broadcasted_iota(jnp.int32, scores[i].shape, 0)
            piece = lax.rem(here + pieces - row // part, pieces)
            key_at = piece * part + row % part
            query_at = lax.broadcasted_iota(jnp.int32, scores[i].shape, 1) // group
            scores[i] = jnp.where(key_at <= query_at, scores[i], LOW)
        top = jnp.max(scores[i].reshape(-1, SUBLANES, query_rows), axis=0)
        tops.append(top if seen is None else jnp.where(seen, top, LOW))
    high = jnp.max(functools.reduce(jnp.maximum, tops), axis=0, keepdims=True)
    if not first:
        old_high = state[0][...]
        high = jnp.maximum(old_high, high)
    weights, sums = [], []
    for score, (_, seen) in zip(scores, blocks):
        base = high if seen is None else jnp.where(seen[:1], high, HIGH)
        expo = jnp.exp2(score - base)
        sums.append(jnp.sum(expo.reshape(-1, SUBLANES, query_rows), axis=0))
        weights.append(expo.astype(jnp.bfloat16))
    total = jnp.sum(functools.reduce(jnp.add, sums), axis=0, keepdims=True)
    accum = jnp.dot(values, jnp.concatenate(weights), preferred_element_type=jnp.float32)
    if not first:
        keep = jnp.exp2(old_high - high)
        total = total + state[1][...] * keep
        accum = accum + state[2][...] * keep
    if last:
        outs[0][...] = (accum * (1.0 / total)).astype(outs[0].dtype).T
    else:
        outs[0][...] = high
        outs[1][...] = total
        outs[2][...] = accum


def attend_call(pieces, part, own, query, state, near, far, last):
    head_width, query_rows = query.shape[0] // 2, query.shape[1]
    whole = pl.BlockSpec(memory_space=pltpu.VMEM)
    first = near is not None
    counts = [rows.shape[0] for rows in far]
    operands = ([near] if first else list(state)) + list(far)
    if last:
        shapes = jax.ShapeDtypeStruct((query_rows, head_width), jnp.bfloat16)
        out_specs = whole
    else:
        shapes = [
            jax.ShapeDtypeStruct((1, query_rows), jnp.float32),
            jax.ShapeDtypeStruct((1, query_rows), jnp.float32),
            jax.ShapeDtypeStruct((head_width, query_rows), jnp.float32),
        ]
        out_specs = [whole] * 3
    pairs = (sum(counts) + first) * query_rows * pieces * part
    return pl.pallas_call(
        functools.partial(attend, pieces, part, first, last, counts),
        out_shape=shapes,
        in_specs=[pl.BlockSpec(memory_space=pltpu.SMEM)] + [whole] * (1 + len(operands)),
        out_specs=out_specs,
        compiler_params=pltpu.CompilerParams(vmem_limit_bytes=24 * MIB),
        cost_estimate=pl.CostEstimate(
            flops=6 * pairs * head_width, bytes_accessed=2 * MIB, transcendentals=pairs
        ),
    )(own, query, *operands)


def shards(queries, keys, values, block_ids):
    rows_dev, all_heads, head_width = queries.shape
    part, kv_heads = keys.shape[:2]
    head_index = lax.axis_index("head")
    pieces = lax.axis_size("head")
    blocks = lax.axis_size("seq")
    heads_out = all_heads // pieces
    own_queries = lax.dynamic_slice_in_dim(queries, head_index * heads_out, heads_out, 1)
    own_queries = own_queries.reshape(rows_dev * heads_out, head_width)
    whole = pl.BlockSpec(memory_space=pltpu.VMEM)
    scaled = pl.pallas_call(
        functools.partial(scale_queries, head_width ** (-0.5)),
        out_shape=jax.ShapeDtypeStruct((2 * head_width, rows_dev * heads_out), jnp.bfloat16),
        in_specs=[whole],
        out_specs=whole,
        compiler_params=pltpu.CompilerParams(vmem_limit_bytes=8 * MIB),
    )(own_queries)
    mark = jnp.broadcast_to(block_ids.astype(jnp.bfloat16)[:, None], (MARK, head_width))
    packed = pl.pallas_call(
        functools.partial(pack, heads_out, all_heads // kv_heads, part, pieces),
        out_shape=[jax.ShapeDtypeStruct((2 * part, head_width), jnp.bfloat16)] * pieces,
        in_specs=[whole],
        out_specs=[whole] * pieces,
        compiler_params=pltpu.CompilerParams(vmem_limit_bytes=4 * MIB),
    )(jnp.concatenate([keys, values]).reshape(2 * part * kv_heads, head_width))
    near = [packed[0]] + [
        lax.ppermute(packed[shift], "head", [(i, (i + shift) % pieces) for i in range(pieces)])
        for shift in range(1, pieces)
    ]
    block = jnp.concatenate(near + [mark])
    fold = functools.partial(attend_call, pieces, part, block_ids, scaled)
    if blocks == 8:

        def swap(rows, flip):
            return lax.ppermute(rows, "seq", [(i, i ^ flip) for i in range(blocks)])

        sent = block[None]
        along_x, along_y, across = swap(sent, 2), swap(sent, 4), swap(sent, 6)
        other = swap(sent, 1)
        state = fold(None, block, [other], False)
        along_x, along_y, across, state = lax.optimization_barrier((along_x, along_y, across, state))
        others = [swap(rows, 1) for rows in (along_x, along_y, across)]
        state = fold(state, None, [along_x, along_y, across], False)
        result = fold(state, None, others, True)
    else:
        far = lax.all_gather(block, "seq", axis=0, tiled=False)
        unit = math.gcd(blocks, 8)
        far = far.reshape((blocks // unit, unit) + block.shape)
        state = fold(None, block, [], False)
        state, _ = lax.scan(lambda held, rows: (tuple(fold(held, None, [rows], False)), None), tuple(state), far[:-1])
        result = fold(state, None, [far[-1]], True)
    return result.reshape(rows_dev, heads_out, head_width)


def solution(mesh):
    return jax.shard_map(
        shards,
        mesh=mesh,
        in_specs=(
            P("seq", None, None),
            P(("seq", "head"), None, None),
            P(("seq", "head"), None, None),
            P("seq"),
        ),
        out_specs=P("seq", "head", None),
        check_vma=False,
    )
```

```python
import functools
import math

import jax
import jax.numpy as jnp
from jax import lax
from jax.experimental import pallas as pl
from jax.experimental.pallas import tpu as pltpu
from jax.sharding import PartitionSpec as P

MARK = 16
COST = 0
SUBLANES = 8
LOW = -1e30
HIGH = 1e30
MIB = 1024 * 1024


def partner(here, shift, count):
    if count & (count - 1):
        return (here + shift) % count, (here + count - shift) % count
    return here ^ shift, here ^ shift


def pack(heads_out, group, part, pieces, rows_ref, *out_refs):
    here = lax.axis_index("head")
    rows = rows_ref.shape[0] // 2
    kv_heads = rows // part
    at = lax.broadcasted_iota(jnp.int32, (part, rows), 0)
    source = lax.broadcasted_iota(jnp.int32, (part, rows), 1)
    picks = [
        jnp.where(source == at * kv_heads + head, 1.0, 0.0).astype(jnp.bfloat16) for head in range(kv_heads)
    ]
    for half in range(2):
        both = rows_ref[pl.ds(half * rows, rows), :]
        chosen = [jnp.dot(pick, both, preferred_element_type=jnp.float32).astype(jnp.bfloat16) for pick in picks]
        for shift, out_ref in enumerate(out_refs):
            kv_head = partner(here, shift, pieces)[0] * heads_out // group
            rows_out = chosen[0]
            for head in range(1, kv_heads):
                rows_out = jnp.where(kv_head == head, chosen[head], rows_out)
            out_ref[pl.ds(half * part, part), :] = rows_out


def scale_queries(scale, query_ref, out_ref):
    head_width = query_ref.shape[1]
    scaled = query_ref[...].astype(jnp.float32) * (scale * math.log2(math.e))
    coarse = scaled.astype(jnp.bfloat16)
    out_ref[:head_width, :] = coarse.T
    out_ref[head_width:, :] = (scaled - coarse.astype(jnp.float32)).astype(jnp.bfloat16).T


def attend(pieces, part, first, last, counts, own_ref, query_ref, *refs):
    refs = list(refs)
    state = None if first else [refs.pop(0) for _ in range(3)]
    near_ref = refs.pop(0) if first else None
    far_refs = [refs.pop(0) for _ in counts]
    outs = refs
    head_width = query_ref.shape[0] // 2
    query_rows = query_ref.shape[1]
    block_rows = pieces * part
    group = query_rows // block_rows
    here = lax.axis_index("head")
    own = own_ref[0].astype(jnp.float32)

    blocks = []
    if first:
        blocks.append((near_ref, None))
    for count, ref in zip(counts, far_refs):
        for block in range(count):
            rows_ref = ref.at[block]
            mark = rows_ref[pl.ds(2 * block_rows, MARK), :].astype(jnp.float32)[:SUBLANES]
            seen = jnp.concatenate([mark] * (query_rows // head_width), axis=1) < own
            blocks.append((rows_ref, seen))

    def side(offset):
        return jnp.concatenate(
            [
                rows_ref[pl.ds((2 * piece + offset) * part, part), :]
                for rows_ref, _ in blocks
                for piece in range(pieces)
            ]
        )

    keys = side(0)
    keys = jnp.concatenate([keys, keys], axis=1)
    values = side(1).T
    scores = jnp.dot(keys, query_ref[...], preferred_element_type=jnp.float32)
    scores = [scores[i * block_rows : (i + 1) * block_rows] for i in range(len(blocks))]
    tops = []
    for i, (_, seen) in enumerate(blocks):
        if seen is None:
            row = lax.broadcasted_iota(jnp.int32, scores[i].shape, 0)
            piece = partner(here, row // part, pieces)[1]
            key_at = piece * part + row % part
            query_at = lax.broadcasted_iota(jnp.int32, scores[i].shape, 1) // group
            scores[i] = jnp.where(key_at <= query_at, scores[i], LOW)
        top = jnp.max(scores[i].reshape(-1, SUBLANES, query_rows), axis=0)
        tops.append(top if seen is None else jnp.where(seen, top, LOW))
    high = jnp.max(functools.reduce(jnp.maximum, tops), axis=0, keepdims=True)
    if not first:
        old_high = state[0][...]
        high = jnp.maximum(old_high, high)
    weights, sums = [], []
    for score, (_, seen) in zip(scores, blocks):
        base = high if seen is None else jnp.where(seen[:1], high, HIGH)
        expo = jnp.exp2(score - base)
        sums.append(jnp.sum(expo.reshape(-1, SUBLANES, query_rows), axis=0))
        weights.append(expo.astype(jnp.bfloat16))
    total = jnp.sum(functools.reduce(jnp.add, sums), axis=0, keepdims=True)
    accum = jnp.dot(values, jnp.concatenate(weights), preferred_element_type=jnp.float32)
    if not first:
        keep = jnp.exp2(old_high - high)
        total = total + state[1][...] * keep
        accum = accum + state[2][...] * keep
    if last:
        outs[0][...] = (accum * (1.0 / total)).astype(outs[0].dtype).T
    else:
        outs[0][...] = high
        outs[1][...] = total
        outs[2][...] = accum


def attend_call(pieces, part, own, query, state, near, far, last):
    head_width, query_rows = query.shape[0] // 2, query.shape[1]
    whole = pl.BlockSpec(memory_space=pltpu.VMEM)
    first = near is not None
    counts = [rows.shape[0] for rows in far]
    operands = ([near] if first else list(state)) + list(far)
    if last:
        shapes = jax.ShapeDtypeStruct((query_rows, head_width), jnp.bfloat16)
        out_specs = whole
    else:
        shapes = [
            jax.ShapeDtypeStruct((1, query_rows), jnp.float32),
            jax.ShapeDtypeStruct((1, query_rows), jnp.float32),
            jax.ShapeDtypeStruct((head_width, query_rows), jnp.float32),
        ]
        out_specs = [whole] * 3
    pairs = (sum(counts) + first)
    return pl.pallas_call(
        functools.partial(attend, pieces, part, first, last, counts),
        out_shape=shapes,
        in_specs=[pl.BlockSpec(memory_space=pltpu.SMEM)] + [whole] * (1 + len(operands)),
        out_specs=out_specs,
        compiler_params=pltpu.CompilerParams(vmem_limit_bytes=24 * MIB),
        cost_estimate=pl.CostEstimate(flops=COST * pairs, bytes_accessed=COST * pairs, transcendentals=0),
    )(own, query, *operands)


def shards(queries, keys, values, block_ids):
    rows_dev, all_heads, head_width = queries.shape
    part, kv_heads = keys.shape[:2]
    head_index = lax.axis_index("head")
    pieces = lax.axis_size("head")
    blocks = lax.axis_size("seq")
    heads_out = all_heads // pieces
    own_queries = lax.dynamic_slice_in_dim(queries, head_index * heads_out, heads_out, 1)
    own_queries = own_queries.reshape(rows_dev * heads_out, head_width)
    whole = pl.BlockSpec(memory_space=pltpu.VMEM)
    scaled = pl.pallas_call(
        functools.partial(scale_queries, head_width ** (-0.5)),
        out_shape=jax.ShapeDtypeStruct((2 * head_width, rows_dev * heads_out), jnp.bfloat16),
        in_specs=[whole],
        out_specs=whole,
        compiler_params=pltpu.CompilerParams(vmem_limit_bytes=8 * MIB),
    )(own_queries)
    mark = jnp.broadcast_to(block_ids.astype(jnp.bfloat16)[:, None], (MARK, head_width))
    packed = pl.pallas_call(
        functools.partial(pack, heads_out, all_heads // kv_heads, part, pieces),
        out_shape=[jax.ShapeDtypeStruct((2 * part, head_width), jnp.bfloat16)] * pieces,
        in_specs=[whole],
        out_specs=[whole] * pieces,
        compiler_params=pltpu.CompilerParams(vmem_limit_bytes=4 * MIB),
    )(jnp.concatenate([keys, values]).reshape(2 * part * kv_heads, head_width))
    near = [packed[0]] + [
        lax.ppermute(packed[shift], "head", [(i, partner(i, shift, pieces)[0]) for i in range(pieces)])
        for shift in range(1, pieces)
    ]
    block = jnp.concatenate(near + [mark])
    fold = functools.partial(attend_call, pieces, part, block_ids, scaled)
    if blocks == 8:

        def swap(rows, flip):
            return lax.ppermute(rows, "seq", [(i, i ^ flip) for i in range(blocks)])

        sent = block[None]
        across, along_y, along_x = swap(sent, 6), swap(sent, 4), swap(sent, 2)
        other = swap(sent, 1)
        state = fold(None, block, [other], False)
        along_x, along_y, state = lax.optimization_barrier((along_x, along_y, state))
        others = [swap(rows, 1) for rows in (along_x, along_y)]
        state = fold(state, None, [along_x, along_y], False)
        across, state = lax.optimization_barrier((across, state))
        other_across = swap(across, 1)
        state = fold(state, None, [across] + others, False)
        result = fold(state, None, [other_across], True)
    else:
        far = lax.all_gather(block, "seq", axis=0, tiled=False)
        unit = math.gcd(blocks, 8)
        far = far.reshape((blocks // unit, unit) + block.shape)
        state = fold(None, block, [], False)
        state, _ = lax.scan(lambda held, rows: (tuple(fold(held, None, [rows], False)), None), tuple(state), far[:-1])
        result = fold(state, None, [far[-1]], True)
    return result.reshape(rows_dev, heads_out, head_width)


def solution(mesh):
    return jax.shard_map(
        shards,
        mesh=mesh,
        in_specs=(
            P("seq", None, None),
            P(("seq", "head"), None, None),
            P(("seq", "head"), None, None),
            P("seq"),
        ),
        out_specs=P("seq", "head", None),
        check_vma=False,
    )
```

```python
import functools
import math

import jax
import jax.numpy as jnp
from jax import lax
from jax.experimental import pallas as pl
from jax.experimental.pallas import tpu as pltpu
from jax.sharding import PartitionSpec as P

MARK = 16
SUBLANES = 8
LOW = -1e30
HIGH = 1e30
MIB = 1024 * 1024


def partner(here, shift, count):
    if count & (count - 1):
        return (here + shift) % count, (here + count - shift) % count
    return here ^ shift, here ^ shift


def pack(copies, part, own_ref, rows_ref, *out_refs):
    kv_here = lax.axis_index("head") // copies
    rows = rows_ref.shape[0] // 2
    kv_heads = rows // part
    at = lax.broadcasted_iota(jnp.int32, (part, rows), 0)
    source = lax.broadcasted_iota(jnp.int32, (part, rows), 1)
    for shift, out_ref in enumerate(out_refs):
        kv_head = lax.rem(kv_here + shift, kv_heads)
        pick = jnp.where(source == at * kv_heads + kv_head, 1.0, 0.0).astype(jnp.bfloat16)
        for half in range(2):
            both = rows_ref[pl.ds(half * rows, rows), :]
            out_ref[pl.ds(half * part, part), :] = jnp.dot(
                pick, both, preferred_element_type=jnp.float32
            ).astype(jnp.bfloat16)
    mark_shape = (MARK, rows_ref.shape[1])
    place = jnp.full(mark_shape, own_ref[0], jnp.int32)
    out_refs[0][pl.ds(2 * part, MARK), :] = place.astype(jnp.float32).astype(jnp.bfloat16)


def scale_queries(scale, query_ref, out_ref):
    head_width = query_ref.shape[1]
    scaled = query_ref[...].astype(jnp.float32) * (scale * math.log2(math.e))
    coarse = scaled.astype(jnp.bfloat16)
    out_ref[:head_width, :] = coarse.T
    out_ref[head_width:, :] = (scaled - coarse.astype(jnp.float32)).astype(jnp.bfloat16).T


def attend(pieces, part, first, last, items, own_ref, query_ref, *refs):
    refs = list(refs)
    state = None if first else [refs.pop(0) for _ in range(3)]
    outs = [refs.pop() for _ in range(1 if last else 3)][::-1]
    head_width = query_ref.shape[0] // 2
    query_rows = query_ref.shape[1]
    group = query_rows // (pieces * part)
    here = lax.axis_index("head")
    own = own_ref[0].astype(jnp.float32)

    blocks = []
    for data, slot, offsets, shifts, mark in items:
        rows_ref = refs[data].at[slot]
        if shifts is None:
            mark_data, mark_slot, mark_at = mark
            place = refs[mark_data][mark_slot, pl.ds(mark_at, MARK), :].astype(jnp.float32)[:SUBLANES]
            seen = jnp.concatenate([place] * (query_rows // head_width), axis=1) < own
        else:
            seen = None
        blocks.append((rows_ref, offsets, shifts, seen))

    def side(half):
        return jnp.concatenate(
            [
                rows_ref[pl.ds(offset + half * part, part), :]
                for rows_ref, offsets, _, _ in blocks
                for offset in offsets
            ]
        )

    keys = side(0)
    keys = jnp.concatenate([keys, keys], axis=1)
    values = side(1).T
    scores = jnp.dot(keys, query_ref[...], preferred_element_type=jnp.float32)
    cuts, tops, at = [], [], 0
    for _, offsets, shifts, seen in blocks:
        score = scores[at : at + len(offsets) * part]
        at += len(offsets) * part
        if seen is None:
            parts = []
            for i, shift in enumerate(shifts):
                cut = score[i * part : (i + 1) * part]
                key_at = partner(here, shift, pieces)[1] * part + lax.broadcasted_iota(jnp.int32, cut.shape, 0)
                query_at = lax.broadcasted_iota(jnp.int32, cut.shape, 1) // group
                parts.append(jnp.where(key_at <= query_at, cut, LOW))
            score = jnp.concatenate(parts)
        top = jnp.max(score.reshape(-1, SUBLANES, query_rows), axis=0)
        cuts.append(score)
        tops.append(top if seen is None else jnp.where(seen, top, LOW))
    high = jnp.max(functools.reduce(jnp.maximum, tops), axis=0, keepdims=True)
    if not first:
        old_high = state[0][...]
        high = jnp.maximum(old_high, high)
    weights, sums = [], []
    for score, (_, _, _, seen) in zip(cuts, blocks):
        base = high if seen is None else jnp.where(seen[:1], high, HIGH)
        expo = jnp.exp2(score - base)
        sums.append(jnp.sum(expo.reshape(-1, SUBLANES, query_rows), axis=0))
        weights.append(expo.astype(jnp.bfloat16))
    total = jnp.sum(functools.reduce(jnp.add, sums), axis=0, keepdims=True)
    accum = jnp.dot(values, jnp.concatenate(weights), preferred_element_type=jnp.float32)
    if not first:
        keep = jnp.exp2(old_high - high)
        total = total + state[1][...] * keep
        accum = accum + state[2][...] * keep
    if last:
        outs[0][...] = (accum * (1.0 / total)).astype(outs[0].dtype).T
    else:
        outs[0][...] = high
        outs[1][...] = total
        outs[2][...] = accum


def attend_call(pieces, part, own, query, state, datas, items, last):
    head_width, query_rows = query.shape[0] // 2, query.shape[1]
    whole = pl.BlockSpec(memory_space=pltpu.VMEM)
    first = state is None
    operands = ([] if first else list(state)) + list(datas)
    if last:
        shapes = jax.ShapeDtypeStruct((query_rows, head_width), jnp.bfloat16)
        out_specs = whole
    else:
        shapes = [
            jax.ShapeDtypeStruct((1, query_rows), jnp.float32),
            jax.ShapeDtypeStruct((1, query_rows), jnp.float32),
            jax.ShapeDtypeStruct((head_width, query_rows), jnp.float32),
        ]
        out_specs = [whole] * 3
    return pl.pallas_call(
        functools.partial(attend, pieces, part, first, last, items),
        out_shape=shapes,
        in_specs=[pl.BlockSpec(memory_space=pltpu.SMEM)] + [whole] * (1 + len(operands)),
        out_specs=out_specs,
        compiler_params=pltpu.CompilerParams(vmem_limit_bytes=24 * MIB),
        cost_estimate=pl.CostEstimate(flops=0, bytes_accessed=0, transcendentals=0),
    )(own, query, *operands)


def shards(queries, keys, values, block_ids):
    rows_dev, all_heads, head_width = queries.shape
    part, kv_heads = keys.shape[:2]
    head_index = lax.axis_index("head")
    pieces = lax.axis_size("head")
    blocks = lax.axis_size("seq")
    heads_out = all_heads // pieces
    own_queries = lax.dynamic_slice_in_dim(queries, head_index * heads_out, heads_out, 1)
    own_queries = own_queries.reshape(rows_dev * heads_out, head_width)
    whole = pl.BlockSpec(memory_space=pltpu.VMEM)
    scaled = pl.pallas_call(
        functools.partial(scale_queries, head_width ** (-0.5)),
        out_shape=jax.ShapeDtypeStruct((2 * head_width, rows_dev * heads_out), jnp.bfloat16),
        in_specs=[whole],
        out_specs=whole,
        compiler_params=pltpu.CompilerParams(vmem_limit_bytes=8 * MIB),
    )(own_queries)
    copies = pieces // kv_heads
    own, *others = pl.pallas_call(
        functools.partial(pack, copies, part),
        out_shape=[
            jax.ShapeDtypeStruct((2 * part + (0 if shift else MARK), head_width), jnp.bfloat16)
            for shift in range(kv_heads)
        ],
        in_specs=[pl.BlockSpec(memory_space=pltpu.SMEM), whole],
        out_specs=[whole] * kv_heads,
        compiler_params=pltpu.CompilerParams(vmem_limit_bytes=4 * MIB),
    )(block_ids, jnp.concatenate([keys, values]).reshape(2 * part * kv_heads, head_width))
    fold = functools.partial(attend_call, pieces, part, block_ids, scaled)

    def along_z(rows, shift):
        return lax.ppermute(rows, "head", [(i, partner(i, shift, pieces)[0]) for i in range(pieces)])

    def along_seq(rows, flip, odd_flip=None):
        flips = (flip, flip if odd_flip is None else odd_flip)
        return lax.ppermute(rows, "seq", [(i, i ^ flips[i & 1]) for i in range(blocks)])

    if blocks == 8 and pieces == 4 and kv_heads == 2:
        far_z = along_z(others[0], 3)
        near = along_seq(own, 2, 4)
        next_z = along_z(others[0], 2)
        pair = jnp.stack([own, near])
        mine = jnp.concatenate([pair, along_seq(pair, 4, 2)])
        rest = jnp.concatenate([next_z, far_z])[None]
        rests = [along_seq(rest, 2, 4), along_seq(rest, 4, 2), along_seq(rest, 6)]
        twin = along_z(mine, 1)
        mine_other, rest_other = along_seq(mine, 1), along_seq(rest, 1)

        def small(data, mark, slots):
            return [(data, slot, (0,), None, (mark, slot, 2 * part)) for slot in slots]

        def large(data, mark, slot):
            return (data, 0, (0, 2 * part), None, (mark, slot, 2 * part))

        state = fold(
            None,
            [mine, rest],
            [(0, 0, (0,), (0,), None), (1, 0, (0, 2 * part), (2, 3), None)] + small(0, 0, range(1, 4)),
            False,
        )
        state = fold(state, [mine_other, rest_other], small(0, 0, range(4)) + [large(1, 0, 0)], False)
        *rests, twin, state = lax.optimization_barrier((*rests, twin, state))
        rests_other = [along_seq(rows, 1) for rows in rests]
        twin_other = along_seq(twin, 1)
        state = fold(
            state,
            [mine, twin] + rests,
            [(1, 0, (0,), (1,), None)]
            + small(1, 0, range(1, 4))
            + [large(2 + i, 0, 1 + i) for i in range(3)],
            False,
        )
        result = fold(
            state,
            [mine_other, twin_other] + rests_other,
            small(1, 0, range(4)) + [large(2 + i, 0, 1 + i) for i in range(3)],
            True,
        )
    else:
        payloads = jnp.stack([own[: 2 * part]] + others)
        kv_here = head_index // copies
        near = []
        for shift in range(pieces):
            kv_there = partner(head_index, shift, pieces)[0] // copies
            rows = lax.dynamic_index_in_dim(payloads, (kv_there - kv_here) % kv_heads, 0, keepdims=False)
            near.append(along_z(rows, shift) if shift else rows)
        block = jnp.concatenate(near + [own[2 * part :]])
        offsets = tuple(2 * part * i for i in range(pieces))
        far = lax.all_gather(block, "seq", axis=0, tiled=False)
        unit = math.gcd(blocks, 8)
        far = far.reshape((blocks // unit, unit) + block.shape)
        items = [(0, i, offsets, None, (0, i, 2 * part * pieces)) for i in range(unit)]
        state = fold(None, [block[None]], [(0, 0, offsets, tuple(range(pieces)), None)], False)
        state, _ = lax.scan(
            lambda held, rows: (tuple(fold(held, [rows], items, False)), None), tuple(state), far[:-1]
        )
        result = fold(state, [far[-1]], items, True)
    return result.reshape(rows_dev, heads_out, head_width)


def solution(mesh):
    return jax.shard_map(
        shards,
        mesh=mesh,
        in_specs=(
            P("seq", None, None),
            P(("seq", "head"), None, None),
            P(("seq", "head"), None, None),
            P("seq"),
        ),
        out_specs=P("seq", "head", None),
        check_vma=False,
    )
```

```python
import functools
import math

import jax
import jax.numpy as jnp
from jax import lax
from jax.experimental import pallas as pl
from jax.experimental.pallas import tpu as pltpu
from jax.sharding import PartitionSpec as P

MARK = 16
SUBLANES = 8
LOW = -1e30
HIGH = 1e30
MIB = 1024 * 1024


def pack(copies, pieces, part, own_ref, rows_ref, *out_refs):
    here = lax.axis_index("head")
    rows = rows_ref.shape[0] // 2
    kv_heads = rows // part
    at = lax.broadcasted_iota(jnp.int32, (part, rows), 0)
    source = lax.broadcasted_iota(jnp.int32, (part, rows), 1)
    picks = [
        jnp.where(source == at * kv_heads + head, 1.0, 0.0).astype(jnp.bfloat16) for head in range(kv_heads)
    ]
    for half in range(2):
        both = rows_ref[pl.ds(half * rows, rows), :]
        chosen = [jnp.dot(pick, both, preferred_element_type=jnp.float32).astype(jnp.bfloat16) for pick in picks]
        for shift, out_ref in enumerate(out_refs):
            kv_head = lax.rem(here + shift, pieces) // copies
            rows_out = chosen[0]
            for head in range(1, kv_heads):
                rows_out = jnp.where(kv_head == head, chosen[head], rows_out)
            out_ref[pl.ds(half * part, part), :] = rows_out
    place = jnp.broadcast_to(own_ref[...].astype(jnp.float32), (MARK, rows_ref.shape[1]))
    out_refs[0][pl.ds(2 * part, MARK), :] = place.astype(jnp.bfloat16)


def scale_queries(scale, query_ref, out_ref):
    head_width = query_ref.shape[1]
    scaled = query_ref[...].astype(jnp.float32) * (scale * math.log2(math.e))
    coarse = scaled.astype(jnp.bfloat16)
    out_ref[:head_width, :] = coarse.T
    out_ref[head_width:, :] = (scaled - coarse.astype(jnp.float32)).astype(jnp.bfloat16).T


def attend(pieces, part, first, last, items, own_ref, query_ref, *refs):
    refs = list(refs)
    state = None if first else [refs.pop(0) for _ in range(3)]
    outs = [refs.pop() for _ in range(1 if last else 3)][::-1]
    head_width = query_ref.shape[0] // 2
    query_rows = query_ref.shape[1]
    group = query_rows // (pieces * part)
    here = lax.axis_index("head")
    own = own_ref[0].astype(jnp.float32)

    blocks = []
    for data, slot, offsets, shifts, mark in items:
        rows_ref = refs[data].at[slot]
        if shifts is None:
            mark_data, mark_slot, mark_at = mark
            place = refs[mark_data][mark_slot, pl.ds(mark_at, MARK), :].astype(jnp.float32)[:SUBLANES]
            seen = jnp.concatenate([place] * (query_rows // head_width), axis=1) < own
        else:
            seen = None
        blocks.append((rows_ref, offsets, shifts, seen))

    def side(half):
        return jnp.concatenate(
            [
                rows_ref[pl.ds(offset + half * part, part), :]
                for rows_ref, offsets, _, _ in blocks
                for offset in offsets
            ]
        )

    keys = side(0)
    keys = jnp.concatenate([keys, keys], axis=1)
    values = side(1).T
    scores = jnp.dot(keys, query_ref[...], preferred_element_type=jnp.float32)
    cuts, tops, at = [], [], 0
    for _, offsets, shifts, seen in blocks:
        score = scores[at : at + len(offsets) * part]
        at += len(offsets) * part
        if seen is None:
            parts = []
            for i, shift in enumerate(shifts):
                cut = score[i * part : (i + 1) * part]
                key_at = lax.rem(here + pieces - shift, pieces) * part + lax.broadcasted_iota(jnp.int32, cut.shape, 0)
                query_at = lax.broadcasted_iota(jnp.int32, cut.shape, 1) // group
                parts.append(jnp.where(key_at <= query_at, cut, LOW))
            score = jnp.concatenate(parts)
        top = jnp.max(score.reshape(-1, SUBLANES, query_rows), axis=0)
        cuts.append(score)
        tops.append(top if seen is None else jnp.where(seen, top, LOW))
    high = jnp.max(functools.reduce(jnp.maximum, tops), axis=0, keepdims=True)
    if not first:
        old_high = state[0][...]
        high = jnp.maximum(old_high, high)
    weights, sums = [], []
    for score, (_, _, _, seen) in zip(cuts, blocks):
        base = high if seen is None else jnp.where(seen[:1], high, HIGH)
        expo = jnp.exp2(score - base)
        sums.append(jnp.sum(expo.reshape(-1, SUBLANES, query_rows), axis=0))
        weights.append(expo.astype(jnp.bfloat16))
    total = jnp.sum(functools.reduce(jnp.add, sums), axis=0, keepdims=True)
    accum = jnp.dot(values, jnp.concatenate(weights), preferred_element_type=jnp.float32)
    if not first:
        keep = jnp.exp2(old_high - high)
        total = total + state[1][...] * keep
        accum = accum + state[2][...] * keep
    if last:
        outs[0][...] = (accum * (1.0 / total)).astype(outs[0].dtype).T
    else:
        outs[0][...] = high
        outs[1][...] = total
        outs[2][...] = accum


def attend_call(pieces, part, own, query, state, datas, items, last, cost=0):
    head_width, query_rows = query.shape[0] // 2, query.shape[1]
    whole = pl.BlockSpec(memory_space=pltpu.VMEM)
    first = state is None
    operands = ([] if first else list(state)) + list(datas)
    if last:
        shapes = jax.ShapeDtypeStruct((query_rows, head_width), jnp.bfloat16)
        out_specs = whole
    else:
        shapes = [
            jax.ShapeDtypeStruct((1, query_rows), jnp.float32),
            jax.ShapeDtypeStruct((1, query_rows), jnp.float32),
            jax.ShapeDtypeStruct((head_width, query_rows), jnp.float32),
        ]
        out_specs = [whole] * 3
    return pl.pallas_call(
        functools.partial(attend, pieces, part, first, last, items),
        out_shape=shapes,
        in_specs=[pl.BlockSpec(memory_space=pltpu.SMEM)] + [whole] * (1 + len(operands)),
        out_specs=out_specs,
        compiler_params=pltpu.CompilerParams(vmem_limit_bytes=24 * MIB),
        cost_estimate=pl.CostEstimate(flops=cost, bytes_accessed=0, transcendentals=0),
    )(own, query, *operands)


def shards(queries, keys, values, block_ids):
    rows_dev, all_heads, head_width = queries.shape
    part, kv_heads = keys.shape[:2]
    head_index = lax.axis_index("head")
    pieces = lax.axis_size("head")
    blocks = lax.axis_size("seq")
    heads_out = all_heads // pieces
    own_queries = lax.dynamic_slice_in_dim(queries, head_index * heads_out, heads_out, 1)
    own_queries = own_queries.reshape(rows_dev * heads_out, head_width)
    whole = pl.BlockSpec(memory_space=pltpu.VMEM)
    scaled = pl.pallas_call(
        functools.partial(scale_queries, head_width ** (-0.5)),
        out_shape=jax.ShapeDtypeStruct((2 * head_width, rows_dev * heads_out), jnp.bfloat16),
        in_specs=[whole],
        out_specs=whole,
        compiler_params=pltpu.CompilerParams(vmem_limit_bytes=8 * MIB),
    )(own_queries)
    own, *payloads = pl.pallas_call(
        functools.partial(pack, pieces // kv_heads, pieces, part),
        out_shape=[
            jax.ShapeDtypeStruct((2 * part + (0 if shift else MARK), head_width), jnp.bfloat16)
            for shift in range(pieces)
        ],
        in_specs=[whole, whole],
        out_specs=[whole] * pieces,
        compiler_params=pltpu.CompilerParams(vmem_limit_bytes=4 * MIB),
    )(block_ids.reshape(1, 1), jnp.concatenate([keys, values]).reshape(2 * part * kv_heads, head_width))
    near = [
        lax.ppermute(rows, "head", [(i, (i + shift + 1) % pieces) for i in range(pieces)])
        for shift, rows in enumerate(payloads)
    ]
    rest = jnp.concatenate(near)
    fold = functools.partial(attend_call, pieces, part, block_ids, scaled)
    shifts = tuple(range(pieces))
    offsets = tuple(2 * part * i for i in range(pieces))

    def swap(rows, flip):
        return lax.ppermute(rows, "seq", [(i, i ^ flip) for i in range(blocks)])

    if blocks == 8:
        rest = rest[None]
        mine = jnp.stack([own] + [swap(own, flip) for flip in (2, 4, 6)])
        rests = [swap(rest, flip) for flip in (2, 4, 6)]

        def small(data, slots):
            return [(data, slot, (0,), None, (data, slot, 2 * part)) for slot in slots]

        def large(data, mark, slot):
            return (data, 0, offsets[:-1], None, (mark, slot, 2 * part))

        state = fold(
            None,
            [mine, rest],
            [(0, 0, (0,), shifts[:1], None), (1, 0, offsets[:-1], shifts[1:], None)] + small(0, range(1, 4)),
            False,
            1000000000,
        )
        mine_other, rest_other = swap(mine, 1), swap(rest, 1)
        state = fold(state, [mine_other, rest_other], small(0, range(4)) + [large(1, 0, 0)], False)
        *rests, state = lax.optimization_barrier((*rests, state))
        rests_other = [swap(rows, 1) for rows in rests]
        state = fold(state, [mine] + rests, [large(i, 0, i) for i in range(1, 4)], False)
        result = fold(state, [mine_other] + rests_other, [large(i, 0, i) for i in range(1, 4)], True)
    else:
        block = jnp.concatenate([own[: 2 * part], rest, own[2 * part :]])
        far = lax.all_gather(block, "seq", axis=0, tiled=False)
        unit = math.gcd(blocks, 8)
        far = far.reshape((blocks // unit, unit) + block.shape)
        items = [(0, i, offsets, None, (0, i, 2 * part * pieces)) for i in range(unit)]
        state = fold(None, [block[None]], [(0, 0, offsets, shifts, None)], False)
        state, _ = lax.scan(
            lambda held, rows: (tuple(fold(held, [rows], items, False)), None), tuple(state), far[:-1]
        )
        result = fold(state, [far[-1]], items, True)
    return result.reshape(rows_dev, heads_out, head_width)


def solution(mesh):
    return jax.shard_map(
        shards,
        mesh=mesh,
        in_specs=(
            P("seq", None, None),
            P(("seq", "head"), None, None),
            P(("seq", "head"), None, None),
            P("seq"),
        ),
        out_specs=P("seq", "head", None),
        check_vma=False,
    )
```

```python
import functools
import math

import jax
import jax.numpy as jnp
from jax import lax
from jax.experimental import pallas as pl
from jax.experimental.pallas import tpu as pltpu
from jax.sharding import PartitionSpec as P

MARK = 16
SUBLANES = 8
LOW = -1e30
HIGH = 1e30
MIB = 1024 * 1024


def partner(here, shift, count):
    if count & (count - 1):
        return (here + shift) % count, (here + count - shift) % count
    return here ^ shift, here ^ shift


def pack(copies, pieces, part, rows_ref, *out_refs):
    here = lax.axis_index("head")
    rows = rows_ref.shape[0] // 2
    kv_heads = rows // part
    at = lax.broadcasted_iota(jnp.int32, (part, rows), 0)
    source = lax.broadcasted_iota(jnp.int32, (part, rows), 1)
    picks = [
        jnp.where(source == at * kv_heads + head, 1.0, 0.0).astype(jnp.bfloat16) for head in range(kv_heads)
    ]
    for half in range(2):
        both = rows_ref[pl.ds(half * rows, rows), :]
        chosen = [jnp.dot(pick, both, preferred_element_type=jnp.float32).astype(jnp.bfloat16) for pick in picks]
        for shift, out_ref in enumerate(out_refs):
            kv_head = partner(here, shift, pieces)[0] // copies
            rows_out = chosen[0]
            for head in range(1, kv_heads):
                rows_out = jnp.where(kv_head == head, chosen[head], rows_out)
            out_ref[pl.ds(half * part, part), :] = rows_out


def scale_queries(scale, query_ref, out_ref):
    head_width = query_ref.shape[1]
    scaled = query_ref[...].astype(jnp.float32) * (scale * math.log2(math.e))
    coarse = scaled.astype(jnp.bfloat16)
    out_ref[:head_width, :] = coarse.T
    out_ref[head_width:, :] = (scaled - coarse.astype(jnp.float32)).astype(jnp.bfloat16).T


def attend(pieces, part, first, last, items, own_ref, query_ref, *refs):
    refs = list(refs)
    state = None if first else [refs.pop(0) for _ in range(3)]
    outs = [refs.pop() for _ in range(1 if last else 3)][::-1]
    head_width = query_ref.shape[0] // 2
    query_rows = query_ref.shape[1]
    group = query_rows // (pieces * part)
    here = lax.axis_index("head")
    own = own_ref[0].astype(jnp.float32)

    blocks = []
    for data, slot, offsets, shifts, mark in items:
        rows_ref = refs[data].at[slot]
        if shifts is None:
            mark_data, mark_slot, mark_at = mark
            place = refs[mark_data][mark_slot, pl.ds(mark_at, MARK), :].astype(jnp.float32)[:SUBLANES]
            seen = jnp.concatenate([place] * (query_rows // head_width), axis=1) < own
        else:
            seen = None
        blocks.append((rows_ref, offsets, shifts, seen))

    def side(half):
        return jnp.concatenate(
            [
                rows_ref[pl.ds(offset + half * part, part), :]
                for rows_ref, offsets, _, _ in blocks
                for offset in offsets
            ]
        )

    keys = side(0)
    keys = jnp.concatenate([keys, keys], axis=1)
    values = side(1).T
    scores = jnp.dot(keys, query_ref[...], preferred_element_type=jnp.float32)
    cuts, tops, at = [], [], 0
    for _, offsets, shifts, seen in blocks:
        score = scores[at : at + len(offsets) * part]
        at += len(offsets) * part
        if seen is None:
            parts = []
            for i, shift in enumerate(shifts):
                cut = score[i * part : (i + 1) * part]
                key_at = partner(here, shift, pieces)[1] * part + lax.broadcasted_iota(jnp.int32, cut.shape, 0)
                query_at = lax.broadcasted_iota(jnp.int32, cut.shape, 1) // group
                parts.append(jnp.where(key_at <= query_at, cut, LOW))
            score = jnp.concatenate(parts)
        top = jnp.max(score.reshape(-1, SUBLANES, query_rows), axis=0)
        cuts.append(score)
        tops.append(top if seen is None else jnp.where(seen, top, LOW))
    high = jnp.max(functools.reduce(jnp.maximum, tops), axis=0, keepdims=True)
    if not first:
        old_high = state[0][...]
        high = jnp.maximum(old_high, high)
    weights, sums = [], []
    for score, (_, _, _, seen) in zip(cuts, blocks):
        base = high if seen is None else jnp.where(seen[:1], high, HIGH)
        expo = jnp.exp2(score - base)
        sums.append(jnp.sum(expo.reshape(-1, SUBLANES, query_rows), axis=0))
        weights.append(expo.astype(jnp.bfloat16))
    total = jnp.sum(functools.reduce(jnp.add, sums), axis=0, keepdims=True)
    accum = jnp.dot(values, jnp.concatenate(weights), preferred_element_type=jnp.float32)
    if not first:
        keep = jnp.exp2(old_high - high)
        total = total + state[1][...] * keep
        accum = accum + state[2][...] * keep
    if last:
        outs[0][...] = (accum * (1.0 / total)).astype(outs[0].dtype).T
    else:
        outs[0][...] = high
        outs[1][...] = total
        outs[2][...] = accum


def attend_call(pieces, part, own, query, state, datas, items, last, cost=0):
    head_width, query_rows = query.shape[0] // 2, query.shape[1]
    whole = pl.BlockSpec(memory_space=pltpu.VMEM)
    first = state is None
    operands = ([] if first else list(state)) + list(datas)
    if last:
        shapes = jax.ShapeDtypeStruct((query_rows, head_width), jnp.bfloat16)
        out_specs = whole
    else:
        shapes = [
            jax.ShapeDtypeStruct((1, query_rows), jnp.float32),
            jax.ShapeDtypeStruct((1, query_rows), jnp.float32),
            jax.ShapeDtypeStruct((head_width, query_rows), jnp.float32),
        ]
        out_specs = [whole] * 3
    return pl.pallas_call(
        functools.partial(attend, pieces, part, first, last, items),
        out_shape=shapes,
        in_specs=[pl.BlockSpec(memory_space=pltpu.SMEM)] + [whole] * (1 + len(operands)),
        out_specs=out_specs,
        compiler_params=pltpu.CompilerParams(vmem_limit_bytes=24 * MIB),
        cost_estimate=pl.CostEstimate(flops=cost, bytes_accessed=0, transcendentals=0),
    )(own, query, *operands)


def shards(queries, keys, values, block_ids):
    rows_dev, all_heads, head_width = queries.shape
    part, kv_heads = keys.shape[:2]
    head_index = lax.axis_index("head")
    pieces = lax.axis_size("head")
    blocks = lax.axis_size("seq")
    heads_out = all_heads // pieces
    own_queries = lax.dynamic_slice_in_dim(queries, head_index * heads_out, heads_out, 1)
    own_queries = own_queries.reshape(rows_dev * heads_out, head_width)
    whole = pl.BlockSpec(memory_space=pltpu.VMEM)
    scaled = pl.pallas_call(
        functools.partial(scale_queries, head_width ** (-0.5)),
        out_shape=jax.ShapeDtypeStruct((2 * head_width, rows_dev * heads_out), jnp.bfloat16),
        in_specs=[whole],
        out_specs=whole,
        compiler_params=pltpu.CompilerParams(vmem_limit_bytes=8 * MIB),
    )(own_queries)
    payloads = pl.pallas_call(
        functools.partial(pack, pieces // kv_heads, pieces, part),
        out_shape=[jax.ShapeDtypeStruct((2 * part, head_width), jnp.bfloat16)] * pieces,
        in_specs=[whole],
        out_specs=[whole] * pieces,
        compiler_params=pltpu.CompilerParams(vmem_limit_bytes=4 * MIB),
    )(jnp.concatenate([keys, values]).reshape(2 * part * kv_heads, head_width))
    mark = jnp.broadcast_to(block_ids.astype(jnp.bfloat16)[:, None], (MARK, head_width))
    near = [payloads[0]] + [
        lax.ppermute(payloads[shift], "head", [(i, partner(i, shift, pieces)[0]) for i in range(pieces)])
        for shift in range(pieces - 1, 0, -1)
    ][::-1]
    fold = functools.partial(attend_call, pieces, part, block_ids, scaled)
    step = 2 * part

    def hop(rows, flip, odd_flip=None):
        flips = (flip, flip if odd_flip is None else odd_flip)
        return lax.ppermute(rows, "seq", [(i, i ^ flips[i & 1]) for i in range(blocks)])

    if blocks == 8 and pieces == 4:
        early = jnp.concatenate([near[0], mark])[None]
        early_pair = jnp.concatenate([early, hop(early, 2, 4)])
        early_far = hop(early_pair, 4, 2)
        late = jnp.concatenate(near[1:])[None]
        late_next = hop(late, 2, 4)
        early_all = jnp.concatenate([early_pair, early_far])
        late_far = hop(jnp.concatenate([late, late_next]), 4, 2)

        def small(data, slots):
            return [(data, slot, (0,), None, (data, slot, step)) for slot in slots]

        def large(data, mark_data, slots, base=0):
            return [
                (data, slot - base, (0, step, 2 * step), None, (mark_data, slot, step)) for slot in slots
            ]

        state = fold(
            None,
            [early_all, late],
            [(0, 0, (0,), (0,), None), (1, 0, (0, step, 2 * step), (1, 2, 3), None)] + small(0, range(1, 4)),
            False,
        )
        early_other, late_other = hop(early_all, 1), hop(late, 1)
        state = fold(state, [early_other, late_other], small(0, range(4)) + large(1, 0, [0]), False)
        late_next_other = hop(late_next, 1)
        state = fold(
            state,
            [early_all, early_other, late_next, late_next_other],
            large(2, 0, [1], 1) + large(3, 1, [1], 1),
            False,
        )
        late_far, state = lax.optimization_barrier((late_far, state))
        late_far_other = hop(late_far, 1)
        state = fold(state, [early_all, late_far], large(1, 0, [2, 3], 2), False)
        result = fold(state, [early_other, late_far_other], large(1, 0, [2, 3], 2), True)
    else:
        block = jnp.concatenate(near + [mark])
        offsets = tuple(step * i for i in range(pieces))
        far = lax.all_gather(block, "seq", axis=0, tiled=False)
        unit = math.gcd(blocks, 8)
        far = far.reshape((blocks // unit, unit) + block.shape)
        each = [(0, i, offsets, None, (0, i, step * pieces)) for i in range(unit)]
        state = fold(None, [block[None]], [(0, 0, offsets, tuple(range(pieces)), None)], False)
        state, _ = lax.scan(
            lambda held, rows: (tuple(fold(held, [rows], each, False)), None), tuple(state), far[:-1]
        )
        result = fold(state, [far[-1]], each, True)
    return result.reshape(rows_dev, heads_out, head_width)


def solution(mesh):
    return jax.shard_map(
        shards,
        mesh=mesh,
        in_specs=(
            P("seq", None, None),
            P(("seq", "head"), None, None),
            P(("seq", "head"), None, None),
            P("seq"),
        ),
        out_specs=P("seq", "head", None),
        check_vma=False,
    )
```

```python
import functools
import math

import jax
import jax.numpy as jnp
from jax import lax
from jax.experimental import pallas as pl
from jax.experimental.pallas import tpu as pltpu
from jax.sharding import PartitionSpec as P

MARK = 16
SUBLANES = 8
LOW = -1e30
HIGH = 1e30
MIB = 1024 * 1024


def pack(copies, pieces, part, kv_heads, rows_ref, *out_refs):
    here = lax.axis_index("head")
    rows = part * kv_heads
    at = lax.broadcasted_iota(jnp.int32, (part, rows), 0)
    source = lax.broadcasted_iota(jnp.int32, (part, rows), 1)
    picks = [
        jnp.where(source == at * kv_heads + head, 1.0, 0.0).astype(jnp.bfloat16) for head in range(kv_heads)
    ]
    for half in range(2):
        both = rows_ref[pl.ds(half * rows, rows), :]
        chosen = [jnp.dot(pick, both, preferred_element_type=jnp.float32).astype(jnp.bfloat16) for pick in picks]
        for shift, out_ref in enumerate(out_refs):
            kv_head = lax.rem(here + shift, pieces) // copies
            rows_out = chosen[0]
            for head in range(1, kv_heads):
                rows_out = jnp.where(kv_head == head, chosen[head], rows_out)
            out_ref[pl.ds(half * part, part), :] = rows_out


def scale_queries(scale, query_ref, out_ref):
    head_width = query_ref.shape[1]
    scaled = query_ref[...].astype(jnp.float32) * (scale * math.log2(math.e))
    coarse = scaled.astype(jnp.bfloat16)
    out_ref[:head_width, :] = coarse.T
    out_ref[head_width:, :] = (scaled - coarse.astype(jnp.float32)).astype(jnp.bfloat16).T


def attend(pieces, part, first, last, items, own_ref, query_ref, *refs):
    refs = list(refs)
    state = None if first else [refs.pop(0) for _ in range(3)]
    outs = [refs.pop() for _ in range(1 if last else 3)][::-1]
    head_width = query_ref.shape[0] // 2
    query_rows = query_ref.shape[1]
    group = query_rows // (pieces * part)
    here = lax.axis_index("head")
    own = own_ref[pl.ds(2 * part, MARK), :].astype(jnp.float32)[:SUBLANES]
    own = jnp.concatenate([own] * (query_rows // head_width), axis=1)

    blocks = []
    for data, slot, offsets, shifts, mark in items:
        rows_ref = refs[data].at[slot]
        if shifts is None:
            mark_data, mark_slot, mark_at = mark
            place = refs[mark_data][mark_slot, pl.ds(mark_at, MARK), :].astype(jnp.float32)[:SUBLANES]
            seen = jnp.concatenate([place] * (query_rows // head_width), axis=1) < own
        else:
            seen = None
        blocks.append((rows_ref, offsets, shifts, seen))

    def side(half):
        return jnp.concatenate(
            [
                rows_ref[pl.ds(offset + half * part, part), :]
                for rows_ref, offsets, _, _ in blocks
                for offset in offsets
            ]
        )

    keys = side(0)
    keys = jnp.concatenate([keys, keys], axis=1)
    values = side(1).T
    scores = jnp.dot(keys, query_ref[...], preferred_element_type=jnp.float32)
    cuts, tops, at = [], [], 0
    for _, offsets, shifts, seen in blocks:
        score = scores[at : at + len(offsets) * part]
        at += len(offsets) * part
        if seen is None:
            parts = []
            for i, shift in enumerate(shifts):
                cut = score[i * part : (i + 1) * part]
                key_at = lax.rem(here + pieces - shift, pieces) * part + lax.broadcasted_iota(jnp.int32, cut.shape, 0)
                query_at = lax.broadcasted_iota(jnp.int32, cut.shape, 1) // group
                parts.append(jnp.where(key_at <= query_at, cut, LOW))
            score = jnp.concatenate(parts)
        top = jnp.max(score.reshape(-1, SUBLANES, query_rows), axis=0)
        cuts.append(score)
        tops.append(top if seen is None else jnp.where(seen, top, LOW))
    high = jnp.max(functools.reduce(jnp.maximum, tops), axis=0, keepdims=True)
    if not first:
        old_high = state[0][...]
        high = jnp.maximum(old_high, high)
    weights, sums = [], []
    for score, (_, _, _, seen) in zip(cuts, blocks):
        base = high if seen is None else jnp.where(seen[:1], high, HIGH)
        expo = jnp.exp2(score - base)
        sums.append(jnp.sum(expo.reshape(-1, SUBLANES, query_rows), axis=0))
        weights.append(expo.astype(jnp.bfloat16))
    total = jnp.sum(functools.reduce(jnp.add, sums), axis=0, keepdims=True)
    accum = jnp.dot(values, jnp.concatenate(weights), preferred_element_type=jnp.float32)
    if not first:
        keep = jnp.exp2(old_high - high)
        total = total + state[1][...] * keep
        accum = accum + state[2][...] * keep
    if last:
        outs[0][...] = (accum * (1.0 / total)).astype(outs[0].dtype).T
    else:
        outs[0][...] = high
        outs[1][...] = total
        outs[2][...] = accum


def attend_call(pieces, part, own, query, state, datas, items, last, cost=0):
    head_width, query_rows = query.shape[0] // 2, query.shape[1]
    whole = pl.BlockSpec(memory_space=pltpu.VMEM)
    first = state is None
    operands = ([] if first else list(state)) + list(datas)
    if last:
        shapes = jax.ShapeDtypeStruct((query_rows, head_width), jnp.bfloat16)
        out_specs = whole
    else:
        shapes = [
            jax.ShapeDtypeStruct((1, query_rows), jnp.float32),
            jax.ShapeDtypeStruct((1, query_rows), jnp.float32),
            jax.ShapeDtypeStruct((head_width, query_rows), jnp.float32),
        ]
        out_specs = [whole] * 3
    return pl.pallas_call(
        functools.partial(attend, pieces, part, first, last, items),
        out_shape=shapes,
        in_specs=[whole] * (2 + len(operands)),
        out_specs=out_specs,
        compiler_params=pltpu.CompilerParams(vmem_limit_bytes=24 * MIB),
        cost_estimate=pl.CostEstimate(flops=cost, bytes_accessed=0, transcendentals=0),
    )(own, query, *operands)


def shards(queries, keys, values, block_ids):
    rows_dev, all_heads, head_width = queries.shape
    part, kv_heads = keys.shape[:2]
    head_index = lax.axis_index("head")
    pieces = lax.axis_size("head")
    blocks = lax.axis_size("seq")
    heads_out = all_heads // pieces
    own_queries = lax.dynamic_slice_in_dim(queries, head_index * heads_out, heads_out, 1)
    own_queries = own_queries.reshape(rows_dev * heads_out, head_width)
    whole = pl.BlockSpec(memory_space=pltpu.VMEM)
    scaled = pl.pallas_call(
        functools.partial(scale_queries, head_width ** (-0.5)),
        out_shape=jax.ShapeDtypeStruct((2 * head_width, rows_dev * heads_out), jnp.bfloat16),
        in_specs=[whole],
        out_specs=whole,
        compiler_params=pltpu.CompilerParams(vmem_limit_bytes=8 * MIB),
    )(own_queries)
    own, *payloads = pl.pallas_call(
        functools.partial(pack, pieces // kv_heads, pieces, part, kv_heads),
        out_shape=[jax.ShapeDtypeStruct((2 * part, head_width), jnp.bfloat16)] * pieces,
        in_specs=[whole],
        out_specs=[whole] * pieces,
        compiler_params=pltpu.CompilerParams(vmem_limit_bytes=4 * MIB),
    )(jnp.concatenate([keys, values]).reshape(2 * part * kv_heads, head_width))
    mark = jnp.broadcast_to(block_ids.astype(jnp.bfloat16)[:, None], (MARK, head_width))
    own = jnp.concatenate([own, mark])
    near = [
        lax.ppermute(rows, "head", [(i, (i + shift + 1) % pieces) for i in range(pieces)])
        for shift, rows in enumerate(payloads)
    ]
    rest = jnp.concatenate(near)
    fold = functools.partial(attend_call, pieces, part, own, scaled)
    shifts = tuple(range(pieces))
    offsets = tuple(2 * part * i for i in range(pieces))

    def swap(rows, flip):
        return lax.ppermute(rows, "seq", [(i, i ^ flip) for i in range(blocks)])

    if blocks == 8:
        rest = rest[None]
        mine = jnp.stack([own] + [swap(own, flip) for flip in (2, 4, 6)])
        rests = [swap(rest, flip) for flip in (2, 4, 6)]

        def small(data, slots):
            return [(data, slot, (0,), None, (data, slot, 2 * part)) for slot in slots]

        def large(data, mark, slot):
            return (data, 0, offsets[:-1], None, (mark, slot, 2 * part))

        state = fold(
            None,
            [mine, rest],
            [(0, 0, (0,), shifts[:1], None), (1, 0, offsets[:-1], shifts[1:], None)] + small(0, range(1, 4)),
            False,
            1000000000,
        )
        mine, rest = lax.optimization_barrier((mine, rest))
        mine_other, rest_other = swap(mine, 1), swap(rest, 1)
        state = fold(state, [mine_other, rest_other], small(0, range(4)) + [large(1, 0, 0)], False)
        along_x, along_y, across = rests
        along_x, along_y, state = lax.optimization_barrier((along_x, along_y, state))
        others = [swap(rows, 1) for rows in (along_x, along_y)]
        state = fold(state, [mine, along_x, along_y], [large(i, 0, i) for i in (1, 2)], False)
        across, state = lax.optimization_barrier((across, state))
        other_across = swap(across, 1)
        state = fold(
            state,
            [mine, mine_other, across] + others,
            [large(2, 0, 3)] + [large(2 + i, 1, i) for i in (1, 2)],
            False,
        )
        result = fold(state, [mine_other, other_across], [large(1, 0, 3)], True)
    else:
        block = jnp.concatenate([own[: 2 * part], rest, own[2 * part :]])
        far = lax.all_gather(block, "seq", axis=0, tiled=False)
        unit = math.gcd(blocks, 8)
        far = far.reshape((blocks // unit, unit) + block.shape)
        items = [(0, i, offsets, None, (0, i, 2 * part * pieces)) for i in range(unit)]
        state = fold(None, [block[None]], [(0, 0, offsets, shifts, None)], False)
        state, _ = lax.scan(
            lambda held, rows: (tuple(fold(held, [rows], items, False)), None), tuple(state), far[:-1]
        )
        result = fold(state, [far[-1]], items, True)
    return result.reshape(rows_dev, heads_out, head_width)


def solution(mesh):
    return jax.shard_map(
        shards,
        mesh=mesh,
        in_specs=(
            P("seq", None, None),
            P(("seq", "head"), None, None),
            P(("seq", "head"), None, None),
            P("seq"),
        ),
        out_specs=P("seq", "head", None),
        check_vma=False,
    )
```

```python
import functools
import math

import jax
import jax.numpy as jnp
from jax import lax
from jax.experimental import pallas as pl
from jax.experimental.pallas import tpu as pltpu
from jax.sharding import PartitionSpec as P

MARK = 16
SUBLANES = 8
FINAL = 256
LOW = -1e30
HIGH = 1e30
MIB = 1024 * 1024


def pack(copies, pieces, part, kv_heads, rows_ref, *out_refs):
    here = lax.axis_index("head")
    rows = part * kv_heads
    at = lax.broadcasted_iota(jnp.int32, (part, rows), 0)
    source = lax.broadcasted_iota(jnp.int32, (part, rows), 1)
    picks = [
        jnp.where(source == at * kv_heads + head, 1.0, 0.0).astype(jnp.bfloat16) for head in range(kv_heads)
    ]
    for half in range(2):
        both = rows_ref[pl.ds(half * rows, rows), :]
        chosen = [jnp.dot(pick, both, preferred_element_type=jnp.float32).astype(jnp.bfloat16) for pick in picks]
        for shift, out_ref in enumerate(out_refs):
            kv_head = lax.rem(here + shift, pieces) // copies
            rows_out = chosen[0]
            for head in range(1, kv_heads):
                rows_out = jnp.where(kv_head == head, chosen[head], rows_out)
            out_ref[pl.ds(half * part, part), :] = rows_out


def scale_queries(scale, query_ref, out_ref):
    head_width = query_ref.shape[1]
    scaled = query_ref[...].astype(jnp.float32) * (scale * math.log2(math.e))
    coarse = scaled.astype(jnp.bfloat16)
    out_ref[:head_width, :] = coarse.T
    out_ref[head_width:, :] = (scaled - coarse.astype(jnp.float32)).astype(jnp.bfloat16).T


def attend(pieces, part, first, last, items, own_ref, query_ref, *refs):
    refs = list(refs)
    state = None if first else [refs.pop(0) for _ in range(3)]
    outs = [refs.pop() for _ in range(3)][::-1]
    head_width = query_ref.shape[0] // 2
    query_rows = query_ref.shape[1]
    group = query_rows // (pieces * part)
    here = lax.axis_index("head")
    own = own_ref[pl.ds(2 * part, MARK), :].astype(jnp.float32)[:SUBLANES]
    own = jnp.concatenate([own] * (query_rows // head_width), axis=1)

    blocks = []
    for data, slot, offsets, shifts, mark in items:
        rows_ref = refs[data].at[slot]
        if shifts is None:
            mark_data, mark_slot, mark_at = mark
            place = refs[mark_data][mark_slot, pl.ds(mark_at, MARK), :].astype(jnp.float32)[:SUBLANES]
            seen = jnp.concatenate([place] * (query_rows // head_width), axis=1) < own
        else:
            seen = None
        blocks.append((rows_ref, offsets, shifts, seen))

    def side(half):
        return jnp.concatenate(
            [
                rows_ref[pl.ds(offset + half * part, part), :]
                for rows_ref, offsets, _, _ in blocks
                for offset in offsets
            ]
        )

    keys = side(0)
    keys = jnp.concatenate([keys, keys], axis=1)
    values = side(1).T
    scores = jnp.dot(keys, query_ref[...], preferred_element_type=jnp.float32)
    cuts, tops, at = [], [], 0
    for _, offsets, shifts, seen in blocks:
        score = scores[at : at + len(offsets) * part]
        at += len(offsets) * part
        if seen is None:
            parts = []
            for i, shift in enumerate(shifts):
                cut = score[i * part : (i + 1) * part]
                key_at = lax.rem(here + pieces - shift, pieces) * part + lax.broadcasted_iota(jnp.int32, cut.shape, 0)
                query_at = lax.broadcasted_iota(jnp.int32, cut.shape, 1) // group
                parts.append(jnp.where(key_at <= query_at, cut, LOW))
            score = jnp.concatenate(parts)
        top = jnp.max(score.reshape(-1, SUBLANES, query_rows), axis=0)
        cuts.append(score)
        tops.append(top if seen is None else jnp.where(seen, top, LOW))
    high = jnp.max(functools.reduce(jnp.maximum, tops), axis=0, keepdims=True)
    if not first:
        old_high = state[0][...]
        high = jnp.maximum(old_high, high)
    weights, sums = [], []
    for score, (_, _, _, seen) in zip(cuts, blocks):
        base = high if seen is None else jnp.where(seen[:1], high, HIGH)
        expo = jnp.exp2(score - base)
        sums.append(jnp.sum(expo.reshape(-1, SUBLANES, query_rows), axis=0))
        weights.append(expo.astype(jnp.bfloat16))
    total = jnp.sum(functools.reduce(jnp.add, sums), axis=0, keepdims=True)
    accum = jnp.dot(values, jnp.concatenate(weights), preferred_element_type=jnp.float32)
    if not first:
        keep = jnp.exp2(old_high - high)
        total = total + state[1][...] * keep
        accum = accum + state[2][...] * keep
    if last:
        out_hbm, out_ref, sems = outs
        inverse = 1.0 / total
        copies = []
        for i in range(query_rows // FINAL):
            span = slice(i * FINAL, (i + 1) * FINAL)
            out_ref[span, :] = (accum[:, span] * inverse[:, span]).astype(out_ref.dtype).T
            copies.append(pltpu.make_async_copy(out_ref.at[span], out_hbm.at[span], sems.at[i]))
            copies[-1].start()
        for copy in copies:
            copy.wait()
    else:
        outs[0][...] = high
        outs[1][...] = total
        outs[2][...] = accum


def attend_call(pieces, part, own, query, state, datas, items, last, cost=0):
    head_width, query_rows = query.shape[0] // 2, query.shape[1]
    whole = pl.BlockSpec(memory_space=pltpu.VMEM)
    first = state is None
    operands = ([] if first else list(state)) + list(datas)
    if last:
        shapes = jax.ShapeDtypeStruct((query_rows, head_width), jnp.bfloat16)
        out_specs = pl.BlockSpec(memory_space=pl.ANY)
        scratch = [
            pltpu.VMEM((query_rows, head_width), jnp.bfloat16),
            pltpu.SemaphoreType.DMA((query_rows // FINAL,)),
        ]
    else:
        scratch = []
        shapes = [
            jax.ShapeDtypeStruct((1, query_rows), jnp.float32),
            jax.ShapeDtypeStruct((1, query_rows), jnp.float32),
            jax.ShapeDtypeStruct((head_width, query_rows), jnp.float32),
        ]
        out_specs = [whole] * 3
    return pl.pallas_call(
        functools.partial(attend, pieces, part, first, last, items),
        out_shape=shapes,
        in_specs=[whole] * (2 + len(operands)),
        out_specs=out_specs,
        scratch_shapes=scratch,
        compiler_params=pltpu.CompilerParams(vmem_limit_bytes=24 * MIB),
        cost_estimate=pl.CostEstimate(flops=cost, bytes_accessed=0, transcendentals=0),
    )(own, query, *operands)


def shards(queries, keys, values, block_ids):
    rows_dev, all_heads, head_width = queries.shape
    part, kv_heads = keys.shape[:2]
    head_index = lax.axis_index("head")
    pieces = lax.axis_size("head")
    blocks = lax.axis_size("seq")
    heads_out = all_heads // pieces
    own_queries = lax.dynamic_slice_in_dim(queries, head_index * heads_out, heads_out, 1)
    own_queries = own_queries.reshape(rows_dev * heads_out, head_width)
    whole = pl.BlockSpec(memory_space=pltpu.VMEM)
    scaled = pl.pallas_call(
        functools.partial(scale_queries, head_width ** (-0.5)),
        out_shape=jax.ShapeDtypeStruct((2 * head_width, rows_dev * heads_out), jnp.bfloat16),
        in_specs=[whole],
        out_specs=whole,
        compiler_params=pltpu.CompilerParams(vmem_limit_bytes=8 * MIB),
    )(own_queries)
    own, *payloads = pl.pallas_call(
        functools.partial(pack, pieces // kv_heads, pieces, part, kv_heads),
        out_shape=[jax.ShapeDtypeStruct((2 * part, head_width), jnp.bfloat16)] * pieces,
        in_specs=[whole],
        out_specs=[whole] * pieces,
        compiler_params=pltpu.CompilerParams(vmem_limit_bytes=4 * MIB),
    )(jnp.concatenate([keys, values]).reshape(2 * part * kv_heads, head_width))
    mark = jnp.broadcast_to(block_ids.astype(jnp.bfloat16)[:, None], (MARK, head_width))
    own = jnp.concatenate([own, mark])
    near = [
        lax.ppermute(rows, "head", [(i, (i + shift + 1) % pieces) for i in range(pieces)])
        for shift, rows in enumerate(payloads)
    ]
    rest = jnp.concatenate(near)
    fold = functools.partial(attend_call, pieces, part, own, scaled)
    shifts = tuple(range(pieces))
    offsets = tuple(2 * part * i for i in range(pieces))

    def swap(rows, flip):
        return lax.ppermute(rows, "seq", [(i, i ^ flip) for i in range(blocks)])

    if blocks == 8:
        rest = rest[None]
        mine = jnp.stack([own] + [swap(own, flip) for flip in (2, 4, 6)])
        rests = [swap(rest, flip) for flip in (2, 4, 6)]

        def small(data, slots):
            return [(data, slot, (0,), None, (data, slot, 2 * part)) for slot in slots]

        def large(data, mark, slot):
            return (data, 0, offsets[:-1], None, (mark, slot, 2 * part))

        state = fold(
            None,
            [mine, rest],
            [(0, 0, (0,), shifts[:1], None), (1, 0, offsets[:-1], shifts[1:], None)] + small(0, range(1, 4)),
            False,
            1000000000,
        )
        mine, rest = lax.optimization_barrier((mine, rest))
        mine_other, rest_other = swap(mine, 1), swap(rest, 1)
        state = fold(state, [mine_other, rest_other], small(0, range(4)) + [large(1, 0, 0)], False)
        along_x, along_y, across = rests
        along_x, along_y, state = lax.optimization_barrier((along_x, along_y, state))
        others = [swap(rows, 1) for rows in (along_x, along_y)]
        state = fold(state, [mine, along_x, along_y], [large(i, 0, i) for i in (1, 2)], False)
        across, state = lax.optimization_barrier((across, state))
        other_across = swap(across, 1)
        state = fold(
            state,
            [mine, mine_other, across] + others,
            [large(2, 0, 3)] + [large(2 + i, 1, i) for i in (1, 2)],
            False,
        )
        result = fold(state, [mine_other, other_across], [large(1, 0, 3)], True)
    else:
        block = jnp.concatenate([own[: 2 * part], rest, own[2 * part :]])
        far = lax.all_gather(block, "seq", axis=0, tiled=False)
        unit = math.gcd(blocks, 8)
        far = far.reshape((blocks // unit, unit) + block.shape)
        items = [(0, i, offsets, None, (0, i, 2 * part * pieces)) for i in range(unit)]
        state = fold(None, [block[None]], [(0, 0, offsets, shifts, None)], False)
        state, _ = lax.scan(
            lambda held, rows: (tuple(fold(held, [rows], items, False)), None), tuple(state), far[:-1]
        )
        result = fold(state, [far[-1]], items, True)
    return result.reshape(rows_dev, heads_out, head_width)


def solution(mesh):
    return jax.shard_map(
        shards,
        mesh=mesh,
        in_specs=(
            P("seq", None, None),
            P(("seq", "head"), None, None),
            P(("seq", "head"), None, None),
            P("seq"),
        ),
        out_specs=P("seq", "head", None),
        check_vma=False,
    )
```

```python
import functools
import math

import jax
import jax.numpy as jnp
from jax import lax
from jax.experimental import pallas as pl
from jax.experimental.pallas import tpu as pltpu
from jax.sharding import PartitionSpec as P

MARK = 16
SUBLANES = 8
FINAL = 256
LOW = -1e30
HIGH = 1e30
MIB = 1024 * 1024


def pack(copies, pieces, part, kv_heads, rows_ref, *out_refs):
    here = lax.axis_index("head")
    rows = part * kv_heads
    at = lax.broadcasted_iota(jnp.int32, (part, rows), 0)
    source = lax.broadcasted_iota(jnp.int32, (part, rows), 1)
    picks = [
        jnp.where(source == at * kv_heads + head, 1.0, 0.0).astype(jnp.bfloat16) for head in range(kv_heads)
    ]
    for half in range(2):
        both = rows_ref[pl.ds(half * rows, rows), :]
        chosen = [jnp.dot(pick, both, preferred_element_type=jnp.float32).astype(jnp.bfloat16) for pick in picks]
        for shift, out_ref in enumerate(out_refs):
            kv_head = lax.rem(here + shift, pieces) // copies
            rows_out = chosen[0]
            for head in range(1, kv_heads):
                rows_out = jnp.where(kv_head == head, chosen[head], rows_out)
            out_ref[pl.ds(half * part, part), :] = rows_out


def scale_queries(scale, query_ref, out_ref):
    head_width = query_ref.shape[1]
    scaled = query_ref[...].astype(jnp.float32) * (scale * math.log2(math.e))
    coarse = scaled.astype(jnp.bfloat16)
    out_ref[:head_width, :] = coarse.T
    out_ref[head_width:, :] = (scaled - coarse.astype(jnp.float32)).astype(jnp.bfloat16).T


def attend(pieces, part, first, last, items, own_ref, query_ref, *refs):
    refs = list(refs)
    state = None if first else [refs.pop(0) for _ in range(3)]
    outs = [refs.pop() for _ in range(3)][::-1]
    head_width = query_ref.shape[0] // 2
    query_rows = query_ref.shape[1]
    group = query_rows // (pieces * part)
    here = lax.axis_index("head")
    own = own_ref[pl.ds(2 * part, MARK), :].astype(jnp.float32)[:SUBLANES]
    own = jnp.concatenate([own] * (query_rows // head_width), axis=1)

    blocks = []
    for data, slot, offsets, shifts, mark in items:
        rows_ref = refs[data].at[slot]
        if shifts is None:
            mark_data, mark_slot, mark_at = mark
            place = refs[mark_data][mark_slot, pl.ds(mark_at, MARK), :].astype(jnp.float32)[:SUBLANES]
            seen = jnp.concatenate([place] * (query_rows // head_width), axis=1) < own
        else:
            seen = None
        blocks.append((rows_ref, offsets, shifts, seen))

    def side(half):
        return jnp.concatenate(
            [
                rows_ref[pl.ds(offset + half * part, part), :]
                for rows_ref, offsets, _, _ in blocks
                for offset in offsets
            ]
        )

    keys = side(0)
    keys = jnp.concatenate([keys, keys], axis=1)
    values = side(1).T
    scores = jnp.dot(keys, query_ref[...], preferred_element_type=jnp.float32)
    cuts, tops, at = [], [], 0
    for _, offsets, shifts, seen in blocks:
        score = scores[at : at + len(offsets) * part]
        at += len(offsets) * part
        if seen is None:
            parts = []
            for i, shift in enumerate(shifts):
                cut = score[i * part : (i + 1) * part]
                key_at = lax.rem(here + pieces - shift, pieces) * part + lax.broadcasted_iota(jnp.int32, cut.shape, 0)
                query_at = lax.broadcasted_iota(jnp.int32, cut.shape, 1) // group
                parts.append(jnp.where(key_at <= query_at, cut, LOW))
            score = jnp.concatenate(parts)
        top = jnp.max(score.reshape(-1, SUBLANES, query_rows), axis=0)
        cuts.append(score)
        tops.append(top if seen is None else jnp.where(seen, top, LOW))
    high = jnp.max(functools.reduce(jnp.maximum, tops), axis=0, keepdims=True)
    if not first:
        old_high = state[0][...]
        high = jnp.maximum(old_high, high)
    weights, sums = [], []
    for score, (_, _, _, seen) in zip(cuts, blocks):
        base = high if seen is None else jnp.where(seen[:1], high, HIGH)
        expo = jnp.exp2(score - base)
        sums.append(jnp.sum(expo.reshape(-1, SUBLANES, query_rows), axis=0))
        weights.append(expo.astype(jnp.bfloat16))
    total = jnp.sum(functools.reduce(jnp.add, sums), axis=0, keepdims=True)
    accum = jnp.dot(values, jnp.concatenate(weights), preferred_element_type=jnp.float32)
    if not first:
        keep = jnp.exp2(old_high - high)
        total = total + state[1][...] * keep
        accum = accum + state[2][...] * keep
    if last:
        out_hbm, out_ref, sems = outs
        inverse = 1.0 / total
        copies = []
        for i in range(query_rows // FINAL):
            span = slice(i * FINAL, (i + 1) * FINAL)
            out_ref[span, :] = (accum[:, span] * inverse[:, span]).astype(out_ref.dtype).T
            copies.append(pltpu.make_async_copy(out_ref.at[span], out_hbm.at[span], sems.at[i]))
            copies[-1].start()
        for copy in copies:
            copy.wait()
    else:
        outs[0][...] = high
        outs[1][...] = total
        outs[2][...] = accum


def attend_call(pieces, part, own, query, state, datas, items, last, cost=0):
    head_width, query_rows = query.shape[0] // 2, query.shape[1]
    whole = pl.BlockSpec(memory_space=pltpu.VMEM)
    first = state is None
    operands = ([] if first else list(state)) + list(datas)
    if last:
        shapes = jax.ShapeDtypeStruct((query_rows, head_width), jnp.bfloat16)
        out_specs = pl.BlockSpec(memory_space=pl.ANY)
        scratch = [
            pltpu.VMEM((query_rows, head_width), jnp.bfloat16),
            pltpu.SemaphoreType.DMA((query_rows // FINAL,)),
        ]
    else:
        scratch = []
        shapes = [
            jax.ShapeDtypeStruct((1, query_rows), jnp.float32),
            jax.ShapeDtypeStruct((1, query_rows), jnp.float32),
            jax.ShapeDtypeStruct((head_width, query_rows), jnp.float32),
        ]
        out_specs = [whole] * 3
    return pl.pallas_call(
        functools.partial(attend, pieces, part, first, last, items),
        out_shape=shapes,
        in_specs=[whole] * (2 + len(operands)),
        out_specs=out_specs,
        scratch_shapes=scratch,
        compiler_params=pltpu.CompilerParams(vmem_limit_bytes=24 * MIB),
        cost_estimate=pl.CostEstimate(flops=cost, bytes_accessed=0, transcendentals=0),
    )(own, query, *operands)


def shards(queries, keys, values, block_ids):
    rows_dev, all_heads, head_width = queries.shape
    part, kv_heads = keys.shape[:2]
    head_index = lax.axis_index("head")
    pieces = lax.axis_size("head")
    blocks = lax.axis_size("seq")
    heads_out = all_heads // pieces
    own_queries = lax.dynamic_slice_in_dim(queries, head_index * heads_out, heads_out, 1)
    own_queries = own_queries.reshape(rows_dev * heads_out, head_width)
    whole = pl.BlockSpec(memory_space=pltpu.VMEM)
    scaled = pl.pallas_call(
        functools.partial(scale_queries, head_width ** (-0.5)),
        out_shape=jax.ShapeDtypeStruct((2 * head_width, rows_dev * heads_out), jnp.bfloat16),
        in_specs=[whole],
        out_specs=whole,
        compiler_params=pltpu.CompilerParams(vmem_limit_bytes=8 * MIB),
    )(own_queries)
    own, *payloads = pl.pallas_call(
        functools.partial(pack, pieces // kv_heads, pieces, part, kv_heads),
        out_shape=[jax.ShapeDtypeStruct((2 * part, head_width), jnp.bfloat16)] * pieces,
        in_specs=[whole],
        out_specs=[whole] * pieces,
        compiler_params=pltpu.CompilerParams(vmem_limit_bytes=4 * MIB),
    )(jnp.concatenate([keys, values]).reshape(2 * part * kv_heads, head_width))
    mark = jnp.broadcast_to(block_ids.astype(jnp.bfloat16)[:, None], (MARK, head_width))
    own = jnp.concatenate([own, mark])
    near = [
        lax.ppermute(rows, "head", [(i, (i + shift + 1) % pieces) for i in range(pieces)])
        for shift, rows in enumerate(payloads)
    ]
    rest = jnp.concatenate(near)
    fold = functools.partial(attend_call, pieces, part, own, scaled)
    shifts = tuple(range(pieces))
    offsets = tuple(2 * part * i for i in range(pieces))

    def swap(rows, flip):
        return lax.ppermute(rows, "seq", [(i, i ^ flip) for i in range(blocks)])

    if blocks == 8:
        rest = rest[None]
        near_x, near_y, near_far = [swap(own, flip) for flip in (2, 4, 6)]
        mine = jnp.stack([own, near_x, near_y])
        along_x, along_y, across = [swap(rest, flip) for flip in (2, 4, 6)]

        def small(data, slots):
            return [(data, slot, (0,), None, (data, slot, 2 * part)) for slot in slots]

        def large(data, mark, slot, at=0):
            return (data, 0, tuple(at + offset for offset in offsets[:-1]), None, (mark, slot, 2 * part))

        state = fold(
            None,
            [mine, rest],
            [(0, 0, (0,), shifts[:1], None), (1, 0, offsets[:-1], shifts[1:], None)] + small(0, (1, 2)),
            False,
            1000000000,
        )
        early_rows = mine.shape[0] * mine.shape[1]
        both_other = swap(jnp.concatenate([mine.reshape(1, early_rows, head_width), rest], axis=1), 1)
        size = own.shape[0]
        state = fold(
            state,
            [both_other, near_far[None]],
            [(0, 0, (size * i,), None, (0, 0, size * i + 2 * part)) for i in range(3)]
            + [(0, 0, tuple(early_rows + offset for offset in offsets[:-1]), None, (0, 0, 2 * part))]
            + small(1, (0,)),
            False,
            0000000,
        )
        along_x, along_y, state = lax.optimization_barrier((along_x, along_y, state))
        others = [swap(rows, 1) for rows in (along_x, along_y)]
        state = fold(state, [mine, along_x, along_y], [large(i, 0, i) for i in (1, 2)], False)
        across, state = lax.optimization_barrier((across, state))
        across = jnp.concatenate([near_far[None], across], axis=1)
        across = lax.optimization_barrier((across, *(others if isinstance(others, list) else [others])))[0]
        other_across = swap(across, 1)
        state = fold(
            state,
            [across, both_other] + others,
            [large(0, 0, 0, size)] + [(1 + i, 0, offsets[:-1], None, (1, 0, size * i + 2 * part)) for i in (1, 2)],
            False,
        )
        result = fold(
            state,
            [other_across],
            [(0, 0, (0,) + tuple(own.shape[0] + offset for offset in offsets[:-1]), None, (0, 0, 2 * part))],
            True,
        )
    else:
        block = jnp.concatenate([own[: 2 * part], rest, own[2 * part :]])
        far = lax.all_gather(block, "seq", axis=0, tiled=False)
        unit = math.gcd(blocks, 8)
        far = far.reshape((blocks // unit, unit) + block.shape)
        items = [(0, i, offsets, None, (0, i, 2 * part * pieces)) for i in range(unit)]
        state = fold(None, [block[None]], [(0, 0, offsets, shifts, None)], False)
        state, _ = lax.scan(
            lambda held, rows: (tuple(fold(held, [rows], items, False)), None), tuple(state), far[:-1]
        )
        result = fold(state, [far[-1]], items, True)
    return result.reshape(rows_dev, heads_out, head_width)


def solution(mesh):
    return jax.shard_map(
        shards,
        mesh=mesh,
        in_specs=(
            P("seq", None, None),
            P(("seq", "head"), None, None),
            P(("seq", "head"), None, None),
            P("seq"),
        ),
        out_specs=P("seq", "head", None),
        check_vma=False,
    )
```

```python
import functools
import math

import jax
import jax.numpy as jnp
from jax import lax
from jax.experimental import pallas as pl
from jax.experimental.pallas import tpu as pltpu
from jax.sharding import PartitionSpec as P

MARK = 16
SUBLANES = 8
FINAL = 256
OVERLAP = 1000000000
LOW = -1e30
HIGH = 1e30
MIB = 1024 * 1024


def pack(copies, pieces, part, kv_heads, rows_ref, *out_refs):
    here = lax.axis_index("head")
    rows = part * kv_heads
    at = lax.broadcasted_iota(jnp.int32, (part, rows), 0)
    source = lax.broadcasted_iota(jnp.int32, (part, rows), 1)
    picks = [
        jnp.where(source == at * kv_heads + head, 1.0, 0.0).astype(jnp.bfloat16) for head in range(kv_heads)
    ]
    for half in range(2):
        both = rows_ref[pl.ds(half * rows, rows), :]
        chosen = [jnp.dot(pick, both, preferred_element_type=jnp.float32).astype(jnp.bfloat16) for pick in picks]
        for shift, out_ref in enumerate(out_refs):
            kv_head = lax.rem(here + shift, pieces) // copies
            rows_out = chosen[0]
            for head in range(1, kv_heads):
                rows_out = jnp.where(kv_head == head, chosen[head], rows_out)
            out_ref[pl.ds(half * part, part), :] = rows_out


def scale_queries(scale, query_ref, out_ref):
    head_width = query_ref.shape[1]
    scaled = query_ref[...].astype(jnp.float32) * (scale * math.log2(math.e))
    coarse = scaled.astype(jnp.bfloat16)
    out_ref[:head_width, :] = coarse.T
    out_ref[head_width:, :] = (scaled - coarse.astype(jnp.float32)).astype(jnp.bfloat16).T


def attend(pieces, part, first, last, items, own_ref, query_ref, *refs):
    refs = list(refs)
    state = None if first else [refs.pop(0) for _ in range(3)]
    outs = [refs.pop() for _ in range(3)][::-1]
    head_width = query_ref.shape[0] // 2
    query_rows = query_ref.shape[1]
    group = query_rows // (pieces * part)
    here = lax.axis_index("head")
    own = own_ref[pl.ds(2 * part, MARK), :].astype(jnp.float32)[:SUBLANES]
    own = jnp.concatenate([own] * (query_rows // head_width), axis=1)

    blocks = []
    for data, slot, offsets, shifts, mark in items:
        rows_ref = refs[data].at[slot]
        if shifts is None:
            mark_data, mark_slot, mark_at = mark
            place = refs[mark_data][mark_slot, pl.ds(mark_at, MARK), :].astype(jnp.float32)[:SUBLANES]
            seen = jnp.concatenate([place] * (query_rows // head_width), axis=1) < own
        else:
            seen = None
        blocks.append((rows_ref, offsets, shifts, seen))

    def side(half):
        return jnp.concatenate(
            [
                rows_ref[pl.ds(offset + half * part, part), :]
                for rows_ref, offsets, _, _ in blocks
                for offset in offsets
            ]
        )

    keys = side(0)
    keys = jnp.concatenate([keys, keys], axis=1)
    values = side(1).T
    scores = jnp.dot(keys, query_ref[...], preferred_element_type=jnp.float32)
    cuts, tops, at = [], [], 0
    for _, offsets, shifts, seen in blocks:
        score = scores[at : at + len(offsets) * part]
        at += len(offsets) * part
        if seen is None:
            parts = []
            for i, shift in enumerate(shifts):
                cut = score[i * part : (i + 1) * part]
                key_at = lax.rem(here + pieces - shift, pieces) * part + lax.broadcasted_iota(jnp.int32, cut.shape, 0)
                query_at = lax.broadcasted_iota(jnp.int32, cut.shape, 1) // group
                parts.append(jnp.where(key_at <= query_at, cut, LOW))
            score = jnp.concatenate(parts)
        top = jnp.max(score.reshape(-1, SUBLANES, query_rows), axis=0)
        cuts.append(score)
        tops.append(top if seen is None else jnp.where(seen, top, LOW))
    high = jnp.max(functools.reduce(jnp.maximum, tops), axis=0, keepdims=True)
    if not first:
        old_high = state[0][...]
        high = jnp.maximum(old_high, high)
    weights, sums = [], []
    for score, (_, _, _, seen) in zip(cuts, blocks):
        base = high if seen is None else jnp.where(seen[:1], high, HIGH)
        expo = jnp.exp2(score - base)
        sums.append(jnp.sum(expo.reshape(-1, SUBLANES, query_rows), axis=0))
        weights.append(expo.astype(jnp.bfloat16))
    total = jnp.sum(functools.reduce(jnp.add, sums), axis=0, keepdims=True)
    accum = jnp.dot(values, jnp.concatenate(weights), preferred_element_type=jnp.float32)
    if not first:
        keep = jnp.exp2(old_high - high)
        total = total + state[1][...] * keep
        accum = accum + state[2][...] * keep
    if last:
        out_hbm, out_ref, sems = outs
        inverse = 1.0 / total
        copies = []
        for i in range(query_rows // FINAL):
            span = slice(i * FINAL, (i + 1) * FINAL)
            out_ref[span, :] = (accum[:, span] * inverse[:, span]).astype(out_ref.dtype).T
            copies.append(pltpu.make_async_copy(out_ref.at[span], out_hbm.at[span], sems.at[i]))
            copies[-1].start()
        for copy in copies:
            copy.wait()
    else:
        outs[0][...] = high
        outs[1][...] = total
        outs[2][...] = accum


def attend_call(pieces, part, own, query, state, datas, items, last, cost=0):
    head_width, query_rows = query.shape[0] // 2, query.shape[1]
    whole = pl.BlockSpec(memory_space=pltpu.VMEM)
    first = state is None
    operands = ([] if first else list(state)) + list(datas)
    if last:
        shapes = jax.ShapeDtypeStruct((query_rows, head_width), jnp.bfloat16)
        out_specs = pl.BlockSpec(memory_space=pl.ANY)
        scratch = [
            pltpu.VMEM((query_rows, head_width), jnp.bfloat16),
            pltpu.SemaphoreType.DMA((query_rows // FINAL,)),
        ]
    else:
        scratch = []
        shapes = [
            jax.ShapeDtypeStruct((1, query_rows), jnp.float32),
            jax.ShapeDtypeStruct((1, query_rows), jnp.float32),
            jax.ShapeDtypeStruct((head_width, query_rows), jnp.float32),
        ]
        out_specs = [whole] * 3
    return pl.pallas_call(
        functools.partial(attend, pieces, part, first, last, items),
        out_shape=shapes,
        in_specs=[whole] * (2 + len(operands)),
        out_specs=out_specs,
        scratch_shapes=scratch,
        compiler_params=pltpu.CompilerParams(vmem_limit_bytes=24 * MIB),
        cost_estimate=pl.CostEstimate(flops=cost, bytes_accessed=0, transcendentals=0),
    )(own, query, *operands)


def shards(queries, keys, values, block_ids):
    rows_dev, all_heads, head_width = queries.shape
    part, kv_heads = keys.shape[:2]
    head_index = lax.axis_index("head")
    pieces = lax.axis_size("head")
    blocks = lax.axis_size("seq")
    heads_out = all_heads // pieces
    own_queries = lax.dynamic_slice_in_dim(queries, head_index * heads_out, heads_out, 1)
    own_queries = own_queries.reshape(rows_dev * heads_out, head_width)
    whole = pl.BlockSpec(memory_space=pltpu.VMEM)
    scaled = pl.pallas_call(
        functools.partial(scale_queries, head_width ** (-0.5)),
        out_shape=jax.ShapeDtypeStruct((2 * head_width, rows_dev * heads_out), jnp.bfloat16),
        in_specs=[whole],
        out_specs=whole,
        compiler_params=pltpu.CompilerParams(vmem_limit_bytes=8 * MIB),
    )(own_queries)
    own, *payloads = pl.pallas_call(
        functools.partial(pack, pieces // kv_heads, pieces, part, kv_heads),
        out_shape=[jax.ShapeDtypeStruct((2 * part, head_width), jnp.bfloat16)] * pieces,
        in_specs=[whole],
        out_specs=[whole] * pieces,
        compiler_params=pltpu.CompilerParams(vmem_limit_bytes=4 * MIB),
    )(jnp.concatenate([keys, values]).reshape(2 * part * kv_heads, head_width))
    mark = jnp.broadcast_to(block_ids.astype(jnp.bfloat16)[:, None], (MARK, head_width))
    own = jnp.concatenate([own, mark])
    near = [
        lax.ppermute(rows, "head", [(i, (i + shift + 1) % pieces) for i in range(pieces)])
        for shift, rows in enumerate(payloads)
    ]
    rest = jnp.concatenate(near)
    fold = functools.partial(attend_call, pieces, part, own, scaled)
    shifts = tuple(range(pieces))
    offsets = tuple(2 * part * i for i in range(pieces))

    def swap(rows, flip):
        return lax.ppermute(rows, "seq", [(i, i ^ flip) for i in range(blocks)])

    if blocks == 8:
        rest = rest[None]

        def hop(rows, even, odd):
            return lax.ppermute(rows, "seq", [(i, i ^ (odd if i & 1 else even)) for i in range(blocks)])

        near_one, near_two, near_far = hop(own, 2, 4), hop(own, 4, 2), swap(own, 6)
        mine = jnp.stack([own, near_one, near_two])
        along_one, along_two = hop(rest, 2, 4), hop(rest, 4, 2)
        across = hop(along_one, 4, 2)

        def small(data, slots):
            return [(data, slot, (0,), None, (data, slot, 2 * part)) for slot in slots]

        def large(data, mark, slot, at=0):
            return (data, 0, tuple(at + offset for offset in offsets[:-1]), None, (mark, slot, 2 * part))

        state = fold(
            None,
            [mine, rest],
            [(0, 0, (0,), shifts[:1], None), (1, 0, offsets[:-1], shifts[1:], None)] + small(0, (1, 2)),
            False,
            OVERLAP,
        )
        early_rows = mine.shape[0] * mine.shape[1]
        both_other = swap(jnp.concatenate([mine.reshape(1, early_rows, head_width), rest], axis=1), 1)
        size = own.shape[0]
        state = fold(
            state,
            [both_other, near_far[None]],
            [(0, 0, (size * i,), None, (0, 0, size * i + 2 * part)) for i in range(3)]
            + [(0, 0, tuple(early_rows + offset for offset in offsets[:-1]), None, (0, 0, 2 * part))]
            + small(1, (0,)),
            False,
            0,
        )
        along_one, along_two, state = lax.optimization_barrier((along_one, along_two, state))
        others = [swap(rows, 1) for rows in (along_one, along_two)]
        state = fold(state, [mine, along_one, along_two], [large(i, 0, i) for i in (1, 2)], False, OVERLAP)
        across, state = lax.optimization_barrier((across, state))
        across = jnp.concatenate([near_far[None], across], axis=1)
        across, *others = lax.optimization_barrier((across, *others))
        other_across = swap(across, 1)
        state = fold(
            state,
            [across, both_other] + others,
            [large(0, 0, 0, size)] + [(1 + i, 0, offsets[:-1], None, (1, 0, size * i + 2 * part)) for i in (1, 2)],
            False,
        )
        result = fold(
            state,
            [other_across],
            [(0, 0, (0,) + tuple(own.shape[0] + offset for offset in offsets[:-1]), None, (0, 0, 2 * part))],
            True,
        )
    else:
        block = jnp.concatenate([own[: 2 * part], rest, own[2 * part :]])
        far = lax.all_gather(block, "seq", axis=0, tiled=False)
        unit = math.gcd(blocks, 8)
        far = far.reshape((blocks // unit, unit) + block.shape)
        items = [(0, i, offsets, None, (0, i, 2 * part * pieces)) for i in range(unit)]
        state = fold(None, [block[None]], [(0, 0, offsets, shifts, None)], False)
        state, _ = lax.scan(
            lambda held, rows: (tuple(fold(held, [rows], items, False)), None), tuple(state), far[:-1]
        )
        result = fold(state, [far[-1]], items, True)
    return result.reshape(rows_dev, heads_out, head_width)


def solution(mesh):
    return jax.shard_map(
        shards,
        mesh=mesh,
        in_specs=(
            P("seq", None, None),
            P(("seq", "head"), None, None),
            P(("seq", "head"), None, None),
            P("seq"),
        ),
        out_specs=P("seq", "head", None),
        check_vma=False,
    )
```

```python
import functools
import math

import jax
import jax.numpy as jnp
from jax import lax
from jax.experimental import pallas as pl
from jax.experimental.pallas import tpu as pltpu
from jax.sharding import PartitionSpec as P

MARK = 16
SUBLANES = 8
FINAL = 256
OVERLAP = 1000000000
LOW = -1e30
HIGH = 1e30
MIB = 1024 * 1024


def pack(copies, pieces, part, kv_heads, rows_ref, *out_refs):
    here = lax.axis_index("head")
    rows = part * kv_heads
    at = lax.broadcasted_iota(jnp.int32, (part, rows), 0)
    source = lax.broadcasted_iota(jnp.int32, (part, rows), 1)
    picks = [
        jnp.where(source == at * kv_heads + head, 1.0, 0.0).astype(jnp.bfloat16) for head in range(kv_heads)
    ]
    for half in range(2):
        both = rows_ref[pl.ds(half * rows, rows), :]
        chosen = [jnp.dot(pick, both, preferred_element_type=jnp.float32).astype(jnp.bfloat16) for pick in picks]
        for shift, out_ref in enumerate(out_refs):
            kv_head = lax.rem(here + shift, pieces) // copies
            rows_out = chosen[0]
            for head in range(1, kv_heads):
                rows_out = jnp.where(kv_head == head, chosen[head], rows_out)
            out_ref[pl.ds(half * part, part), :] = rows_out


def scale_queries(scale, query_ref, out_ref):
    head_width = query_ref.shape[1]
    scaled = query_ref[...].astype(jnp.float32) * (scale * math.log2(math.e))
    coarse = scaled.astype(jnp.bfloat16)
    out_ref[:head_width, :] = coarse.T
    out_ref[head_width:, :] = (scaled - coarse.astype(jnp.float32)).astype(jnp.bfloat16).T


def attend(pieces, part, first, last, items, own_ref, query_ref, *refs):
    refs = list(refs)
    state = None if first else [refs.pop(0) for _ in range(3)]
    outs = [refs.pop() for _ in range(3)][::-1]
    head_width = query_ref.shape[0] // 2
    query_rows = query_ref.shape[1]
    group = query_rows // (pieces * part)
    here = lax.axis_index("head")
    own = own_ref[pl.ds(2 * part, MARK), :].astype(jnp.float32)[:SUBLANES]
    own = jnp.concatenate([own] * (query_rows // head_width), axis=1)

    blocks = []
    for data, slot, offsets, shifts, mark in items:
        rows_ref = refs[data].at[slot]
        if shifts is None:
            mark_data, mark_slot, mark_at = mark
            place = refs[mark_data][mark_slot, pl.ds(mark_at, MARK), :].astype(jnp.float32)[:SUBLANES]
            seen = jnp.concatenate([place] * (query_rows // head_width), axis=1) < own
        else:
            seen = None
        blocks.append((rows_ref, offsets, shifts, seen))

    def side(half):
        return jnp.concatenate(
            [
                rows_ref[pl.ds(offset + half * part, part), :]
                for rows_ref, offsets, _, _ in blocks
                for offset in offsets
            ]
        )

    keys = side(0)
    keys = jnp.concatenate([keys, keys], axis=1)
    values = side(1).T
    scores = jnp.dot(keys, query_ref[...], preferred_element_type=jnp.float32)
    cuts, tops, at = [], [], 0
    for _, offsets, shifts, seen in blocks:
        score = scores[at : at + len(offsets) * part]
        at += len(offsets) * part
        if seen is None:
            parts = []
            for i, shift in enumerate(shifts):
                cut = score[i * part : (i + 1) * part]
                key_at = lax.rem(here + pieces - shift, pieces) * part + lax.broadcasted_iota(jnp.int32, cut.shape, 0)
                query_at = lax.broadcasted_iota(jnp.int32, cut.shape, 1) // group
                parts.append(jnp.where(key_at <= query_at, cut, LOW))
            score = jnp.concatenate(parts)
        top = jnp.max(score.reshape(-1, SUBLANES, query_rows), axis=0)
        cuts.append(score)
        tops.append(top if seen is None else jnp.where(seen, top, LOW))
    high = jnp.max(functools.reduce(jnp.maximum, tops), axis=0, keepdims=True)
    if not first:
        old_high = state[0][...]
        high = jnp.maximum(old_high, high)
    weights, sums = [], []
    for score, (_, _, _, seen) in zip(cuts, blocks):
        base = high if seen is None else jnp.where(seen[:1], high, HIGH)
        expo = jnp.exp2(score - base)
        sums.append(jnp.sum(expo.reshape(-1, SUBLANES, query_rows), axis=0))
        weights.append(expo.astype(jnp.bfloat16))
    total = jnp.sum(functools.reduce(jnp.add, sums), axis=0, keepdims=True)
    accum = jnp.dot(values, jnp.concatenate(weights), preferred_element_type=jnp.float32)
    if not first:
        keep = jnp.exp2(old_high - high)
        total = total + state[1][...] * keep
        accum = accum + state[2][...] * keep
    if last:
        out_hbm, out_ref, sems = outs
        inverse = 1.0 / total
        copies = []
        for i in range(query_rows // FINAL):
            span = slice(i * FINAL, (i + 1) * FINAL)
            out_ref[span, :] = (accum[:, span] * inverse[:, span]).astype(out_ref.dtype).T
            copies.append(pltpu.make_async_copy(out_ref.at[span], out_hbm.at[span], sems.at[i]))
            copies[-1].start()
        for copy in copies:
            copy.wait()
    else:
        outs[0][...] = high
        outs[1][...] = total
        outs[2][...] = accum


def attend_call(pieces, part, own, query, state, datas, items, last, cost=0):
    head_width, query_rows = query.shape[0] // 2, query.shape[1]
    whole = pl.BlockSpec(memory_space=pltpu.VMEM)
    first = state is None
    operands = ([] if first else list(state)) + list(datas)
    if last:
        shapes = jax.ShapeDtypeStruct((query_rows, head_width), jnp.bfloat16)
        out_specs = pl.BlockSpec(memory_space=pl.ANY)
        scratch = [
            pltpu.VMEM((query_rows, head_width), jnp.bfloat16),
            pltpu.SemaphoreType.DMA((query_rows // FINAL,)),
        ]
    else:
        scratch = []
        shapes = [
            jax.ShapeDtypeStruct((1, query_rows), jnp.float32),
            jax.ShapeDtypeStruct((1, query_rows), jnp.float32),
            jax.ShapeDtypeStruct((head_width, query_rows), jnp.float32),
        ]
        out_specs = [whole] * 3
    return pl.pallas_call(
        functools.partial(attend, pieces, part, first, last, items),
        out_shape=shapes,
        in_specs=[whole] * (2 + len(operands)),
        out_specs=out_specs,
        scratch_shapes=scratch,
        compiler_params=pltpu.CompilerParams(vmem_limit_bytes=24 * MIB),
        cost_estimate=pl.CostEstimate(flops=cost, bytes_accessed=0, transcendentals=0),
    )(own, query, *operands)


def shards(queries, keys, values, block_ids):
    rows_dev, all_heads, head_width = queries.shape
    part, kv_heads = keys.shape[:2]
    head_index = lax.axis_index("head")
    pieces = lax.axis_size("head")
    blocks = lax.axis_size("seq")
    heads_out = all_heads // pieces
    own_queries = lax.dynamic_slice_in_dim(queries, head_index * heads_out, heads_out, 1)
    own_queries = own_queries.reshape(rows_dev * heads_out, head_width)
    whole = pl.BlockSpec(memory_space=pltpu.VMEM)
    scaled = pl.pallas_call(
        functools.partial(scale_queries, head_width ** (-0.5)),
        out_shape=jax.ShapeDtypeStruct((2 * head_width, rows_dev * heads_out), jnp.bfloat16),
        in_specs=[whole],
        out_specs=whole,
        compiler_params=pltpu.CompilerParams(vmem_limit_bytes=8 * MIB),
    )(own_queries)
    own, *payloads = pl.pallas_call(
        functools.partial(pack, pieces // kv_heads, pieces, part, kv_heads),
        out_shape=[jax.ShapeDtypeStruct((2 * part, head_width), jnp.bfloat16)] * pieces,
        in_specs=[whole],
        out_specs=[whole] * pieces,
        compiler_params=pltpu.CompilerParams(vmem_limit_bytes=4 * MIB),
    )(jnp.concatenate([keys, values]).reshape(2 * part * kv_heads, head_width))
    mark = jnp.broadcast_to(block_ids.astype(jnp.bfloat16)[:, None], (MARK, head_width))
    own = jnp.concatenate([own, mark])
    near = [
        lax.ppermute(rows, "head", [(i, (i + shift + 1) % pieces) for i in range(pieces)])
        for shift, rows in enumerate(payloads)
    ]
    rest = jnp.concatenate(near)
    fold = functools.partial(attend_call, pieces, part, own, scaled)
    shifts = tuple(range(pieces))
    offsets = tuple(2 * part * i for i in range(pieces))

    def swap(rows, flip):
        return lax.ppermute(rows, "seq", [(i, i ^ flip) for i in range(blocks)])

    if blocks == 8:
        rest = rest[None]
        ways = ((4, 2), (2, 6), (6, 4))

        def hop(rows, way):
            return lax.ppermute(rows, "seq", [(i, i ^ way[i & 1]) for i in range(blocks)])

        near_one, near_two, near_last = [hop(own, way) for way in ways]
        mine = jnp.stack([own, near_one, near_two])
        along_one, along_two, along_last = [hop(rest, way) for way in ways]

        def small(data, slots):
            return [(data, slot, (0,), None, (data, slot, 2 * part)) for slot in slots]

        def large(data, mark, slot, at=0):
            return (data, 0, tuple(at + offset for offset in offsets[:-1]), None, (mark, slot, 2 * part))

        state = fold(
            None,
            [mine, rest],
            [(0, 0, (0,), shifts[:1], None), (1, 0, offsets[:-1], shifts[1:], None)] + small(0, (1, 2)),
            False,
            OVERLAP,
        )
        early_rows = mine.shape[0] * mine.shape[1]
        both_other = swap(jnp.concatenate([mine.reshape(1, early_rows, head_width), rest], axis=1), 1)
        size = own.shape[0]
        state = fold(
            state,
            [both_other, near_last[None]],
            [(0, 0, (size * i,), None, (0, 0, size * i + 2 * part)) for i in range(3)]
            + [(0, 0, tuple(early_rows + offset for offset in offsets[:-1]), None, (0, 0, 2 * part))]
            + small(1, (0,)),
            False,
        )
        along_one, along_two, state = lax.optimization_barrier((along_one, along_two, state))
        others = [swap(rows, 1) for rows in (along_one, along_two)]
        state = fold(state, [mine, along_one, along_two], [large(i, 0, i) for i in (1, 2)], False)
        along_last, state = lax.optimization_barrier((along_last, state))
        along_last = jnp.concatenate([near_last[None], along_last], axis=1)
        along_last, *others = lax.optimization_barrier((along_last, *others))
        other_last = swap(along_last, 1)
        state = fold(
            state,
            [along_last, both_other] + others,
            [large(0, 0, 0, size)] + [(1 + i, 0, offsets[:-1], None, (1, 0, size * i + 2 * part)) for i in (1, 2)],
            False,
        )
        result = fold(
            state,
            [other_last],
            [(0, 0, (0,) + tuple(own.shape[0] + offset for offset in offsets[:-1]), None, (0, 0, 2 * part))],
            True,
        )
    else:
        block = jnp.concatenate([own[: 2 * part], rest, own[2 * part :]])
        far = lax.all_gather(block, "seq", axis=0, tiled=False)
        unit = math.gcd(blocks, 8)
        far = far.reshape((blocks // unit, unit) + block.shape)
        items = [(0, i, offsets, None, (0, i, 2 * part * pieces)) for i in range(unit)]
        state = fold(None, [block[None]], [(0, 0, offsets, shifts, None)], False)
        state, _ = lax.scan(
            lambda held, rows: (tuple(fold(held, [rows], items, False)), None), tuple(state), far[:-1]
        )
        result = fold(state, [far[-1]], items, True)
    return result.reshape(rows_dev, heads_out, head_width)


def solution(mesh):
    return jax.shard_map(
        shards,
        mesh=mesh,
        in_specs=(
            P("seq", None, None),
            P(("seq", "head"), None, None),
            P(("seq", "head"), None, None),
            P("seq"),
        ),
        out_specs=P("seq", "head", None),
        check_vma=False,
    )
```

```python
import functools
import math

import jax
import jax.numpy as jnp
from jax import lax
from jax.experimental import pallas as pl
from jax.experimental.pallas import tpu as pltpu
from jax.sharding import PartitionSpec as P

MARK = 16
SUBLANES = 8
FINAL = 256
OVERLAP = 1000000000
LOW = -1e30
HIGH = 1e30
MIB = 1024 * 1024


def pack(copies, pieces, part, kv_heads, rows_ref, *out_refs):
    here = lax.axis_index("head")
    rows = part * kv_heads
    at = lax.broadcasted_iota(jnp.int32, (part, rows), 0)
    source = lax.broadcasted_iota(jnp.int32, (part, rows), 1)
    picks = [
        jnp.where(source == at * kv_heads + head, 1.0, 0.0).astype(jnp.bfloat16) for head in range(kv_heads)
    ]
    for half in range(2):
        both = rows_ref[pl.ds(half * rows, rows), :]
        chosen = [jnp.dot(pick, both, preferred_element_type=jnp.float32).astype(jnp.bfloat16) for pick in picks]
        for shift, out_ref in enumerate(out_refs):
            kv_head = lax.rem(here + shift, pieces) // copies
            rows_out = chosen[0]
            for head in range(1, kv_heads):
                rows_out = jnp.where(kv_head == head, chosen[head], rows_out)
            out_ref[pl.ds(half * part, part), :] = rows_out


def scale_queries(scale, query_ref, out_ref):
    head_width = query_ref.shape[1]
    scaled = query_ref[...].astype(jnp.float32) * (scale * math.log2(math.e))
    coarse = scaled.astype(jnp.bfloat16)
    out_ref[:head_width, :] = coarse.T
    out_ref[head_width:, :] = (scaled - coarse.astype(jnp.float32)).astype(jnp.bfloat16).T


def attend(pieces, part, first, last, items, own_ref, query_ref, *refs):
    refs = list(refs)
    state = None if first else [refs.pop(0) for _ in range(3)]
    outs = [refs.pop() for _ in range(3)][::-1]
    head_width = query_ref.shape[0] // 2
    query_rows = query_ref.shape[1]
    group = query_rows // (pieces * part)
    here = lax.axis_index("head")
    own = own_ref[pl.ds(2 * part, MARK), :].astype(jnp.float32)[:SUBLANES]
    own = jnp.concatenate([own] * (query_rows // head_width), axis=1)

    blocks = []
    for data, slot, offsets, shifts, mark in items:
        rows_ref = refs[data].at[slot]
        if shifts is None:
            mark_data, mark_slot, mark_at = mark
            place = refs[mark_data][mark_slot, pl.ds(mark_at, MARK), :].astype(jnp.float32)[:SUBLANES]
            seen = jnp.concatenate([place] * (query_rows // head_width), axis=1) < own
        else:
            seen = None
        blocks.append((rows_ref, offsets, shifts, seen))

    def side(half):
        return jnp.concatenate(
            [
                rows_ref[pl.ds(offset + half * part, part), :]
                for rows_ref, offsets, _, _ in blocks
                for offset in offsets
            ]
        )

    keys = side(0)
    keys = jnp.concatenate([keys, keys], axis=1)
    values = side(1).T
    scores = jnp.dot(keys, query_ref[...], preferred_element_type=jnp.float32)
    cuts, tops, at = [], [], 0
    for _, offsets, shifts, seen in blocks:
        score = scores[at : at + len(offsets) * part]
        at += len(offsets) * part
        if seen is None:
            parts = []
            for i, shift in enumerate(shifts):
                cut = score[i * part : (i + 1) * part]
                key_at = lax.rem(here + pieces - shift, pieces) * part + lax.broadcasted_iota(jnp.int32, cut.shape, 0)
                query_at = lax.broadcasted_iota(jnp.int32, cut.shape, 1) // group
                parts.append(jnp.where(key_at <= query_at, cut, LOW))
            score = jnp.concatenate(parts)
        top = jnp.max(score.reshape(-1, SUBLANES, query_rows), axis=0)
        cuts.append(score)
        tops.append(top if seen is None else jnp.where(seen, top, LOW))
    high = jnp.max(functools.reduce(jnp.maximum, tops), axis=0, keepdims=True)
    if not first:
        old_high = state[0][...]
        high = jnp.maximum(old_high, high)
    weights, sums = [], []
    for score, (_, _, _, seen) in zip(cuts, blocks):
        base = high if seen is None else jnp.where(seen[:1], high, HIGH)
        expo = jnp.exp2(score - base)
        sums.append(jnp.sum(expo.reshape(-1, SUBLANES, query_rows), axis=0))
        weights.append(expo.astype(jnp.bfloat16))
    total = jnp.sum(functools.reduce(jnp.add, sums), axis=0, keepdims=True)
    accum = jnp.dot(values, jnp.concatenate(weights), preferred_element_type=jnp.float32)
    if not first:
        keep = jnp.exp2(old_high - high)
        total = total + state[1][...] * keep
        accum = accum + state[2][...] * keep
    if last:
        out_hbm, out_ref, sems = outs
        inverse = 1.0 / total
        copies = []
        for i in range(query_rows // FINAL):
            span = slice(i * FINAL, (i + 1) * FINAL)
            out_ref[span, :] = (accum[:, span] * inverse[:, span]).astype(out_ref.dtype).T
            copies.append(pltpu.make_async_copy(out_ref.at[span], out_hbm.at[span], sems.at[i]))
            copies[-1].start()
        for copy in copies:
            copy.wait()
    else:
        outs[0][...] = high
        outs[1][...] = total
        outs[2][...] = accum


def attend_call(pieces, part, own, query, state, datas, items, last, cost=0):
    head_width, query_rows = query.shape[0] // 2, query.shape[1]
    whole = pl.BlockSpec(memory_space=pltpu.VMEM)
    first = state is None
    operands = ([] if first else list(state)) + list(datas)
    if last:
        shapes = jax.ShapeDtypeStruct((query_rows, head_width), jnp.bfloat16)
        out_specs = pl.BlockSpec(memory_space=pl.ANY)
        scratch = [
            pltpu.VMEM((query_rows, head_width), jnp.bfloat16),
            pltpu.SemaphoreType.DMA((query_rows // FINAL,)),
        ]
    else:
        scratch = []
        shapes = [
            jax.ShapeDtypeStruct((1, query_rows), jnp.float32),
            jax.ShapeDtypeStruct((1, query_rows), jnp.float32),
            jax.ShapeDtypeStruct((head_width, query_rows), jnp.float32),
        ]
        out_specs = [whole] * 3
    return pl.pallas_call(
        functools.partial(attend, pieces, part, first, last, items),
        out_shape=shapes,
        in_specs=[whole] * (2 + len(operands)),
        out_specs=out_specs,
        scratch_shapes=scratch,
        compiler_params=pltpu.CompilerParams(vmem_limit_bytes=24 * MIB),
        cost_estimate=pl.CostEstimate(flops=cost, bytes_accessed=0, transcendentals=0),
    )(own, query, *operands)


def shards(queries, keys, values, block_ids):
    rows_dev, all_heads, head_width = queries.shape
    part, kv_heads = keys.shape[:2]
    head_index = lax.axis_index("head")
    pieces = lax.axis_size("head")
    blocks = lax.axis_size("seq")
    heads_out = all_heads // pieces
    own_queries = lax.dynamic_slice_in_dim(queries, head_index * heads_out, heads_out, 1)
    own_queries = own_queries.reshape(rows_dev * heads_out, head_width)
    whole = pl.BlockSpec(memory_space=pltpu.VMEM)
    scaled = pl.pallas_call(
        functools.partial(scale_queries, head_width ** (-0.5)),
        out_shape=jax.ShapeDtypeStruct((2 * head_width, rows_dev * heads_out), jnp.bfloat16),
        in_specs=[whole],
        out_specs=whole,
        compiler_params=pltpu.CompilerParams(vmem_limit_bytes=8 * MIB),
    )(own_queries)
    own, *payloads = pl.pallas_call(
        functools.partial(pack, pieces // kv_heads, pieces, part, kv_heads),
        out_shape=[jax.ShapeDtypeStruct((2 * part, head_width), jnp.bfloat16)] * pieces,
        in_specs=[whole],
        out_specs=[whole] * pieces,
        compiler_params=pltpu.CompilerParams(vmem_limit_bytes=4 * MIB),
    )(jnp.concatenate([keys, values]).reshape(2 * part * kv_heads, head_width))
    mark = jnp.broadcast_to(block_ids.astype(jnp.bfloat16)[:, None], (MARK, head_width))
    own = jnp.concatenate([own, mark])
    near = [
        lax.ppermute(rows, "head", [(i, (i + shift + 1) % pieces) for i in range(pieces)])
        for shift, rows in enumerate(payloads)
    ]
    rest = jnp.concatenate(near)
    fold = functools.partial(attend_call, pieces, part, own, scaled)
    shifts = tuple(range(pieces))
    offsets = tuple(2 * part * i for i in range(pieces))

    def swap(rows, flip):
        return lax.ppermute(rows, "seq", [(i, i ^ flip) for i in range(blocks)])

    if blocks == 8:
        rest = rest[None]
        ways = ((2, 4), (6, 2), (4, 6))

        def hop(rows, way):
            return lax.ppermute(rows, "seq", [(i, i ^ way[i & 1]) for i in range(blocks)])

        near_one, near_two, near_last = [hop(own, way) for way in ways]
        mine = jnp.stack([own, near_one, near_two])
        along_one, along_two, along_last = [hop(rest, way) for way in ways]

        def small(data, slots):
            return [(data, slot, (0,), None, (data, slot, 2 * part)) for slot in slots]

        def large(data, mark, slot, at=0):
            return (data, 0, tuple(at + offset for offset in offsets[:-1]), None, (mark, slot, 2 * part))

        state = fold(
            None,
            [mine, rest],
            [(0, 0, (0,), shifts[:1], None), (1, 0, offsets[:-1], shifts[1:], None)] + small(0, (1, 2)),
            False,
            OVERLAP,
        )
        early_rows = mine.shape[0] * mine.shape[1]
        both_other = swap(jnp.concatenate([mine.reshape(1, early_rows, head_width), rest], axis=1), 1)
        size = own.shape[0]
        state = fold(
            state,
            [both_other, near_last[None]],
            [(0, 0, (size * i,), None, (0, 0, size * i + 2 * part)) for i in range(3)]
            + [(0, 0, tuple(early_rows + offset for offset in offsets[:-1]), None, (0, 0, 2 * part))]
            + small(1, (0,)),
            False,
        )
        along_one, along_two, state = lax.optimization_barrier((along_one, along_two, state))
        others = [swap(rows, 1) for rows in (along_one, along_two)]
        state = fold(state, [mine, along_one, along_two], [large(i, 0, i) for i in (1, 2)], False)
        along_last, state = lax.optimization_barrier((along_last, state))
        along_last = jnp.concatenate([near_last[None], along_last], axis=1)
        along_last, *others = lax.optimization_barrier((along_last, *others))
        other_last = swap(along_last, 1)
        state = fold(
            state,
            [along_last, both_other] + others,
            [large(0, 0, 0, size)] + [(1 + i, 0, offsets[:-1], None, (1, 0, size * i + 2 * part)) for i in (1, 2)],
            False,
        )
        result = fold(
            state,
            [other_last],
            [(0, 0, (0,) + tuple(own.shape[0] + offset for offset in offsets[:-1]), None, (0, 0, 2 * part))],
            True,
        )
    else:
        block = jnp.concatenate([own[: 2 * part], rest, own[2 * part :]])
        far = lax.all_gather(block, "seq", axis=0, tiled=False)
        unit = math.gcd(blocks, 8)
        far = far.reshape((blocks // unit, unit) + block.shape)
        items = [(0, i, offsets, None, (0, i, 2 * part * pieces)) for i in range(unit)]
        state = fold(None, [block[None]], [(0, 0, offsets, shifts, None)], False)
        state, _ = lax.scan(
            lambda held, rows: (tuple(fold(held, [rows], items, False)), None), tuple(state), far[:-1]
        )
        result = fold(state, [far[-1]], items, True)
    return result.reshape(rows_dev, heads_out, head_width)


def solution(mesh):
    return jax.shard_map(
        shards,
        mesh=mesh,
        in_specs=(
            P("seq", None, None),
            P(("seq", "head"), None, None),
            P(("seq", "head"), None, None),
            P("seq"),
        ),
        out_specs=P("seq", "head", None),
        check_vma=False,
    )
```

```python
import functools
import math

import jax
import jax.numpy as jnp
from jax import lax
from jax.experimental import pallas as pl
from jax.experimental.pallas import tpu as pltpu
from jax.sharding import PartitionSpec as P

MARK = 16
SUBLANES = 8
FINAL = 256
OVERLAP = 1000000000
LOW = -1e30
HIGH = 1e30
MIB = 1024 * 1024


def pack(copies, pieces, part, kv_heads, rows_ref, *out_refs):
    here = lax.axis_index("head")
    rows = part * kv_heads
    at = lax.broadcasted_iota(jnp.int32, (part, rows), 0)
    source = lax.broadcasted_iota(jnp.int32, (part, rows), 1)
    picks = [
        jnp.where(source == at * kv_heads + head, 1.0, 0.0).astype(jnp.bfloat16) for head in range(kv_heads)
    ]
    for half in range(2):
        both = rows_ref[pl.ds(half * rows, rows), :]
        chosen = [jnp.dot(pick, both, preferred_element_type=jnp.float32).astype(jnp.bfloat16) for pick in picks]
        for shift, out_ref in enumerate(out_refs):
            kv_head = lax.rem(here + shift, pieces) // copies
            rows_out = chosen[0]
            for head in range(1, kv_heads):
                rows_out = jnp.where(kv_head == head, chosen[head], rows_out)
            out_ref[pl.ds(half * part, part), :] = rows_out


def scale_queries(scale, query_ref, out_ref):
    head_width = query_ref.shape[1]
    scaled = query_ref[...].astype(jnp.float32) * (scale * math.log2(math.e))
    coarse = scaled.astype(jnp.bfloat16)
    out_ref[:head_width, :] = coarse.T
    out_ref[head_width:, :] = (scaled - coarse.astype(jnp.float32)).astype(jnp.bfloat16).T


def attend(pieces, part, first, last, items, own_ref, query_ref, *refs):
    refs = list(refs)
    state = None if first else [refs.pop(0) for _ in range(3)]
    outs = [refs.pop() for _ in range(3)][::-1]
    head_width = query_ref.shape[0] // 2
    query_rows = query_ref.shape[1]
    group = query_rows // (pieces * part)
    here = lax.axis_index("head")
    own = own_ref[pl.ds(2 * part, MARK), :].astype(jnp.float32)[:SUBLANES]
    own = jnp.concatenate([own] * (query_rows // head_width), axis=1)

    blocks = []
    for data, slot, offsets, shifts, mark in items:
        rows_ref = refs[data].at[slot]
        if shifts is None:
            mark_data, mark_slot, mark_at = mark
            place = refs[mark_data][mark_slot, pl.ds(mark_at, MARK), :].astype(jnp.float32)[:SUBLANES]
            seen = jnp.concatenate([place] * (query_rows // head_width), axis=1) < own
        else:
            seen = None
        blocks.append((rows_ref, offsets, shifts, seen))

    def side(half):
        return jnp.concatenate(
            [
                rows_ref[pl.ds(offset + half * part, part), :]
                for rows_ref, offsets, _, _ in blocks
                for offset in offsets
            ]
        )

    keys = side(0)
    keys = jnp.concatenate([keys, keys], axis=1)
    values = side(1).T
    scores = jnp.dot(keys, query_ref[...], preferred_element_type=jnp.float32)
    cuts, tops, at = [], [], 0
    for _, offsets, shifts, seen in blocks:
        score = scores[at : at + len(offsets) * part]
        at += len(offsets) * part
        if seen is None:
            parts = []
            for i, shift in enumerate(shifts):
                cut = score[i * part : (i + 1) * part]
                key_at = lax.rem(here + pieces - shift, pieces) * part + lax.broadcasted_iota(jnp.int32, cut.shape, 0)
                query_at = lax.broadcasted_iota(jnp.int32, cut.shape, 1) // group
                parts.append(jnp.where(key_at <= query_at, cut, LOW))
            score = jnp.concatenate(parts)
        top = jnp.max(score.reshape(-1, SUBLANES, query_rows), axis=0)
        cuts.append(score)
        tops.append(top if seen is None else jnp.where(seen, top, LOW))
    high = jnp.max(functools.reduce(jnp.maximum, tops), axis=0, keepdims=True)
    if not first:
        old_high = state[0][...]
        high = jnp.maximum(old_high, high)
    weights, sums = [], []
    for score, (_, _, _, seen) in zip(cuts, blocks):
        base = high if seen is None else jnp.where(seen[:1], high, HIGH)
        expo = jnp.exp2(score - base)
        sums.append(jnp.sum(expo.reshape(-1, SUBLANES, query_rows), axis=0))
        weights.append(expo.astype(jnp.bfloat16))
    total = jnp.sum(functools.reduce(jnp.add, sums), axis=0, keepdims=True)
    accum = jnp.dot(values, jnp.concatenate(weights), preferred_element_type=jnp.float32)
    if not first:
        keep = jnp.exp2(old_high - high)
        total = total + state[1][...] * keep
        accum = accum + state[2][...] * keep
    if last:
        out_hbm, out_ref, sems = outs
        inverse = 1.0 / total
        copies = []
        for i in range(query_rows // FINAL):
            span = slice(i * FINAL, (i + 1) * FINAL)
            out_ref[span, :] = (accum[:, span] * inverse[:, span]).astype(out_ref.dtype).T
            copies.append(pltpu.make_async_copy(out_ref.at[span], out_hbm.at[span], sems.at[i]))
            copies[-1].start()
        for copy in copies:
            copy.wait()
    else:
        outs[0][...] = high
        outs[1][...] = total
        outs[2][...] = accum


def attend_call(pieces, part, own, query, state, datas, items, last, cost=0):
    head_width, query_rows = query.shape[0] // 2, query.shape[1]
    whole = pl.BlockSpec(memory_space=pltpu.VMEM)
    first = state is None
    operands = ([] if first else list(state)) + list(datas)
    if last:
        shapes = jax.ShapeDtypeStruct((query_rows, head_width), jnp.bfloat16)
        out_specs = pl.BlockSpec(memory_space=pl.ANY)
        scratch = [
            pltpu.VMEM((query_rows, head_width), jnp.bfloat16),
            pltpu.SemaphoreType.DMA((query_rows // FINAL,)),
        ]
    else:
        scratch = []
        shapes = [
            jax.ShapeDtypeStruct((1, query_rows), jnp.float32),
            jax.ShapeDtypeStruct((1, query_rows), jnp.float32),
            jax.ShapeDtypeStruct((head_width, query_rows), jnp.float32),
        ]
        out_specs = [whole] * 3
    return pl.pallas_call(
        functools.partial(attend, pieces, part, first, last, items),
        out_shape=shapes,
        in_specs=[whole] * (2 + len(operands)),
        out_specs=out_specs,
        scratch_shapes=scratch,
        compiler_params=pltpu.CompilerParams(vmem_limit_bytes=24 * MIB),
        cost_estimate=pl.CostEstimate(flops=cost, bytes_accessed=0, transcendentals=0),
    )(own, query, *operands)


def shards(queries, keys, values, block_ids):
    rows_dev, all_heads, head_width = queries.shape
    part, kv_heads = keys.shape[:2]
    head_index = lax.axis_index("head")
    pieces = lax.axis_size("head")
    blocks = lax.axis_size("seq")
    heads_out = all_heads // pieces
    own_queries = lax.dynamic_slice_in_dim(queries, head_index * heads_out, heads_out, 1)
    own_queries = own_queries.reshape(rows_dev * heads_out, head_width)
    whole = pl.BlockSpec(memory_space=pltpu.VMEM)
    scaled = pl.pallas_call(
        functools.partial(scale_queries, head_width ** (-0.5)),
        out_shape=jax.ShapeDtypeStruct((2 * head_width, rows_dev * heads_out), jnp.bfloat16),
        in_specs=[whole],
        out_specs=whole,
        compiler_params=pltpu.CompilerParams(vmem_limit_bytes=8 * MIB),
    )(own_queries)
    own, *payloads = pl.pallas_call(
        functools.partial(pack, pieces // kv_heads, pieces, part, kv_heads),
        out_shape=[jax.ShapeDtypeStruct((2 * part, head_width), jnp.bfloat16)] * pieces,
        in_specs=[whole],
        out_specs=[whole] * pieces,
        compiler_params=pltpu.CompilerParams(vmem_limit_bytes=4 * MIB),
    )(jnp.concatenate([keys, values]).reshape(2 * part * kv_heads, head_width))
    mark = jnp.broadcast_to(block_ids.astype(jnp.bfloat16)[:, None], (MARK, head_width))
    own = jnp.concatenate([own, mark])
    near = [
        lax.ppermute(rows, "head", [(i, (i + shift + 1) % pieces) for i in range(pieces)])
        for shift, rows in enumerate(payloads)
    ]
    rest = jnp.concatenate(near)
    fold = functools.partial(attend_call, pieces, part, own, scaled)
    shifts = tuple(range(pieces))
    offsets = tuple(2 * part * i for i in range(pieces))

    def swap(rows, flip):
        return lax.ppermute(rows, "seq", [(i, i ^ flip) for i in range(blocks)])

    if blocks == 8:
        rest = rest[None]
        ways = ((2, 4), (6, 6), (4, 2))

        def hop(rows, way):
            return lax.ppermute(rows, "seq", [(i, i ^ way[i & 1]) for i in range(blocks)])

        near_one, near_two, near_last = [hop(own, way) for way in ways]
        mine = jnp.stack([own, near_one, near_two])
        along_one, along_two, along_last = [hop(rest, way) for way in ways]

        def small(data, slots):
            return [(data, slot, (0,), None, (data, slot, 2 * part)) for slot in slots]

        def large(data, mark, slot, at=0):
            return (data, 0, tuple(at + offset for offset in offsets[:-1]), None, (mark, slot, 2 * part))

        state = fold(
            None,
            [mine, rest],
            [(0, 0, (0,), shifts[:1], None), (1, 0, offsets[:-1], shifts[1:], None)] + small(0, (1, 2)),
            False,
            OVERLAP,
        )
        early_rows = mine.shape[0] * mine.shape[1]
        both_other = swap(jnp.concatenate([mine.reshape(1, early_rows, head_width), rest], axis=1), 1)
        size = own.shape[0]
        state = fold(
            state,
            [both_other, near_last[None]],
            [(0, 0, (size * i,), None, (0, 0, size * i + 2 * part)) for i in range(3)]
            + [(0, 0, tuple(early_rows + offset for offset in offsets[:-1]), None, (0, 0, 2 * part))]
            + small(1, (0,)),
            False,
        )
        along_one, along_two, state = lax.optimization_barrier((along_one, along_two, state))
        others = swap(jnp.concatenate([along_one, along_two]), 1)
        state = fold(state, [mine, along_one, along_two], [large(i, 0, i) for i in (1, 2)], False)
        along_last, state = lax.optimization_barrier((along_last, state))
        along_last = jnp.concatenate([near_last[None], along_last], axis=1)
        along_last, others = lax.optimization_barrier((along_last, others))
        other_last = swap(along_last, 1)
        state = fold(
            state,
            [along_last, both_other, others],
            [large(0, 0, 0, size)] + [(2, i - 1, offsets[:-1], None, (1, 0, size * i + 2 * part)) for i in (1, 2)],
            False,
        )
        result = fold(
            state,
            [other_last],
            [(0, 0, (0,) + tuple(own.shape[0] + offset for offset in offsets[:-1]), None, (0, 0, 2 * part))],
            True,
        )
    else:
        block = jnp.concatenate([own[: 2 * part], rest, own[2 * part :]])
        far = lax.all_gather(block, "seq", axis=0, tiled=False)
        unit = math.gcd(blocks, 8)
        far = far.reshape((blocks // unit, unit) + block.shape)
        items = [(0, i, offsets, None, (0, i, 2 * part * pieces)) for i in range(unit)]
        state = fold(None, [block[None]], [(0, 0, offsets, shifts, None)], False)
        state, _ = lax.scan(
            lambda held, rows: (tuple(fold(held, [rows], items, False)), None), tuple(state), far[:-1]
        )
        result = fold(state, [far[-1]], items, True)
    return result.reshape(rows_dev, heads_out, head_width)


def solution(mesh):
    return jax.shard_map(
        shards,
        mesh=mesh,
        in_specs=(
            P("seq", None, None),
            P(("seq", "head"), None, None),
            P(("seq", "head"), None, None),
            P("seq"),
        ),
        out_specs=P("seq", "head", None),
        check_vma=False,
    )
```

```python
import functools
import math

import jax
import jax.numpy as jnp
from jax import lax
from jax.experimental import pallas as pl
from jax.experimental.pallas import tpu as pltpu
from jax.sharding import PartitionSpec as P

MARK = 16
SUBLANES = 8
FINAL = 256
OVERLAP = 1000000000
LOW = -1e30
HIGH = 1e30
MIB = 1024 * 1024


def pack(copies, pieces, part, kv_heads, rows_ref, *out_refs):
    here = lax.axis_index("head")
    rows = part * kv_heads
    at = lax.broadcasted_iota(jnp.int32, (part, rows), 0)
    source = lax.broadcasted_iota(jnp.int32, (part, rows), 1)
    picks = [
        jnp.where(source == at * kv_heads + head, 1.0, 0.0).astype(jnp.bfloat16) for head in range(kv_heads)
    ]
    for half in range(2):
        both = rows_ref[pl.ds(half * rows, rows), :]
        chosen = [jnp.dot(pick, both, preferred_element_type=jnp.float32).astype(jnp.bfloat16) for pick in picks]
        for shift, out_ref in enumerate(out_refs):
            kv_head = lax.rem(here + shift, pieces) // copies
            rows_out = chosen[0]
            for head in range(1, kv_heads):
                rows_out = jnp.where(kv_head == head, chosen[head], rows_out)
            out_ref[pl.ds(half * part, part), :] = rows_out


def turn_queries(query_ref, out_ref):
    out_ref[...] = query_ref[...].T


def attend(pieces, part, first, last, items, own_ref, query_ref, *refs):
    refs = list(refs)
    state = None if first else [refs.pop(0) for _ in range(3)]
    outs = [refs.pop() for _ in range(3)][::-1]
    head_width = query_ref.shape[0]
    factor = head_width ** (-0.5) * math.log2(math.e)
    query_rows = query_ref.shape[1]
    group = query_rows // (pieces * part)
    here = lax.axis_index("head")
    own = own_ref[pl.ds(2 * part, MARK), :].astype(jnp.float32)[:SUBLANES]
    own = jnp.concatenate([own] * (query_rows // head_width), axis=1)

    blocks = []
    for data, slot, offsets, shifts, mark in items:
        rows_ref = refs[data].at[slot]
        if shifts is None:
            mark_data, mark_slot, mark_at = mark
            place = refs[mark_data][mark_slot, pl.ds(mark_at, MARK), :].astype(jnp.float32)[:SUBLANES]
            seen = jnp.concatenate([place] * (query_rows // head_width), axis=1) < own
        else:
            seen = None
        blocks.append((rows_ref, offsets, shifts, seen))

    def side(half):
        return jnp.concatenate(
            [
                rows_ref[pl.ds(offset + half * part, part), :]
                for rows_ref, offsets, _, _ in blocks
                for offset in offsets
            ]
        )

    keys = side(0)
    values = side(1).T
    scores = jnp.dot(keys, query_ref[...], preferred_element_type=jnp.float32)
    cuts, tops, at = [], [], 0
    for _, offsets, shifts, seen in blocks:
        score = scores[at : at + len(offsets) * part]
        at += len(offsets) * part
        if seen is None:
            parts = []
            for i, shift in enumerate(shifts):
                cut = score[i * part : (i + 1) * part]
                key_at = lax.rem(here + pieces - shift, pieces) * part + lax.broadcasted_iota(jnp.int32, cut.shape, 0)
                query_at = lax.broadcasted_iota(jnp.int32, cut.shape, 1) // group
                parts.append(jnp.where(key_at <= query_at, cut, LOW))
            score = jnp.concatenate(parts)
        top = jnp.max(score.reshape(-1, SUBLANES, query_rows), axis=0)
        cuts.append(score)
        tops.append(top if seen is None else jnp.where(seen, top, LOW))
    high = jnp.max(functools.reduce(jnp.maximum, tops), axis=0, keepdims=True)
    if not first:
        old_high = state[0][...]
        high = jnp.maximum(old_high, high)
    weights, sums = [], []
    for score, (_, _, _, seen) in zip(cuts, blocks):
        base = high if seen is None else jnp.where(seen[:1], high, HIGH)
        expo = jnp.exp2((score - base) * factor)
        sums.append(jnp.sum(expo.reshape(-1, SUBLANES, query_rows), axis=0))
        weights.append(expo.astype(jnp.bfloat16))
    total = jnp.sum(functools.reduce(jnp.add, sums), axis=0, keepdims=True)
    accum = jnp.dot(values, jnp.concatenate(weights), preferred_element_type=jnp.float32)
    if not first:
        keep = jnp.exp2((old_high - high) * factor)
        total = total + state[1][...] * keep
        accum = accum + state[2][...] * keep
    if last:
        out_hbm, out_ref, sems = outs
        inverse = 1.0 / total
        copies = []
        for i in range(query_rows // FINAL):
            span = slice(i * FINAL, (i + 1) * FINAL)
            out_ref[span, :] = (accum[:, span] * inverse[:, span]).astype(out_ref.dtype).T
            copies.append(pltpu.make_async_copy(out_ref.at[span], out_hbm.at[span], sems.at[i]))
            copies[-1].start()
        for copy in copies:
            copy.wait()
    else:
        outs[0][...] = high
        outs[1][...] = total
        outs[2][...] = accum


def attend_call(pieces, part, own, query, state, datas, items, last, cost=0):
    head_width, query_rows = query.shape
    whole = pl.BlockSpec(memory_space=pltpu.VMEM)
    first = state is None
    operands = ([] if first else list(state)) + list(datas)
    if last:
        shapes = jax.ShapeDtypeStruct((query_rows, head_width), jnp.bfloat16)
        out_specs = pl.BlockSpec(memory_space=pl.ANY)
        scratch = [
            pltpu.VMEM((query_rows, head_width), jnp.bfloat16),
            pltpu.SemaphoreType.DMA((query_rows // FINAL,)),
        ]
    else:
        scratch = []
        shapes = [
            jax.ShapeDtypeStruct((1, query_rows), jnp.float32),
            jax.ShapeDtypeStruct((1, query_rows), jnp.float32),
            jax.ShapeDtypeStruct((head_width, query_rows), jnp.float32),
        ]
        out_specs = [whole] * 3
    return pl.pallas_call(
        functools.partial(attend, pieces, part, first, last, items),
        out_shape=shapes,
        in_specs=[whole] * (2 + len(operands)),
        out_specs=out_specs,
        scratch_shapes=scratch,
        compiler_params=pltpu.CompilerParams(vmem_limit_bytes=24 * MIB),
        cost_estimate=pl.CostEstimate(flops=cost, bytes_accessed=0, transcendentals=0),
    )(own, query, *operands)


def shards(queries, keys, values, block_ids):
    rows_dev, all_heads, head_width = queries.shape
    part, kv_heads = keys.shape[:2]
    head_index = lax.axis_index("head")
    pieces = lax.axis_size("head")
    blocks = lax.axis_size("seq")
    heads_out = all_heads // pieces
    own_queries = lax.dynamic_slice_in_dim(queries, head_index * heads_out, heads_out, 1)
    own_queries = own_queries.reshape(rows_dev * heads_out, head_width)
    whole = pl.BlockSpec(memory_space=pltpu.VMEM)
    turned = pl.pallas_call(
        turn_queries,
        out_shape=jax.ShapeDtypeStruct((head_width, rows_dev * heads_out), jnp.bfloat16),
        in_specs=[whole],
        out_specs=whole,
        compiler_params=pltpu.CompilerParams(vmem_limit_bytes=8 * MIB),
    )(own_queries)
    own, *payloads = pl.pallas_call(
        functools.partial(pack, pieces // kv_heads, pieces, part, kv_heads),
        out_shape=[jax.ShapeDtypeStruct((2 * part, head_width), jnp.bfloat16)] * pieces,
        in_specs=[whole],
        out_specs=[whole] * pieces,
        compiler_params=pltpu.CompilerParams(vmem_limit_bytes=4 * MIB),
    )(jnp.concatenate([keys, values]).reshape(2 * part * kv_heads, head_width))
    mark = jnp.broadcast_to(block_ids.astype(jnp.bfloat16)[:, None], (MARK, head_width))
    own = jnp.concatenate([own, mark])
    near = [
        lax.ppermute(rows, "head", [(i, (i + shift + 1) % pieces) for i in range(pieces)])
        for shift, rows in enumerate(payloads)
    ]
    rest = jnp.concatenate(near)
    fold = functools.partial(attend_call, pieces, part, own, turned)
    shifts = tuple(range(pieces))
    offsets = tuple(2 * part * i for i in range(pieces))

    def swap(rows, flip):
        return lax.ppermute(rows, "seq", [(i, i ^ flip) for i in range(blocks)])

    if blocks == 8:
        rest = rest[None]
        ways = ((2, 4), (6, 6), (4, 2))

        def hop(rows, way):
            return lax.ppermute(rows, "seq", [(i, i ^ way[i & 1]) for i in range(blocks)])

        near_one, near_two, near_last = [hop(own, way) for way in ways]
        mine = jnp.stack([own, near_one, near_two])
        along_one, along_two, along_last = [hop(rest, way) for way in ways]

        def small(data, slots):
            return [(data, slot, (0,), None, (data, slot, 2 * part)) for slot in slots]

        def large(data, mark, slot, at=0):
            return (data, 0, tuple(at + offset for offset in offsets[:-1]), None, (mark, slot, 2 * part))

        state = fold(
            None,
            [mine, rest],
            [(0, 0, (0,), shifts[:1], None), (1, 0, offsets[:-1], shifts[1:], None)] + small(0, (1, 2)),
            False,
            OVERLAP,
        )
        early_rows = mine.shape[0] * mine.shape[1]
        both_other = swap(jnp.concatenate([mine.reshape(1, early_rows, head_width), rest], axis=1), 1)
        size = own.shape[0]
        state = fold(
            state,
            [both_other, near_last[None]],
            [(0, 0, (size * i,), None, (0, 0, size * i + 2 * part)) for i in range(3)]
            + [(0, 0, tuple(early_rows + offset for offset in offsets[:-1]), None, (0, 0, 2 * part))]
            + small(1, (0,)),
            False,
        )
        along_one, along_two, state = lax.optimization_barrier((along_one, along_two, state))
        others = swap(jnp.concatenate([along_one, along_two]), 1)
        state = fold(state, [mine, along_one, along_two], [large(i, 0, i) for i in (1, 2)], False)
        along_last, state = lax.optimization_barrier((along_last, state))
        along_last = jnp.concatenate([near_last[None], along_last], axis=1)
        along_last, others = lax.optimization_barrier((along_last, others))
        other_last = swap(along_last, 1)
        state = fold(
            state,
            [along_last, both_other, others],
            [large(0, 0, 0, size)] + [(2, i - 1, offsets[:-1], None, (1, 0, size * i + 2 * part)) for i in (1, 2)],
            False,
        )
        result = fold(
            state,
            [other_last],
            [(0, 0, (0,) + tuple(own.shape[0] + offset for offset in offsets[:-1]), None, (0, 0, 2 * part))],
            True,
        )
    else:
        block = jnp.concatenate([own[: 2 * part], rest, own[2 * part :]])
        far = lax.all_gather(block, "seq", axis=0, tiled=False)
        unit = math.gcd(blocks, 8)
        far = far.reshape((blocks // unit, unit) + block.shape)
        items = [(0, i, offsets, None, (0, i, 2 * part * pieces)) for i in range(unit)]
        state = fold(None, [block[None]], [(0, 0, offsets, shifts, None)], False)
        state, _ = lax.scan(
            lambda held, rows: (tuple(fold(held, [rows], items, False)), None), tuple(state), far[:-1]
        )
        result = fold(state, [far[-1]], items, True)
    return result.reshape(rows_dev, heads_out, head_width)


def solution(mesh):
    return jax.shard_map(
        shards,
        mesh=mesh,
        in_specs=(
            P("seq", None, None),
            P(("seq", "head"), None, None),
            P(("seq", "head"), None, None),
            P("seq"),
        ),
        out_specs=P("seq", "head", None),
        check_vma=False,
    )
```

```python
import functools
import math

import jax
import jax.numpy as jnp
from jax import lax
from jax.experimental import pallas as pl
from jax.experimental.pallas import tpu as pltpu
from jax.sharding import PartitionSpec as P

MARK = 16
SUBLANES = 8
FINAL = 256
OVERLAP = 0
LOW = -1e30
HIGH = 1e30
MIB = 1024 * 1024


def pack(copies, pieces, part, kv_heads, rows_ref, *out_refs):
    here = lax.axis_index("head")
    rows = part * kv_heads
    at = lax.broadcasted_iota(jnp.int32, (part, rows), 0)
    source = lax.broadcasted_iota(jnp.int32, (part, rows), 1)
    picks = [
        jnp.where(source == at * kv_heads + head, 1.0, 0.0).astype(jnp.bfloat16) for head in range(kv_heads)
    ]
    for half in range(2):
        both = rows_ref[pl.ds(half * rows, rows), :]
        chosen = [jnp.dot(pick, both, preferred_element_type=jnp.float32).astype(jnp.bfloat16) for pick in picks]
        for shift, out_ref in enumerate(out_refs):
            kv_head = lax.rem(here + shift, pieces) // copies
            rows_out = chosen[0]
            for head in range(1, kv_heads):
                rows_out = jnp.where(kv_head == head, chosen[head], rows_out)
            out_ref[pl.ds(half * part, part), :] = rows_out


def scale_queries(scale, query_ref, out_ref):
    head_width = query_ref.shape[1]
    scaled = query_ref[...].astype(jnp.float32) * (scale * math.log2(math.e))
    coarse = scaled.astype(jnp.bfloat16)
    out_ref[:head_width, :] = coarse.T
    out_ref[head_width:, :] = (scaled - coarse.astype(jnp.float32)).astype(jnp.bfloat16).T


def attend(pieces, part, first, last, items, own_ref, query_ref, *refs):
    refs = list(refs)
    state = None if first else [refs.pop(0) for _ in range(3)]
    outs = [refs.pop() for _ in range(3)][::-1]
    head_width = query_ref.shape[0] // 2
    query_rows = query_ref.shape[1]
    group = query_rows // (pieces * part)
    here = lax.axis_index("head")
    own = own_ref[pl.ds(2 * part, MARK), :].astype(jnp.float32)[:SUBLANES]
    own = jnp.concatenate([own] * (query_rows // head_width), axis=1)

    blocks = []
    for data, slot, offsets, shifts, mark in items:
        rows_ref = refs[data].at[slot]
        if shifts is None:
            mark_data, mark_slot, mark_at = mark
            place = refs[mark_data][mark_slot, pl.ds(mark_at, MARK), :].astype(jnp.float32)[:SUBLANES]
            seen = jnp.concatenate([place] * (query_rows // head_width), axis=1) < own
        else:
            seen = None
        blocks.append((rows_ref, offsets, shifts, seen))

    def side(half):
        return jnp.concatenate(
            [
                rows_ref[pl.ds(offset + half * part, part), :]
                for rows_ref, offsets, _, _ in blocks
                for offset in offsets
            ]
        )

    keys = side(0)
    keys = jnp.concatenate([keys, keys], axis=1)
    values = side(1).T
    scores = jnp.dot(keys, query_ref[...], preferred_element_type=jnp.float32)
    cuts, tops, at = [], [], 0
    for _, offsets, shifts, seen in blocks:
        score = scores[at : at + len(offsets) * part]
        at += len(offsets) * part
        if seen is None:
            parts = []
            for i, shift in enumerate(shifts):
                cut = score[i * part : (i + 1) * part]
                key_at = lax.rem(here + pieces - shift, pieces) * part + lax.broadcasted_iota(jnp.int32, cut.shape, 0)
                query_at = lax.broadcasted_iota(jnp.int32, cut.shape, 1) // group
                parts.append(jnp.where(key_at <= query_at, cut, LOW))
            score = jnp.concatenate(parts)
        top = jnp.max(score.reshape(-1, SUBLANES, query_rows), axis=0)
        cuts.append(score)
        tops.append(top if seen is None else jnp.where(seen, top, LOW))
    high = jnp.max(functools.reduce(jnp.maximum, tops), axis=0, keepdims=True)
    if not first:
        old_high = state[0][...]
        high = jnp.maximum(old_high, high)
    weights, sums = [], []
    for score, (_, _, _, seen) in zip(cuts, blocks):
        base = high if seen is None else jnp.where(seen[:1], high, HIGH)
        expo = jnp.exp2(score - base)
        sums.append(jnp.sum(expo.reshape(-1, SUBLANES, query_rows), axis=0))
        weights.append(expo.astype(jnp.bfloat16))
    total = jnp.sum(functools.reduce(jnp.add, sums), axis=0, keepdims=True)
    accum = jnp.dot(values, jnp.concatenate(weights), preferred_element_type=jnp.float32)
    if not first:
        keep = jnp.exp2(old_high - high)
        total = total + state[1][...] * keep
        accum = accum + state[2][...] * keep
    if last:
        out_hbm, out_ref, sems = outs
        inverse = 1.0 / total
        copies = []
        for i in range(query_rows // FINAL):
            span = slice(i * FINAL, (i + 1) * FINAL)
            out_ref[span, :] = (accum[:, span] * inverse[:, span]).astype(out_ref.dtype).T
            copies.append(pltpu.make_async_copy(out_ref.at[span], out_hbm.at[span], sems.at[i]))
            copies[-1].start()
        for copy in copies:
            copy.wait()
    else:
        outs[0][...] = high
        outs[1][...] = total
        outs[2][...] = accum


def attend_call(pieces, part, own, query, state, datas, items, last, cost=0):
    head_width, query_rows = query.shape[0] // 2, query.shape[1]
    whole = pl.BlockSpec(memory_space=pltpu.VMEM)
    first = state is None
    operands = ([] if first else list(state)) + list(datas)
    if last:
        shapes = jax.ShapeDtypeStruct((query_rows, head_width), jnp.bfloat16)
        out_specs = pl.BlockSpec(memory_space=pl.ANY)
        scratch = [
            pltpu.VMEM((query_rows, head_width), jnp.bfloat16),
            pltpu.SemaphoreType.DMA((query_rows // FINAL,)),
        ]
    else:
        scratch = []
        shapes = [
            jax.ShapeDtypeStruct((1, query_rows), jnp.float32),
            jax.ShapeDtypeStruct((1, query_rows), jnp.float32),
            jax.ShapeDtypeStruct((head_width, query_rows), jnp.float32),
        ]
        out_specs = [whole] * 3
    return pl.pallas_call(
        functools.partial(attend, pieces, part, first, last, items),
        out_shape=shapes,
        in_specs=[whole] * (2 + len(operands)),
        out_specs=out_specs,
        scratch_shapes=scratch,
        compiler_params=pltpu.CompilerParams(vmem_limit_bytes=24 * MIB),
        cost_estimate=pl.CostEstimate(flops=cost, bytes_accessed=0, transcendentals=0),
    )(own, query, *operands)


def shards(queries, keys, values, block_ids):
    rows_dev, all_heads, head_width = queries.shape
    part, kv_heads = keys.shape[:2]
    head_index = lax.axis_index("head")
    pieces = lax.axis_size("head")
    blocks = lax.axis_size("seq")
    heads_out = all_heads // pieces
    own_queries = lax.dynamic_slice_in_dim(queries, head_index * heads_out, heads_out, 1)
    own_queries = own_queries.reshape(rows_dev * heads_out, head_width)
    whole = pl.BlockSpec(memory_space=pltpu.VMEM)
    scaled = pl.pallas_call(
        functools.partial(scale_queries, head_width ** (-0.5)),
        out_shape=jax.ShapeDtypeStruct((2 * head_width, rows_dev * heads_out), jnp.bfloat16),
        in_specs=[whole],
        out_specs=whole,
        compiler_params=pltpu.CompilerParams(vmem_limit_bytes=8 * MIB),
    )(own_queries)
    own, *payloads = pl.pallas_call(
        functools.partial(pack, pieces // kv_heads, pieces, part, kv_heads),
        out_shape=[jax.ShapeDtypeStruct((2 * part, head_width), jnp.bfloat16)] * pieces,
        in_specs=[whole],
        out_specs=[whole] * pieces,
        compiler_params=pltpu.CompilerParams(vmem_limit_bytes=4 * MIB),
    )(jnp.concatenate([keys, values]).reshape(2 * part * kv_heads, head_width))
    mark = jnp.broadcast_to(block_ids.astype(jnp.bfloat16)[:, None], (MARK, head_width))
    own = jnp.concatenate([own, mark])
    near = [
        lax.ppermute(rows, "head", [(i, (i + shift + 1) % pieces) for i in range(pieces)])
        for shift, rows in enumerate(payloads)
    ]
    rest = jnp.concatenate(near)
    fold = functools.partial(attend_call, pieces, part, own, scaled)
    shifts = tuple(range(pieces))
    offsets = tuple(2 * part * i for i in range(pieces))

    def swap(rows, flip):
        return lax.ppermute(rows, "seq", [(i, i ^ flip) for i in range(blocks)])

    if blocks == 8:
        rest = rest[None]
        ways = ((2, 4), (6, 6), (4, 2))

        def hop(rows, way):
            return lax.ppermute(rows, "seq", [(i, i ^ way[i & 1]) for i in range(blocks)])

        near_one, near_two = [hop(own, way) for way in ways[:2]]
        mine = jnp.stack([own, near_one, near_two])
        along_one, along_two = [hop(rest, way) for way in ways[:2]]
        along_last = hop(jnp.concatenate([own[None], rest], axis=1), ways[2])

        def small(data, slots):
            return [(data, slot, (0,), None, (data, slot, 2 * part)) for slot in slots]

        def large(data, mark, slot, at=0):
            return (data, 0, tuple(at + offset for offset in offsets[:-1]), None, (mark, slot, 2 * part))

        state = fold(
            None,
            [mine, rest],
            [(0, 0, (0,), shifts[:1], None), (1, 0, offsets[:-1], shifts[1:], None)] + small(0, (1, 2)),
            False,
            OVERLAP,
        )
        early_rows = mine.shape[0] * mine.shape[1]
        both_other = swap(jnp.concatenate([mine.reshape(1, early_rows, head_width), rest], axis=1), 1)
        size = own.shape[0]
        state = fold(
            state,
            [both_other],
            [(0, 0, (size * i,), None, (0, 0, size * i + 2 * part)) for i in range(3)]
            + [(0, 0, tuple(early_rows + offset for offset in offsets[:-1]), None, (0, 0, 2 * part))],
            False,
        )
        along_one, along_two, state = lax.optimization_barrier((along_one, along_two, state))
        others = [swap(rows, 1) for rows in (along_one, along_two)]
        state = fold(state, [mine, along_one, along_two], [large(i, 0, i) for i in (1, 2)], False)
        along_last, state = lax.optimization_barrier((along_last, state))
        along_last, *others = lax.optimization_barrier((along_last, *others))
        other_last = swap(along_last, 1)
        state = fold(
            state,
            [along_last, both_other] + others,
            [(0, 0, (0,) + tuple(size + offset for offset in offsets[:-1]), None, (0, 0, 2 * part))] + [(1 + i, 0, offsets[:-1], None, (1, 0, size * i + 2 * part)) for i in (1, 2)],
            False,
        )
        result = fold(
            state,
            [other_last],
            [(0, 0, (0,) + tuple(own.shape[0] + offset for offset in offsets[:-1]), None, (0, 0, 2 * part))],
            True,
        )
    else:
        block = jnp.concatenate([own[: 2 * part], rest, own[2 * part :]])
        far = lax.all_gather(block, "seq", axis=0, tiled=False)
        unit = math.gcd(blocks, 8)
        far = far.reshape((blocks // unit, unit) + block.shape)
        items = [(0, i, offsets, None, (0, i, 2 * part * pieces)) for i in range(unit)]
        state = fold(None, [block[None]], [(0, 0, offsets, shifts, None)], False)
        state, _ = lax.scan(
            lambda held, rows: (tuple(fold(held, [rows], items, False)), None), tuple(state), far[:-1]
        )
        result = fold(state, [far[-1]], items, True)
    return result.reshape(rows_dev, heads_out, head_width)


def solution(mesh):
    return jax.shard_map(
        shards,
        mesh=mesh,
        in_specs=(
            P("seq", None, None),
            P(("seq", "head"), None, None),
            P(("seq", "head"), None, None),
            P("seq"),
        ),
        out_specs=P("seq", "head", None),
        check_vma=False,
    )
```

```python
import functools
import math

import jax
import jax.numpy as jnp
from jax import lax
from jax.experimental import pallas as pl
from jax.experimental.pallas import tpu as pltpu
from jax.sharding import PartitionSpec as P

MARK = 16
SUBLANES = 8
FINAL = 256
OVERLAP = 0
LOW = -1e30
HIGH = 1e30
MIB = 1024 * 1024


def pack(copies, pieces, part, kv_heads, rows_ref, *out_refs):
    here = lax.axis_index("head")
    rows = part * kv_heads
    at = lax.broadcasted_iota(jnp.int32, (part, rows), 0)
    source = lax.broadcasted_iota(jnp.int32, (part, rows), 1)
    picks = [
        jnp.where(source == at * kv_heads + head, 1.0, 0.0).astype(jnp.bfloat16) for head in range(kv_heads)
    ]
    for half in range(2):
        both = rows_ref[pl.ds(half * rows, rows), :]
        chosen = [jnp.dot(pick, both, preferred_element_type=jnp.float32).astype(jnp.bfloat16) for pick in picks]
        for shift, out_ref in enumerate(out_refs):
            kv_head = lax.rem(here + shift, pieces) // copies
            rows_out = chosen[0]
            for head in range(1, kv_heads):
                rows_out = jnp.where(kv_head == head, chosen[head], rows_out)
            out_ref[pl.ds(half * part, part), :] = rows_out


def scale_queries(scale, query_ref, out_ref):
    head_width = query_ref.shape[1]
    scaled = query_ref[...].astype(jnp.float32) * (scale * math.log2(math.e))
    coarse = scaled.astype(jnp.bfloat16)
    out_ref[:head_width, :] = coarse.T
    out_ref[head_width:, :] = (scaled - coarse.astype(jnp.float32)).astype(jnp.bfloat16).T


def attend(pieces, part, first, last, items, own_ref, query_ref, *refs):
    refs = list(refs)
    state = None if first else [refs.pop(0) for _ in range(3)]
    outs = [refs.pop() for _ in range(3)][::-1]
    head_width = query_ref.shape[0] // 2
    query_rows = query_ref.shape[1]
    group = query_rows // (pieces * part)
    here = lax.axis_index("head")
    own = own_ref[pl.ds(2 * part, MARK), :].astype(jnp.float32)[:SUBLANES]
    own = jnp.concatenate([own] * (query_rows // head_width), axis=1)

    blocks = []
    for data, slot, offsets, shifts, mark in items:
        rows_ref = refs[data].at[slot]
        if shifts is None:
            mark_data, mark_slot, mark_at = mark
            place = refs[mark_data][mark_slot, pl.ds(mark_at, MARK), :].astype(jnp.float32)[:SUBLANES]
            seen = jnp.concatenate([place] * (query_rows // head_width), axis=1) < own
        else:
            seen = None
        blocks.append((rows_ref, offsets, shifts, seen))

    def side(half):
        return jnp.concatenate(
            [
                rows_ref[pl.ds(offset + half * part, part), :]
                for rows_ref, offsets, _, _ in blocks
                for offset in offsets
            ]
        )

    keys = side(0)
    keys = jnp.concatenate([keys, keys], axis=1)
    values = side(1).T
    scores = jnp.dot(keys, query_ref[...], preferred_element_type=jnp.float32)
    cuts, tops, at = [], [], 0
    for _, offsets, shifts, seen in blocks:
        score = scores[at : at + len(offsets) * part]
        at += len(offsets) * part
        if seen is None:
            parts = []
            for i, shift in enumerate(shifts):
                cut = score[i * part : (i + 1) * part]
                key_at = lax.rem(here + pieces - shift, pieces) * part + lax.broadcasted_iota(jnp.int32, cut.shape, 0)
                query_at = lax.broadcasted_iota(jnp.int32, cut.shape, 1) // group
                parts.append(jnp.where(key_at <= query_at, cut, LOW))
            score = jnp.concatenate(parts)
        top = jnp.max(score.reshape(-1, SUBLANES, query_rows), axis=0)
        cuts.append(score)
        tops.append(top if seen is None else jnp.where(seen, top, LOW))
    high = jnp.max(functools.reduce(jnp.maximum, tops), axis=0, keepdims=True)
    if not first:
        old_high = state[0][...]
        high = jnp.maximum(old_high, high)
    weights, sums = [], []
    for score, (_, _, _, seen) in zip(cuts, blocks):
        base = high if seen is None else jnp.where(seen[:1], high, HIGH)
        expo = jnp.exp2(score - base)
        sums.append(jnp.sum(expo.reshape(-1, SUBLANES, query_rows), axis=0))
        weights.append(expo.astype(jnp.bfloat16))
    total = jnp.sum(functools.reduce(jnp.add, sums), axis=0, keepdims=True)
    accum = jnp.dot(values, jnp.concatenate(weights), preferred_element_type=jnp.float32)
    if not first:
        keep = jnp.exp2(old_high - high)
        total = total + state[1][...] * keep
        accum = accum + state[2][...] * keep
    if last:
        out_hbm, out_ref, sems = outs
        inverse = 1.0 / total
        copies = []
        for i in range(query_rows // FINAL):
            span = slice(i * FINAL, (i + 1) * FINAL)
            out_ref[span, :] = (accum[:, span] * inverse[:, span]).astype(out_ref.dtype).T
            copies.append(pltpu.make_async_copy(out_ref.at[span], out_hbm.at[span], sems.at[i]))
            copies[-1].start()
        for copy in copies:
            copy.wait()
    else:
        outs[0][...] = high
        outs[1][...] = total
        outs[2][...] = accum


def attend_call(pieces, part, own, query, state, datas, items, last, cost=0):
    head_width, query_rows = query.shape[0] // 2, query.shape[1]
    whole = pl.BlockSpec(memory_space=pltpu.VMEM)
    first = state is None
    operands = ([] if first else list(state)) + list(datas)
    if last:
        shapes = jax.ShapeDtypeStruct((query_rows, head_width), jnp.bfloat16)
        out_specs = pl.BlockSpec(memory_space=pl.ANY)
        scratch = [
            pltpu.VMEM((query_rows, head_width), jnp.bfloat16),
            pltpu.SemaphoreType.DMA((query_rows // FINAL,)),
        ]
    else:
        scratch = []
        shapes = [
            jax.ShapeDtypeStruct((1, query_rows), jnp.float32),
            jax.ShapeDtypeStruct((1, query_rows), jnp.float32),
            jax.ShapeDtypeStruct((head_width, query_rows), jnp.float32),
        ]
        out_specs = [whole] * 3
    return pl.pallas_call(
        functools.partial(attend, pieces, part, first, last, items),
        out_shape=shapes,
        in_specs=[whole] * (2 + len(operands)),
        out_specs=out_specs,
        scratch_shapes=scratch,
        compiler_params=pltpu.CompilerParams(vmem_limit_bytes=24 * MIB),
        cost_estimate=pl.CostEstimate(flops=cost, bytes_accessed=0, transcendentals=0),
    )(own, query, *operands)


def shards(queries, keys, values, block_ids):
    rows_dev, all_heads, head_width = queries.shape
    part, kv_heads = keys.shape[:2]
    head_index = lax.axis_index("head")
    pieces = lax.axis_size("head")
    blocks = lax.axis_size("seq")
    heads_out = all_heads // pieces
    own_queries = lax.dynamic_slice_in_dim(queries, head_index * heads_out, heads_out, 1)
    own_queries = own_queries.reshape(rows_dev * heads_out, head_width)
    whole = pl.BlockSpec(memory_space=pltpu.VMEM)
    scaled = pl.pallas_call(
        functools.partial(scale_queries, head_width ** (-0.5)),
        out_shape=jax.ShapeDtypeStruct((2 * head_width, rows_dev * heads_out), jnp.bfloat16),
        in_specs=[whole],
        out_specs=whole,
        compiler_params=pltpu.CompilerParams(vmem_limit_bytes=8 * MIB),
    )(own_queries)
    own, *payloads = pl.pallas_call(
        functools.partial(pack, pieces // kv_heads, pieces, part, kv_heads),
        out_shape=[jax.ShapeDtypeStruct((2 * part, head_width), jnp.bfloat16)] * pieces,
        in_specs=[whole],
        out_specs=[whole] * pieces,
        compiler_params=pltpu.CompilerParams(vmem_limit_bytes=4 * MIB),
    )(jnp.concatenate([keys, values]).reshape(2 * part * kv_heads, head_width))
    mark = jnp.broadcast_to(block_ids.astype(jnp.bfloat16)[:, None], (MARK, head_width))
    own = jnp.concatenate([own, mark])
    near = [
        lax.ppermute(rows, "head", [(i, (i + shift + 1) % pieces) for i in range(pieces)])
        for shift, rows in enumerate(payloads)
    ]
    rest = jnp.concatenate(near)
    fold = functools.partial(attend_call, pieces, part, own, scaled)
    shifts = tuple(range(pieces))
    offsets = tuple(2 * part * i for i in range(pieces))

    def swap(rows, flip):
        return lax.ppermute(rows, "seq", [(i, i ^ flip) for i in range(blocks)])

    if blocks == 8:
        rest = rest[None]
        ways = ((4, 2), (2, 4), (6, 6))

        def hop(rows, way):
            return lax.ppermute(rows, "seq", [(i, i ^ way[i & 1]) for i in range(blocks)])

        near_one, near_two = [hop(own, way) for way in ways[:2]]
        mine = jnp.stack([own, near_one, near_two])
        along_one, along_two = [hop(rest, way) for way in ways[:2]]
        along_last = hop(jnp.concatenate([own[None], rest], axis=1), ways[2])

        def small(data, slots):
            return [(data, slot, (0,), None, (data, slot, 2 * part)) for slot in slots]

        def large(data, mark, slot, at=0):
            return (data, 0, tuple(at + offset for offset in offsets[:-1]), None, (mark, slot, 2 * part))

        state = fold(
            None,
            [mine, rest],
            [(0, 0, (0,), shifts[:1], None), (1, 0, offsets[:-1], shifts[1:], None)] + small(0, (1, 2)),
            False,
            OVERLAP,
        )
        early_rows = mine.shape[0] * mine.shape[1]
        both_other = swap(jnp.concatenate([mine.reshape(1, early_rows, head_width), rest], axis=1), 1)
        size = own.shape[0]
        state = fold(
            state,
            [both_other],
            [(0, 0, (size * i,), None, (0, 0, size * i + 2 * part)) for i in range(3)]
            + [(0, 0, tuple(early_rows + offset for offset in offsets[:-1]), None, (0, 0, 2 * part))],
            False,
        )
        along_one, along_two, state = lax.optimization_barrier((along_one, along_two, state))
        others = [swap(rows, 1) for rows in (along_one, along_two)]
        state = fold(state, [mine, along_one, along_two], [large(i, 0, i) for i in (1, 2)], False)
        along_last, state = lax.optimization_barrier((along_last, state))
        along_last, *others = lax.optimization_barrier((along_last, *others))
        other_last = swap(along_last, 1)
        state = fold(
            state,
            [along_last, both_other] + others,
            [(0, 0, (0,) + tuple(size + offset for offset in offsets[:-1]), None, (0, 0, 2 * part))] + [(1 + i, 0, offsets[:-1], None, (1, 0, size * i + 2 * part)) for i in (1, 2)],
            False,
        )
        result = fold(
            state,
            [other_last],
            [(0, 0, (0,) + tuple(own.shape[0] + offset for offset in offsets[:-1]), None, (0, 0, 2 * part))],
            True,
        )
    else:
        block = jnp.concatenate([own[: 2 * part], rest, own[2 * part :]])
        far = lax.all_gather(block, "seq", axis=0, tiled=False)
        unit = math.gcd(blocks, 8)
        far = far.reshape((blocks // unit, unit) + block.shape)
        items = [(0, i, offsets, None, (0, i, 2 * part * pieces)) for i in range(unit)]
        state = fold(None, [block[None]], [(0, 0, offsets, shifts, None)], False)
        state, _ = lax.scan(
            lambda held, rows: (tuple(fold(held, [rows], items, False)), None), tuple(state), far[:-1]
        )
        result = fold(state, [far[-1]], items, True)
    return result.reshape(rows_dev, heads_out, head_width)


def solution(mesh):
    return jax.shard_map(
        shards,
        mesh=mesh,
        in_specs=(
            P("seq", None, None),
            P(("seq", "head"), None, None),
            P(("seq", "head"), None, None),
            P("seq"),
        ),
        out_specs=P("seq", "head", None),
        check_vma=False,
    )
```

```python
import functools
import math

import jax
import jax.numpy as jnp
from jax import lax
from jax.experimental import pallas as pl
from jax.experimental.pallas import tpu as pltpu
from jax.sharding import PartitionSpec as P

MARK = 16
SUBLANES = 8
FINAL = 256
OVERLAP = 0
LOW = -1e30
HIGH = 1e30
MIB = 1024 * 1024


def pack(copies, pieces, part, kv_heads, rows_ref, *out_refs):
    here = lax.axis_index("head")
    rows = part * kv_heads
    at = lax.broadcasted_iota(jnp.int32, (part, rows), 0)
    source = lax.broadcasted_iota(jnp.int32, (part, rows), 1)
    picks = [
        jnp.where(source == at * kv_heads + head, 1.0, 0.0).astype(jnp.bfloat16) for head in range(kv_heads)
    ]
    for half in range(2):
        both = rows_ref[pl.ds(half * rows, rows), :]
        chosen = [jnp.dot(pick, both, preferred_element_type=jnp.float32).astype(jnp.bfloat16) for pick in picks]
        for shift, out_ref in enumerate(out_refs):
            kv_head = lax.rem(here + shift, pieces) // copies
            rows_out = chosen[0]
            for head in range(1, kv_heads):
                rows_out = jnp.where(kv_head == head, chosen[head], rows_out)
            out_ref[pl.ds(half * part, part), :] = rows_out


def scale_queries(scale, query_ref, out_ref):
    head_width = query_ref.shape[1]
    scaled = query_ref[...].astype(jnp.float32) * (scale * math.log2(math.e))
    coarse = scaled.astype(jnp.bfloat16)
    out_ref[:head_width, :] = coarse.T
    out_ref[head_width:, :] = (scaled - coarse.astype(jnp.float32)).astype(jnp.bfloat16).T


def attend(pieces, part, first, last, items, own_ref, query_ref, *refs):
    refs = list(refs)
    state = None if first else [refs.pop(0) for _ in range(3)]
    outs = [refs.pop() for _ in range(3)][::-1]
    head_width = query_ref.shape[0] // 2
    query_rows = query_ref.shape[1]
    group = query_rows // (pieces * part)
    here = lax.axis_index("head")
    own = own_ref[pl.ds(2 * part, MARK), :].astype(jnp.float32)[:SUBLANES]
    own = jnp.concatenate([own] * (query_rows // head_width), axis=1)

    blocks = []
    for data, slot, offsets, shifts, mark in items:
        rows_ref = refs[data].at[slot]
        if shifts is None:
            mark_data, mark_slot, mark_at = mark
            place = refs[mark_data][mark_slot, pl.ds(mark_at, MARK), :].astype(jnp.float32)[:SUBLANES]
            seen = jnp.concatenate([place] * (query_rows // head_width), axis=1) < own
        else:
            seen = None
        blocks.append((rows_ref, offsets, shifts, seen))

    def side(half):
        return jnp.concatenate(
            [
                rows_ref[pl.ds(offset + half * part, part), :]
                for rows_ref, offsets, _, _ in blocks
                for offset in offsets
            ]
        )

    keys = side(0)
    keys = jnp.concatenate([keys, keys], axis=1)
    values = side(1).T
    scores = jnp.dot(keys, query_ref[...], preferred_element_type=jnp.float32)
    cuts, tops, at = [], [], 0
    for _, offsets, shifts, seen in blocks:
        score = scores[at : at + len(offsets) * part]
        at += len(offsets) * part
        if seen is None:
            parts = []
            for i, shift in enumerate(shifts):
                cut = score[i * part : (i + 1) * part]
                key_at = lax.rem(here + pieces - shift, pieces) * part + lax.broadcasted_iota(jnp.int32, cut.shape, 0)
                query_at = lax.broadcasted_iota(jnp.int32, cut.shape, 1) // group
                parts.append(jnp.where(key_at <= query_at, cut, LOW))
            score = jnp.concatenate(parts)
        top = jnp.max(score.reshape(-1, SUBLANES, query_rows), axis=0)
        cuts.append(score)
        tops.append(top if seen is None else jnp.where(seen, top, LOW))
    high = jnp.max(functools.reduce(jnp.maximum, tops), axis=0, keepdims=True)
    if not first:
        old_high = state[0][...]
        high = jnp.maximum(old_high, high)
    weights, sums = [], []
    for score, (_, _, _, seen) in zip(cuts, blocks):
        base = high if seen is None else jnp.where(seen[:1], high, HIGH)
        expo = jnp.exp2(score - base)
        sums.append(jnp.sum(expo.reshape(-1, SUBLANES, query_rows), axis=0))
        weights.append(expo.astype(jnp.bfloat16))
    total = jnp.sum(functools.reduce(jnp.add, sums), axis=0, keepdims=True)
    accum = jnp.dot(values, jnp.concatenate(weights), preferred_element_type=jnp.float32)
    if not first:
        keep = jnp.exp2(old_high - high)
        total = total + state[1][...] * keep
        accum = accum + state[2][...] * keep
    if last:
        out_hbm, out_ref, sems = outs
        inverse = 1.0 / total
        copies = []
        for i in range(query_rows // FINAL):
            span = slice(i * FINAL, (i + 1) * FINAL)
            out_ref[span, :] = (accum[:, span] * inverse[:, span]).astype(out_ref.dtype).T
            copies.append(pltpu.make_async_copy(out_ref.at[span], out_hbm.at[span], sems.at[i]))
            copies[-1].start()
        for copy in copies:
            copy.wait()
    else:
        outs[0][...] = high
        outs[1][...] = total
        outs[2][...] = accum


def attend_call(pieces, part, own, query, state, datas, items, last, cost=0):
    head_width, query_rows = query.shape[0] // 2, query.shape[1]
    whole = pl.BlockSpec(memory_space=pltpu.VMEM)
    first = state is None
    operands = ([] if first else list(state)) + list(datas)
    if last:
        shapes = jax.ShapeDtypeStruct((query_rows, head_width), jnp.bfloat16)
        out_specs = pl.BlockSpec(memory_space=pl.ANY)
        scratch = [
            pltpu.VMEM((query_rows, head_width), jnp.bfloat16),
            pltpu.SemaphoreType.DMA((query_rows // FINAL,)),
        ]
    else:
        scratch = []
        shapes = [
            jax.ShapeDtypeStruct((1, query_rows), jnp.float32),
            jax.ShapeDtypeStruct((1, query_rows), jnp.float32),
            jax.ShapeDtypeStruct((head_width, query_rows), jnp.float32),
        ]
        out_specs = [whole] * 3
    return pl.pallas_call(
        functools.partial(attend, pieces, part, first, last, items),
        out_shape=shapes,
        in_specs=[whole] * (2 + len(operands)),
        out_specs=out_specs,
        scratch_shapes=scratch,
        compiler_params=pltpu.CompilerParams(vmem_limit_bytes=24 * MIB),
        cost_estimate=pl.CostEstimate(flops=cost, bytes_accessed=0, transcendentals=0),
    )(own, query, *operands)


def shards(queries, keys, values, block_ids):
    rows_dev, all_heads, head_width = queries.shape
    part, kv_heads = keys.shape[:2]
    head_index = lax.axis_index("head")
    pieces = lax.axis_size("head")
    blocks = lax.axis_size("seq")
    heads_out = all_heads // pieces
    own_queries = lax.dynamic_slice_in_dim(queries, head_index * heads_out, heads_out, 1)
    own_queries = own_queries.reshape(rows_dev * heads_out, head_width)
    whole = pl.BlockSpec(memory_space=pltpu.VMEM)
    scaled = pl.pallas_call(
        functools.partial(scale_queries, head_width ** (-0.5)),
        out_shape=jax.ShapeDtypeStruct((2 * head_width, rows_dev * heads_out), jnp.bfloat16),
        in_specs=[whole],
        out_specs=whole,
        compiler_params=pltpu.CompilerParams(vmem_limit_bytes=8 * MIB),
    )(own_queries)
    own, *payloads = pl.pallas_call(
        functools.partial(pack, pieces // kv_heads, pieces, part, kv_heads),
        out_shape=[jax.ShapeDtypeStruct((2 * part, head_width), jnp.bfloat16)] * pieces,
        in_specs=[whole],
        out_specs=[whole] * pieces,
        compiler_params=pltpu.CompilerParams(vmem_limit_bytes=4 * MIB),
    )(jnp.concatenate([keys, values]).reshape(2 * part * kv_heads, head_width))
    mark = jnp.broadcast_to(block_ids.astype(jnp.bfloat16)[:, None], (MARK, head_width))
    own = jnp.concatenate([own, mark])
    near = [
        lax.ppermute(rows, "head", [(i, (i + shift + 1) % pieces) for i in range(pieces)])
        for shift, rows in enumerate(payloads)
    ]
    rest = jnp.concatenate(near)
    fold = functools.partial(attend_call, pieces, part, own, scaled)
    shifts = tuple(range(pieces))
    offsets = tuple(2 * part * i for i in range(pieces))

    def swap(rows, flip):
        return lax.ppermute(rows, "seq", [(i, i ^ flip) for i in range(blocks)])

    if blocks == 8:
        rest = rest[None]
        ways = ((2, 6), (6, 2), (4, 4))

        def hop(rows, way):
            return lax.ppermute(rows, "seq", [(i, i ^ way[i & 1]) for i in range(blocks)])

        near_one, near_two = [hop(own, way) for way in ways[:2]]
        mine = jnp.stack([own, near_one, near_two])
        along_one, along_two = [hop(rest, way) for way in ways[:2]]
        along_last = hop(jnp.concatenate([own[None], rest], axis=1), ways[2])

        def small(data, slots):
            return [(data, slot, (0,), None, (data, slot, 2 * part)) for slot in slots]

        def large(data, mark, slot, at=0):
            return (data, 0, tuple(at + offset for offset in offsets[:-1]), None, (mark, slot, 2 * part))

        state = fold(
            None,
            [mine, rest],
            [(0, 0, (0,), shifts[:1], None), (1, 0, offsets[:-1], shifts[1:], None)] + small(0, (1, 2)),
            False,
            OVERLAP,
        )
        early_rows = mine.shape[0] * mine.shape[1]
        both_other = swap(jnp.concatenate([mine.reshape(1, early_rows, head_width), rest], axis=1), 1)
        size = own.shape[0]
        state = fold(
            state,
            [both_other],
            [(0, 0, (size * i,), None, (0, 0, size * i + 2 * part)) for i in range(3)]
            + [(0, 0, tuple(early_rows + offset for offset in offsets[:-1]), None, (0, 0, 2 * part))],
            False,
        )
        along_one, along_two, state = lax.optimization_barrier((along_one, along_two, state))
        others = [swap(rows, 1) for rows in (along_one, along_two)]
        state = fold(state, [mine, along_one, along_two], [large(i, 0, i) for i in (1, 2)], False)
        along_last, state = lax.optimization_barrier((along_last, state))
        along_last, *others = lax.optimization_barrier((along_last, *others))
        other_last = swap(along_last, 1)
        state = fold(
            state,
            [along_last, both_other] + others,
            [(0, 0, (0,) + tuple(size + offset for offset in offsets[:-1]), None, (0, 0, 2 * part))] + [(1 + i, 0, offsets[:-1], None, (1, 0, size * i + 2 * part)) for i in (1, 2)],
            False,
        )
        result = fold(
            state,
            [other_last],
            [(0, 0, (0,) + tuple(own.shape[0] + offset for offset in offsets[:-1]), None, (0, 0, 2 * part))],
            True,
        )
    else:
        block = jnp.concatenate([own[: 2 * part], rest, own[2 * part :]])
        far = lax.all_gather(block, "seq", axis=0, tiled=False)
        unit = math.gcd(blocks, 8)
        far = far.reshape((blocks // unit, unit) + block.shape)
        items = [(0, i, offsets, None, (0, i, 2 * part * pieces)) for i in range(unit)]
        state = fold(None, [block[None]], [(0, 0, offsets, shifts, None)], False)
        state, _ = lax.scan(
            lambda held, rows: (tuple(fold(held, [rows], items, False)), None), tuple(state), far[:-1]
        )
        result = fold(state, [far[-1]], items, True)
    return result.reshape(rows_dev, heads_out, head_width)


def solution(mesh):
    return jax.shard_map(
        shards,
        mesh=mesh,
        in_specs=(
            P("seq", None, None),
            P(("seq", "head"), None, None),
            P(("seq", "head"), None, None),
            P("seq"),
        ),
        out_specs=P("seq", "head", None),
        check_vma=False,
    )
```

```python
import functools
import math

import jax
import jax.numpy as jnp
from jax import lax
from jax.experimental import pallas as pl
from jax.experimental.pallas import tpu as pltpu
from jax.sharding import PartitionSpec as P

MARK = 16
SUBLANES = 8
FINAL = 256
OVERLAP = 0
LOW = -1e30
HIGH = 1e30
MIB = 1024 * 1024


def pack(copies, pieces, part, kv_heads, rows_ref, *out_refs):
    here = lax.axis_index("head")
    rows = part * kv_heads
    at = lax.broadcasted_iota(jnp.int32, (part, rows), 0)
    source = lax.broadcasted_iota(jnp.int32, (part, rows), 1)
    picks = [
        jnp.where(source == at * kv_heads + head, 1.0, 0.0).astype(jnp.bfloat16) for head in range(kv_heads)
    ]
    for half in range(2):
        both = rows_ref[pl.ds(half * rows, rows), :]
        chosen = [jnp.dot(pick, both, preferred_element_type=jnp.float32).astype(jnp.bfloat16) for pick in picks]
        for shift, out_ref in enumerate(out_refs):
            kv_head = lax.rem(here + shift, pieces) // copies
            rows_out = chosen[0]
            for head in range(1, kv_heads):
                rows_out = jnp.where(kv_head == head, chosen[head], rows_out)
            out_ref[pl.ds(half * part, part), :] = rows_out


def scale_queries(scale, query_ref, out_ref):
    head_width = query_ref.shape[1]
    scaled = query_ref[...].astype(jnp.float32) * (scale * math.log2(math.e))
    coarse = scaled.astype(jnp.bfloat16)
    out_ref[:head_width, :] = coarse.T
    out_ref[head_width:, :] = (scaled - coarse.astype(jnp.float32)).astype(jnp.bfloat16).T


def attend(pieces, part, first, last, items, own_ref, query_ref, *refs):
    refs = list(refs)
    state = None if first else [refs.pop(0) for _ in range(3)]
    outs = [refs.pop() for _ in range(3)][::-1]
    head_width = query_ref.shape[0] // 2
    query_rows = query_ref.shape[1]
    group = query_rows // (pieces * part)
    here = lax.axis_index("head")
    own = own_ref[pl.ds(2 * part, MARK), :].astype(jnp.float32)[:SUBLANES]
    own = jnp.concatenate([own] * (query_rows // head_width), axis=1)

    blocks = []
    for data, slot, offsets, shifts, mark in items:
        rows_ref = refs[data].at[slot]
        if shifts is None:
            mark_data, mark_slot, mark_at = mark
            place = refs[mark_data][mark_slot, pl.ds(mark_at, MARK), :].astype(jnp.float32)[:SUBLANES]
            seen = jnp.concatenate([place] * (query_rows // head_width), axis=1) < own
        else:
            seen = None
        blocks.append((rows_ref, offsets, shifts, seen))

    def side(half):
        return jnp.concatenate(
            [
                rows_ref[pl.ds(offset + half * part, part), :]
                for rows_ref, offsets, _, _ in blocks
                for offset in offsets
            ]
        )

    keys = side(0)
    keys = jnp.concatenate([keys, keys], axis=1)
    values = side(1).T
    scores = jnp.dot(keys, query_ref[...], preferred_element_type=jnp.float32)
    cuts, tops, at = [], [], 0
    for _, offsets, shifts, seen in blocks:
        score = scores[at : at + len(offsets) * part]
        at += len(offsets) * part
        if seen is None:
            parts = []
            for i, shift in enumerate(shifts):
                cut = score[i * part : (i + 1) * part]
                key_at = lax.rem(here + pieces - shift, pieces) * part + lax.broadcasted_iota(jnp.int32, cut.shape, 0)
                query_at = lax.broadcasted_iota(jnp.int32, cut.shape, 1) // group
                parts.append(jnp.where(key_at <= query_at, cut, LOW))
            score = jnp.concatenate(parts)
        top = jnp.max(score.reshape(-1, SUBLANES, query_rows), axis=0)
        cuts.append(score)
        tops.append(top if seen is None else jnp.where(seen, top, LOW))
    high = jnp.max(functools.reduce(jnp.maximum, tops), axis=0, keepdims=True)
    if not first:
        old_high = state[0][...]
        high = jnp.maximum(old_high, high)
    weights, sums = [], []
    for score, (_, _, _, seen) in zip(cuts, blocks):
        base = high if seen is None else jnp.where(seen[:1], high, HIGH)
        expo = jnp.exp2(score - base)
        sums.append(jnp.sum(expo.reshape(-1, SUBLANES, query_rows), axis=0))
        weights.append(expo.astype(jnp.bfloat16))
    total = jnp.sum(functools.reduce(jnp.add, sums), axis=0, keepdims=True)
    accum = jnp.dot(values, jnp.concatenate(weights), preferred_element_type=jnp.float32)
    if not first:
        keep = jnp.exp2(old_high - high)
        total = total + state[1][...] * keep
        accum = accum + state[2][...] * keep
    if last:
        out_hbm, out_ref, sems = outs
        inverse = 1.0 / total
        copies = []
        for i in range(query_rows // FINAL):
            span = slice(i * FINAL, (i + 1) * FINAL)
            out_ref[span, :] = (accum[:, span] * inverse[:, span]).astype(out_ref.dtype).T
            copies.append(pltpu.make_async_copy(out_ref.at[span], out_hbm.at[span], sems.at[i]))
            copies[-1].start()
        for copy in copies:
            copy.wait()
    else:
        outs[0][...] = high
        outs[1][...] = total
        outs[2][...] = accum


def attend_call(pieces, part, own, query, state, datas, items, last, cost=0):
    head_width, query_rows = query.shape[0] // 2, query.shape[1]
    whole = pl.BlockSpec(memory_space=pltpu.VMEM)
    first = state is None
    operands = ([] if first else list(state)) + list(datas)
    if last:
        shapes = jax.ShapeDtypeStruct((query_rows, head_width), jnp.bfloat16)
        out_specs = pl.BlockSpec(memory_space=pl.ANY)
        scratch = [
            pltpu.VMEM((query_rows, head_width), jnp.bfloat16),
            pltpu.SemaphoreType.DMA((query_rows // FINAL,)),
        ]
    else:
        scratch = []
        shapes = [
            jax.ShapeDtypeStruct((1, query_rows), jnp.float32),
            jax.ShapeDtypeStruct((1, query_rows), jnp.float32),
            jax.ShapeDtypeStruct((head_width, query_rows), jnp.float32),
        ]
        out_specs = [whole] * 3
    return pl.pallas_call(
        functools.partial(attend, pieces, part, first, last, items),
        out_shape=shapes,
        in_specs=[whole] * (2 + len(operands)),
        out_specs=out_specs,
        scratch_shapes=scratch,
        compiler_params=pltpu.CompilerParams(vmem_limit_bytes=24 * MIB),
        cost_estimate=pl.CostEstimate(flops=cost, bytes_accessed=0, transcendentals=0),
    )(own, query, *operands)


def shards(queries, keys, values, block_ids):
    rows_dev, all_heads, head_width = queries.shape
    part, kv_heads = keys.shape[:2]
    head_index = lax.axis_index("head")
    pieces = lax.axis_size("head")
    blocks = lax.axis_size("seq")
    heads_out = all_heads // pieces
    own_queries = lax.dynamic_slice_in_dim(queries, head_index * heads_out, heads_out, 1)
    own_queries = own_queries.reshape(rows_dev * heads_out, head_width)
    whole = pl.BlockSpec(memory_space=pltpu.VMEM)
    scaled = pl.pallas_call(
        functools.partial(scale_queries, head_width ** (-0.5)),
        out_shape=jax.ShapeDtypeStruct((2 * head_width, rows_dev * heads_out), jnp.bfloat16),
        in_specs=[whole],
        out_specs=whole,
        compiler_params=pltpu.CompilerParams(vmem_limit_bytes=8 * MIB),
    )(own_queries)
    own, *payloads = pl.pallas_call(
        functools.partial(pack, pieces // kv_heads, pieces, part, kv_heads),
        out_shape=[jax.ShapeDtypeStruct((2 * part, head_width), jnp.bfloat16)] * pieces,
        in_specs=[whole],
        out_specs=[whole] * pieces,
        compiler_params=pltpu.CompilerParams(vmem_limit_bytes=4 * MIB),
    )(jnp.concatenate([keys, values]).reshape(2 * part * kv_heads, head_width))
    mark = jnp.broadcast_to(block_ids.astype(jnp.bfloat16)[:, None], (MARK, head_width))
    own = jnp.concatenate([own, mark])
    near = [
        lax.ppermute(rows, "head", [(i, (i + shift + 1) % pieces) for i in range(pieces)])
        for shift, rows in enumerate(payloads)
    ]
    rest = jnp.concatenate(near)
    fold = functools.partial(attend_call, pieces, part, own, scaled)
    shifts = tuple(range(pieces))
    offsets = tuple(2 * part * i for i in range(pieces))

    def swap(rows, flip):
        return lax.ppermute(rows, "seq", [(i, i ^ flip) for i in range(blocks)])

    if blocks == 8:
        rest = rest[None]
        ways = ((4, 2), (6, 6), (2, 4))

        def hop(rows, way):
            return lax.ppermute(rows, "seq", [(i, i ^ way[i & 1]) for i in range(blocks)])

        near_one, near_two = [hop(own, way) for way in ways[:2]]
        mine = jnp.stack([own, near_one, near_two])
        along_one, along_two = [hop(rest, way) for way in ways[:2]]
        along_last = hop(jnp.concatenate([own[None], rest], axis=1), ways[2])

        def small(data, slots):
            return [(data, slot, (0,), None, (data, slot, 2 * part)) for slot in slots]

        def large(data, mark, slot, at=0):
            return (data, 0, tuple(at + offset for offset in offsets[:-1]), None, (mark, slot, 2 * part))

        state = fold(
            None,
            [mine, rest],
            [(0, 0, (0,), shifts[:1], None), (1, 0, offsets[:-1], shifts[1:], None)] + small(0, (1, 2)),
            False,
            OVERLAP,
        )
        early_rows = mine.shape[0] * mine.shape[1]
        both_other = swap(jnp.concatenate([mine.reshape(1, early_rows, head_width), rest], axis=1), 1)
        size = own.shape[0]
        state = fold(
            state,
            [both_other],
            [(0, 0, (size * i,), None, (0, 0, size * i + 2 * part)) for i in range(3)]
            + [(0, 0, tuple(early_rows + offset for offset in offsets[:-1]), None, (0, 0, 2 * part))],
            False,
        )
        along_one, along_two, state = lax.optimization_barrier((along_one, along_two, state))
        others = [swap(rows, 1) for rows in (along_one, along_two)]
        state = fold(state, [mine, along_one, along_two], [large(i, 0, i) for i in (1, 2)], False)
        along_last, state = lax.optimization_barrier((along_last, state))
        along_last, *others = lax.optimization_barrier((along_last, *others))
        other_last = swap(along_last, 1)
        state = fold(
            state,
            [along_last, both_other] + others,
            [(0, 0, (0,) + tuple(size + offset for offset in offsets[:-1]), None, (0, 0, 2 * part))] + [(1 + i, 0, offsets[:-1], None, (1, 0, size * i + 2 * part)) for i in (1, 2)],
            False,
        )
        result = fold(
            state,
            [other_last],
            [(0, 0, (0,) + tuple(own.shape[0] + offset for offset in offsets[:-1]), None, (0, 0, 2 * part))],
            True,
        )
    else:
        block = jnp.concatenate([own[: 2 * part], rest, own[2 * part :]])
        far = lax.all_gather(block, "seq", axis=0, tiled=False)
        unit = math.gcd(blocks, 8)
        far = far.reshape((blocks // unit, unit) + block.shape)
        items = [(0, i, offsets, None, (0, i, 2 * part * pieces)) for i in range(unit)]
        state = fold(None, [block[None]], [(0, 0, offsets, shifts, None)], False)
        state, _ = lax.scan(
            lambda held, rows: (tuple(fold(held, [rows], items, False)), None), tuple(state), far[:-1]
        )
        result = fold(state, [far[-1]], items, True)
    return result.reshape(rows_dev, heads_out, head_width)


def solution(mesh):
    return jax.shard_map(
        shards,
        mesh=mesh,
        in_specs=(
            P("seq", None, None),
            P(("seq", "head"), None, None),
            P(("seq", "head"), None, None),
            P("seq"),
        ),
        out_specs=P("seq", "head", None),
        check_vma=False,
    )
```

```python
import functools
import math

import jax
import jax.numpy as jnp
from jax import lax
from jax.experimental import pallas as pl
from jax.experimental.pallas import tpu as pltpu
from jax.sharding import PartitionSpec as P

MARK = 16
SUBLANES = 8
FINAL = 512
OVERLAP = 0
LOW = -1e30
HIGH = 1e30
MIB = 1024 * 1024


def pack(copies, pieces, part, kv_heads, rows_ref, *out_refs):
    here = lax.axis_index("head")
    rows = part * kv_heads
    at = lax.broadcasted_iota(jnp.int32, (part, rows), 0)
    source = lax.broadcasted_iota(jnp.int32, (part, rows), 1)
    picks = [
        jnp.where(source == at * kv_heads + head, 1.0, 0.0).astype(jnp.bfloat16) for head in range(kv_heads)
    ]
    for half in range(2):
        both = rows_ref[pl.ds(half * rows, rows), :]
        chosen = [jnp.dot(pick, both, preferred_element_type=jnp.float32).astype(jnp.bfloat16) for pick in picks]
        for shift, out_ref in enumerate(out_refs):
            kv_head = lax.rem(here + shift, pieces) // copies
            rows_out = chosen[0]
            for head in range(1, kv_heads):
                rows_out = jnp.where(kv_head == head, chosen[head], rows_out)
            out_ref[pl.ds(half * part, part), :] = rows_out


def scale_queries(scale, query_ref, out_ref):
    head_width = query_ref.shape[1]
    scaled = query_ref[...].astype(jnp.float32) * (scale * math.log2(math.e))
    coarse = scaled.astype(jnp.bfloat16)
    out_ref[:head_width, :] = coarse.T
    out_ref[head_width:, :] = (scaled - coarse.astype(jnp.float32)).astype(jnp.bfloat16).T


def attend(pieces, part, first, last, items, own_ref, query_ref, *refs):
    refs = list(refs)
    state = None if first else [refs.pop(0) for _ in range(3)]
    outs = [refs.pop() for _ in range(3)][::-1]
    head_width = query_ref.shape[0] // 2
    query_rows = query_ref.shape[1]
    group = query_rows // (pieces * part)
    here = lax.axis_index("head")
    own = own_ref[pl.ds(2 * part, MARK), :].astype(jnp.float32)[:SUBLANES]
    own = jnp.concatenate([own] * (query_rows // head_width), axis=1)

    blocks = []
    for data, slot, offsets, shifts, mark in items:
        rows_ref = refs[data].at[slot]
        if shifts is None:
            mark_data, mark_slot, mark_at = mark
            place = refs[mark_data][mark_slot, pl.ds(mark_at, MARK), :].astype(jnp.float32)[:SUBLANES]
            seen = jnp.concatenate([place] * (query_rows // head_width), axis=1) < own
        else:
            seen = None
        blocks.append((rows_ref, offsets, shifts, seen))

    def side(half):
        return jnp.concatenate(
            [
                rows_ref[pl.ds(offset + half * part, part), :]
                for rows_ref, offsets, _, _ in blocks
                for offset in offsets
            ]
        )

    keys = side(0)
    keys = jnp.concatenate([keys, keys], axis=1)
    values = side(1).T
    scores = jnp.dot(keys, query_ref[...], preferred_element_type=jnp.float32)
    cuts, tops, at = [], [], 0
    for _, offsets, shifts, seen in blocks:
        score = scores[at : at + len(offsets) * part]
        at += len(offsets) * part
        if seen is None:
            parts = []
            for i, shift in enumerate(shifts):
                cut = score[i * part : (i + 1) * part]
                key_at = lax.rem(here + pieces - shift, pieces) * part + lax.broadcasted_iota(jnp.int32, cut.shape, 0)
                query_at = lax.broadcasted_iota(jnp.int32, cut.shape, 1) // group
                parts.append(jnp.where(key_at <= query_at, cut, LOW))
            score = jnp.concatenate(parts)
        top = jnp.max(score.reshape(-1, SUBLANES, query_rows), axis=0)
        cuts.append(score)
        tops.append(top if seen is None else jnp.where(seen, top, LOW))
    high = jnp.max(functools.reduce(jnp.maximum, tops), axis=0, keepdims=True)
    if not first:
        old_high = state[0][...]
        high = jnp.maximum(old_high, high)
    weights, sums = [], []
    for score, (_, _, _, seen) in zip(cuts, blocks):
        base = high if seen is None else jnp.where(seen[:1], high, HIGH)
        expo = jnp.exp2(score - base)
        sums.append(jnp.sum(expo.reshape(-1, SUBLANES, query_rows), axis=0))
        weights.append(expo.astype(jnp.bfloat16))
    total = jnp.sum(functools.reduce(jnp.add, sums), axis=0, keepdims=True)
    accum = jnp.dot(values, jnp.concatenate(weights), preferred_element_type=jnp.float32)
    if not first:
        keep = jnp.exp2(old_high - high)
        total = total + state[1][...] * keep
        accum = accum + state[2][...] * keep
    if last:
        out_hbm, out_ref, sems = outs
        inverse = 1.0 / total
        copies = []
        for i in range(query_rows // FINAL):
            span = slice(i * FINAL, (i + 1) * FINAL)
            out_ref[span, :] = (accum[:, span] * inverse[:, span]).astype(out_ref.dtype).T
            copies.append(pltpu.make_async_copy(out_ref.at[span], out_hbm.at[span], sems.at[i]))
            copies[-1].start()
        for copy in copies:
            copy.wait()
    else:
        outs[0][...] = high
        outs[1][...] = total
        outs[2][...] = accum


def attend_call(pieces, part, own, query, state, datas, items, last, cost=0):
    head_width, query_rows = query.shape[0] // 2, query.shape[1]
    whole = pl.BlockSpec(memory_space=pltpu.VMEM)
    first = state is None
    operands = ([] if first else list(state)) + list(datas)
    if last:
        shapes = jax.ShapeDtypeStruct((query_rows, head_width), jnp.bfloat16)
        out_specs = pl.BlockSpec(memory_space=pl.ANY)
        scratch = [
            pltpu.VMEM((query_rows, head_width), jnp.bfloat16),
            pltpu.SemaphoreType.DMA((query_rows // FINAL,)),
        ]
    else:
        scratch = []
        shapes = [
            jax.ShapeDtypeStruct((1, query_rows), jnp.float32),
            jax.ShapeDtypeStruct((1, query_rows), jnp.float32),
            jax.ShapeDtypeStruct((head_width, query_rows), jnp.float32),
        ]
        out_specs = [whole] * 3
    return pl.pallas_call(
        functools.partial(attend, pieces, part, first, last, items),
        out_shape=shapes,
        in_specs=[whole] * (2 + len(operands)),
        out_specs=out_specs,
        scratch_shapes=scratch,
        compiler_params=pltpu.CompilerParams(vmem_limit_bytes=24 * MIB),
        cost_estimate=pl.CostEstimate(flops=cost, bytes_accessed=0, transcendentals=0),
    )(own, query, *operands)


def shards(queries, keys, values, block_ids):
    rows_dev, all_heads, head_width = queries.shape
    part, kv_heads = keys.shape[:2]
    head_index = lax.axis_index("head")
    pieces = lax.axis_size("head")
    blocks = lax.axis_size("seq")
    heads_out = all_heads // pieces
    own_queries = lax.dynamic_slice_in_dim(queries, head_index * heads_out, heads_out, 1)
    own_queries = own_queries.reshape(rows_dev * heads_out, head_width)
    whole = pl.BlockSpec(memory_space=pltpu.VMEM)
    scaled = pl.pallas_call(
        functools.partial(scale_queries, head_width ** (-0.5)),
        out_shape=jax.ShapeDtypeStruct((2 * head_width, rows_dev * heads_out), jnp.bfloat16),
        in_specs=[whole],
        out_specs=whole,
        compiler_params=pltpu.CompilerParams(vmem_limit_bytes=8 * MIB),
    )(own_queries)
    own, *payloads = pl.pallas_call(
        functools.partial(pack, pieces // kv_heads, pieces, part, kv_heads),
        out_shape=[jax.ShapeDtypeStruct((2 * part, head_width), jnp.bfloat16)] * pieces,
        in_specs=[whole],
        out_specs=[whole] * pieces,
        compiler_params=pltpu.CompilerParams(vmem_limit_bytes=4 * MIB),
    )(jnp.concatenate([keys, values]).reshape(2 * part * kv_heads, head_width))
    mark = jnp.broadcast_to(block_ids.astype(jnp.bfloat16)[:, None], (MARK, head_width))
    own = jnp.concatenate([own, mark])
    near = [
        lax.ppermute(rows, "head", [(i, (i + shift + 1) % pieces) for i in range(pieces)])
        for shift, rows in enumerate(payloads)
    ]
    rest = jnp.concatenate(near)
    fold = functools.partial(attend_call, pieces, part, own, scaled)
    shifts = tuple(range(pieces))
    offsets = tuple(2 * part * i for i in range(pieces))

    def swap(rows, flip):
        return lax.ppermute(rows, "seq", [(i, i ^ flip) for i in range(blocks)])

    if blocks == 8:
        rest = rest[None]
        ways = ((2, 4), (6, 6), (4, 2))

        def hop(rows, way):
            return lax.ppermute(rows, "seq", [(i, i ^ way[i & 1]) for i in range(blocks)])

        near_one, near_two = [hop(own, way) for way in ways[:2]]
        mine = jnp.stack([own, near_one, near_two])
        along_one, along_two = [hop(rest, way) for way in ways[:2]]
        along_last = hop(jnp.concatenate([own[None], rest], axis=1), ways[2])

        def small(data, slots):
            return [(data, slot, (0,), None, (data, slot, 2 * part)) for slot in slots]

        def large(data, mark, slot, at=0):
            return (data, 0, tuple(at + offset for offset in offsets[:-1]), None, (mark, slot, 2 * part))

        state = fold(
            None,
            [mine, rest],
            [(0, 0, (0,), shifts[:1], None), (1, 0, offsets[:-1], shifts[1:], None)] + small(0, (1, 2)),
            False,
            OVERLAP,
        )
        early_rows = mine.shape[0] * mine.shape[1]
        both_other = swap(jnp.concatenate([mine.reshape(1, early_rows, head_width), rest], axis=1), 1)
        size = own.shape[0]
        state = fold(
            state,
            [both_other],
            [(0, 0, (size * i,), None, (0, 0, size * i + 2 * part)) for i in range(3)]
            + [(0, 0, tuple(early_rows + offset for offset in offsets[:-1]), None, (0, 0, 2 * part))],
            False,
        )
        along_one, along_two, state = lax.optimization_barrier((along_one, along_two, state))
        others = [swap(rows, 1) for rows in (along_one, along_two)]
        state = fold(state, [mine, along_one, along_two], [large(i, 0, i) for i in (1, 2)], False)
        along_last, state = lax.optimization_barrier((along_last, state))
        along_last, *others = lax.optimization_barrier((along_last, *others))
        other_last = swap(along_last, 1)
        state = fold(
            state,
            [along_last, both_other] + others,
            [(0, 0, (0,) + tuple(size + offset for offset in offsets[:-1]), None, (0, 0, 2 * part))] + [(1 + i, 0, offsets[:-1], None, (1, 0, size * i + 2 * part)) for i in (1, 2)],
            False,
        )
        result = fold(
            state,
            [other_last],
            [(0, 0, (0,) + tuple(own.shape[0] + offset for offset in offsets[:-1]), None, (0, 0, 2 * part))],
            True,
        )
    else:
        block = jnp.concatenate([own[: 2 * part], rest, own[2 * part :]])
        far = lax.all_gather(block, "seq", axis=0, tiled=False)
        unit = math.gcd(blocks, 8)
        far = far.reshape((blocks // unit, unit) + block.shape)
        items = [(0, i, offsets, None, (0, i, 2 * part * pieces)) for i in range(unit)]
        state = fold(None, [block[None]], [(0, 0, offsets, shifts, None)], False)
        state, _ = lax.scan(
            lambda held, rows: (tuple(fold(held, [rows], items, False)), None), tuple(state), far[:-1]
        )
        result = fold(state, [far[-1]], items, True)
    return result.reshape(rows_dev, heads_out, head_width)


def solution(mesh):
    return jax.shard_map(
        shards,
        mesh=mesh,
        in_specs=(
            P("seq", None, None),
            P(("seq", "head"), None, None),
            P(("seq", "head"), None, None),
            P("seq"),
        ),
        out_specs=P("seq", "head", None),
        check_vma=False,
    )
```
